32 devices in a mesh: segment: 2 (over core), rows: 4 (over z), dp: 4 (over y, x).
Axes of the slice: x: 2, y: 2, z: 4, core: 2. Of those that a mesh axis runs over, the one named last changes fastest.
Arguments:
- coarse: bfloat16 [8, 100, 48, 256], P(('segment', 'dp'), None, 'rows'), may hold values from -6 to 6
- target: bfloat16 [8, 64, 48, 256], P(('segment', 'dp'), None, 'rows'), may hold values from -6 to 6
- noise: bfloat16 [8, 4, 64, 64, 144], P(('segment', 'dp'), 'rows'), may hold values from -6 to 6
- regions: int32 [8, 4, 32, 4], P(('segment', 'dp')), may hold values from 0 to 244, as said below
- reg_conv: bfloat16 [128, 900], replicated, may hold values from -0.1875 to 0.1875
- reg_out: bfloat16 [64, 128], replicated, may hold values from -0.5 to 0.5
- conv_one: bfloat16 [128, 1152], replicated, may hold values from -0.1875 to 0.1875
- conv_two: bfloat16 [128, 1152], replicated, may hold values from -0.1875 to 0.1875
- out_proj: bfloat16 [64, 128], replicated, may hold values from -0.5 to 0.5
- step_embed: float32 [32, 128], replicated, may hold values from -3 to 3
Outputs:
- mean_field: bfloat16 [8, 64, 48, 256], P(('segment', 'dp'), None, 'rows')
- owner_loss: float32 [8, 4], P(('segment', 'dp'), 'rows')
- grad_conv_one: float32 [128, 1152], replicated
- grad_conv_two: float32 [128, 1152], replicated
- grad_out_proj: float32 [64, 128], replicated
- grad_embed: float32 [32, 128], replicated
The draws below stay inside these ranges and needn't reach their ends.
Inputs may be any that keep to these rules, and one draw needn't show every extreme that they name: `regions`: for sample s, strip i and entry k: entry 0 is the patch's row offset within strip i (0 on the last strip), entry 1 its first column, at most 244, entry 2 its owner, entry 3 its noise level below 32. Every owner receives 2 * 32, 32 or 16 patches of a sample; for each owner with 64 there is one with 32 and two with 16. No strip lists more than 16 patches for one owner, and some strip lists exactly 16 for one owner.
All inputs are finite; a program needn't handle non-finite values.
Results may differ from the reference program's by a relative error of at most 0.0048.
Values may be sent and summed in bfloat16 or wider, within the bound.
No kernel may reach another device: no remote copies, remote signals or barrier semaphores. Data moves between devices by JAX's collectives and lax.ppermute only.
A program may use at most 192 MiB of HBM per device.

```python
import math
import jax
import jax.numpy as jnp
from jax import lax

CIN = 100
CT = 64
REG = 128
DC = 128
NT = 32
PATCH = 12
KS = 32
W = 256
NS = 8
H = 48
CAP = 16
MOST = 64
N_ROWS = 4


def draw_sample_regions(key):
    subkeys = jax.random.split(key, 4)
    pattern = jnp.array([2 * KS, KS, KS // 2, KS // 2], dtype=jnp.int32)
    owner_loads = jnp.tile(pattern, N_ROWS // 4)
    ranking = jax.random.permutation(subkeys[0], N_ROWS).astype(jnp.int32)
    bounds = jnp.cumsum(owner_loads)
    tokens = jnp.arange(N_ROWS * KS, dtype=jnp.int32)
    rank_ids = jnp.sum((tokens[:, None] >= bounds[None, :]).astype(jnp.int32), axis=1)
    owner_of = ranking[rank_ids]
    run_ids = tokens // CAP
    source_row = run_ids % N_ROWS
    slot_index = run_ids // N_ROWS * CAP + tokens % CAP
    owner_table = jnp.zeros((N_ROWS, KS), jnp.int32).at[source_row, slot_index].set(owner_of)
    offsets = jax.random.randint(subkeys[1], (N_ROWS, KS), 0, PATCH, dtype=jnp.int32)
    last_strip = jnp.arange(N_ROWS, dtype=jnp.int32)[:, None] == N_ROWS - 1
    offsets = jnp.where(last_strip, 0, offsets)
    first_cols = jax.random.randint(subkeys[2], (N_ROWS, KS), 0, W - PATCH + 1, dtype=jnp.int32)
    step_ids = jax.random.randint(subkeys[3], (N_ROWS, KS), 0, NT, dtype=jnp.int32)
    return jnp.stack([offsets, first_cols, owner_table, step_ids], axis=-1).astype(jnp.int32)


def draw_regions(key, part):
    sample_keys = jax.random.split(jax.random.fold_in(key, 17), NS)
    return jax.vmap(draw_sample_regions)(sample_keys)


def shard_levels(own_key, extent, pieces, least, largest):
    def one(dim, parts):
        draws = jax.random.uniform(jax.random.fold_in(jax.random.fold_in(own_key, 6), dim), (parts,), jnp.float32, least / len(pieces), largest / len(pieces))
        return jnp.repeat(jnp.exp(draws), extent[dim] // parts).reshape((-1,) + (1,) * (len(extent) - dim - 1))

    factor_of = one(*pieces[0])
    for cut in pieces[1:]:
        factor_of = factor_of * one(*cut)
    return factor_of


def centred(key, extent, deviation, bound, pieces=(), kind=jnp.bfloat16):
    drawn = jax.random.normal(key, extent, jnp.float32) * deviation
    if len(pieces) > 0:
        drawn = shard_levels(key, extent, pieces, -0.22, 0.18) * drawn
    return jnp.clip(drawn, min=-bound, max=bound).astype(kind)


def setup_inputs(seed: int = 0) -> dict:
    arg_keys = jax.random.split(jax.random.key(seed), 11)
    return {
        "coarse": centred(arg_keys[0], (NS, CIN, H, W), 1.0, 6.0, ((0, 8), (2, 4))),
        "target": centred(arg_keys[1], (NS, CT, H, W), 1.0, 6.0, ((0, 8), (2, 4))),
        "noise": centred(arg_keys[2], (NS, N_ROWS, MOST, CT, PATCH * PATCH), 1.0, 6.0, ((0, 8), (1, 4))),
        "regions": draw_regions(jax.random.fold_in(arg_keys[10], 71), 0),
        "reg_conv": centred(arg_keys[4], (REG, 9 * CIN), (9 * CIN) ** -0.5, 0.1875),
        "reg_out": centred(arg_keys[5], (CT, REG), REG ** -0.5, 0.5),
        "conv_one": centred(arg_keys[6], (DC, 18 * CT), (18 * CT) ** -0.5, 0.1875),
        "conv_two": centred(arg_keys[7], (DC, 9 * DC), (9 * DC) ** -0.5, 0.1875),
        "out_proj": centred(arg_keys[8], (CT, DC), DC ** -0.5, 0.5),
        "step_embed": centred(arg_keys[9], (NT, DC), 0.5, 3.0, (), jnp.float32),
    }


TAPS = ((-1, -1), (-1, 0), (-1, 1), (0, -1), (0, 0), (0, 1), (1, -1), (1, 0), (1, 1))

def shifted(values, row_step, col_step, stride):
    length = values.shape[-1]
    margin = stride + 1
    widths = [(0, 0)] * (values.ndim - 1) + [(margin, margin)]
    padded = jnp.pad(values, widths)
    offset = margin + row_step * stride + col_step
    moved = lax.slice_in_dim(padded, offset, offset + length, axis=values.ndim - 1)
    column = jnp.arange(length, dtype=jnp.int32) % stride + col_step
    inside = (column >= 0) & (column < stride)
    return jnp.where(inside, moved, jnp.zeros((), moved.dtype))

def columns(values, stride):
    return jnp.concatenate([shifted(values, row_step, col_step, stride) for row_step, col_step in TAPS], axis=-2)

def fold(gradients, stride):
    width = gradients.shape[-2] // 9
    result = jnp.zeros(gradients.shape[:-2] + (width, gradients.shape[-1]), jnp.float32)
    for position, (row_step, col_step) in enumerate(TAPS):
        piece = gradients[..., position * width:(position + 1) * width, :]
        result = result + shifted(piece, -row_step, -col_step, stride)
    return result

def noise_levels(level_count):
    steps_f = jnp.arange(level_count, dtype=jnp.float32)
    return 0.1 * jnp.exp(steps_f * (math.log(100.0) / (level_count - 1)))

def silu_slope(values):
    gate = jax.nn.sigmoid(values)
    return gate * (1.0 + values * (1.0 - gate))

def product(form, left, right):
    return jnp.einsum(form, left.astype(jnp.float32), right.astype(jnp.float32), precision=lax.Precision.HIGHEST)

def regress(grid_rows, reg_conv, reg_out):
    channels, height, width = grid_rows.shape
    flat = grid_rows.reshape(channels, height * width)
    hidden = product('ok,kp->op', reg_conv, columns(flat, width))
    activated = jax.nn.silu(hidden).astype(jnp.bfloat16)
    mean_flat = product('co,op->cp', reg_out, activated).astype(jnp.bfloat16)
    return mean_flat.reshape(reg_out.shape[0], height, width)

def patch_block(mean_part, target_part, noise_part, step_ids, in_use, weights):
    conv_one, conv_two, out_proj, step_embed = weights
    stride = PATCH
    level_count = step_embed.shape[0]
    sigma_table = noise_levels(level_count)
    step_hot = (step_ids[:, None] == jnp.arange(level_count, dtype=jnp.int32)[None, :]).astype(jnp.float32)
    sigma = lax.optimization_barrier(jnp.sum(step_hot * sigma_table[None, :], axis=1))
    sigma_sq = sigma * sigma + 1.0
    scale_in = (1.0 / jnp.sqrt(sigma_sq))[:, None, None]
    scale_skip = (1.0 / sigma_sq)[:, None, None]
    scale_out = (sigma / jnp.sqrt(sigma_sq))[:, None, None]
    weight_loss = sigma_sq / (sigma * sigma)
    mean_float = mean_part.astype(jnp.float32)
    residual = target_part.astype(jnp.float32) - mean_float
    noisy = residual + sigma[:, None, None] * noise_part.astype(jnp.float32)
    inputs = jnp.concatenate([scale_in * noisy, mean_float], axis=1).astype(jnp.bfloat16)
    cols_in = columns(inputs, stride)
    embedded = lax.optimization_barrier(jnp.sum(step_hot[:, :, None] * step_embed[None, :, :], axis=1))
    pre_one = product('ok,bkp->bop', conv_one, cols_in) + embedded[:, :, None]
    act_one = jax.nn.silu(pre_one).astype(jnp.bfloat16)
    cols_one = columns(act_one, stride)
    pre_two = product('ok,bkp->bop', conv_two, cols_one)
    act_two = jax.nn.silu(pre_two).astype(jnp.bfloat16)
    output = product('co,bop->bcp', out_proj, act_two)
    error = scale_skip * noisy + scale_out * output - residual
    losses = weight_loss * lax.optimization_barrier(jnp.mean(error * error, axis=(1, 2))) * in_use
    factor = 2.0 * weight_loss * in_use / (error.shape[1] * error.shape[2])
    grad_output = (factor[:, None, None] * scale_out * error).astype(jnp.bfloat16)
    grad_proj = product('bcp,bop->co', grad_output, act_two)
    grad_act_two = product('co,bcp->bop', out_proj, grad_output)
    grad_pre_two = (grad_act_two * silu_slope(pre_two)).astype(jnp.bfloat16)
    grad_two = product('bop,bkp->ok', grad_pre_two, cols_one)
    grad_cols = product('ok,bop->bkp', conv_two, grad_pre_two)
    grad_act_one = fold(grad_cols, stride)
    grad_pre_one = (grad_act_one * silu_slope(pre_one)).astype(jnp.bfloat16)
    grad_one = product('bop,bkp->ok', grad_pre_one, cols_in)
    pixel_sums = lax.optimization_barrier(jnp.sum(grad_pre_one.astype(jnp.float32), axis=2))
    grad_table = lax.optimization_barrier(jnp.sum(step_hot[:, :, None] * pixel_sums[:, None, :], axis=0))
    return (losses, (grad_one, grad_two, grad_proj, grad_table))

def run_blocks(mean_part, target_part, noise_part, step_ids, in_use, weights):
    patch_count = mean_part.shape[0]
    blocks = patch_count // 4

    def regroup(values):
        return values.reshape((blocks, 4) + values.shape[1:])

    def advance(running, group_block):
        losses, gradients = patch_block(group_block[0], group_block[1], group_block[2], group_block[3], group_block[4], weights)
        summed = (running[0] + gradients[0], running[1] + gradients[1], running[2] + gradients[2], running[3] + gradients[3])
        return (summed, losses)
    initial = (jnp.zeros(weights[0].shape, jnp.float32), jnp.zeros(weights[1].shape, jnp.float32), jnp.zeros(weights[2].shape, jnp.float32), jnp.zeros(weights[3].shape, jnp.float32))
    stacked = (regroup(mean_part), regroup(target_part), regroup(noise_part), regroup(step_ids), regroup(in_use))
    gradients, losses = lax.scan(advance, initial, stacked)
    return (losses.reshape(patch_count), gradients)

def owner_tables(region_rows, strips):
    owners = region_rows[:, :, 2]
    owner_hot = (owners[:, :, None] == jnp.arange(strips, dtype=jnp.int32)[None, None, :]).astype(jnp.int32)
    pair_rank = lax.optimization_barrier(jnp.sum((jnp.cumsum(owner_hot, axis=1) - owner_hot) * owner_hot, axis=2))
    flat_hot = owner_hot.reshape(-1, strips)
    owner_slot = lax.optimization_barrier(jnp.sum((jnp.cumsum(flat_hot, axis=0) - flat_hot) * flat_hot, axis=1)).reshape(owners.shape)
    return (owners, pair_rank, owner_slot)

def reference(coarse, target, noise, regions, reg_conv, reg_out, conv_one, conv_two, out_proj, step_embed):
    weights = (conv_one, conv_two, out_proj, step_embed)
    strips = regions.shape[1]
    per_strip = regions.shape[2]
    means = []
    owner_rows = []
    totals = None
    zero_index = jnp.zeros((), jnp.int32)
    for sample in range(coarse.shape[0]):
        mean_grid = regress(coarse[sample], reg_conv, reg_out)
        pair_grid = jnp.stack([mean_grid, target[sample]])
        region_rows = regions[sample]
        owners, pair_rank, owner_slot = owner_tables(region_rows, strips)
        flat_regions = region_rows.reshape(strips * per_strip, 4)
        top_rows = jnp.arange(strips * per_strip, dtype=jnp.int32) // per_strip * PATCH + flat_regions[:, 0]

        def cut(row_at, col_at):
            piece = lax.dynamic_slice(pair_grid, (zero_index, zero_index, row_at.astype(jnp.int32), col_at.astype(jnp.int32)), (2, pair_grid.shape[1], PATCH, PATCH))
            return piece.reshape(2, pair_grid.shape[1], PATCH * PATCH)
        patches = jax.vmap(cut)(top_rows, flat_regions[:, 1])
        patch_noise = noise[sample][owners.reshape(-1), owner_slot.reshape(-1)]
        in_use = jnp.ones((strips * per_strip,), jnp.float32)
        losses, gradients = run_blocks(patches[:, 0], patches[:, 1], patch_noise, flat_regions[:, 3], in_use, weights)
        owner_hot = (owners.reshape(-1)[:, None] == jnp.arange(strips, dtype=jnp.int32)[None, :]).astype(jnp.float32)
        owner_rows.append(lax.optimization_barrier(jnp.sum(owner_hot * losses[:, None], axis=0)))
        means.append(mean_grid)
        if totals is None:
            totals = gradients
        else:
            totals = (totals[0] + gradients[0], totals[1] + gradients[1], totals[2] + gradients[2], totals[3] + gradients[3])
    return (jnp.stack(means), jnp.stack(owner_rows), totals[0], totals[1], totals[2], totals[3])
```

```python
import functools
import math

import jax
import jax.numpy as jnp
from jax import lax
from jax.experimental import pallas as pl
from jax.experimental.pallas import tpu as pltpu
from jax.sharding import PartitionSpec as P

BF = jnp.bfloat16
F32 = jnp.float32
TAPS = tuple((a, b) for a in (-1, 0, 1) for b in (-1, 0, 1))
NT_FORM = (((1,), (1,)), ((), ()))
TN_FORM = (((0,), (0,)), ((), ()))
LIMIT = 48 * 1024 * 1024


def matmul(left, right):
    return jnp.dot(left, right, preferred_element_type=F32)


def whole(shape):
    return pl.BlockSpec(memory_space=pltpu.VMEM)


VM = pl.BlockSpec(memory_space=pltpu.VMEM)
SM = pl.BlockSpec(memory_space=pltpu.SMEM)


def call(kernel, outs, ins, specs, scratch=(), cost=0):
    return pl.pallas_call(
        kernel,
        out_shape=outs,
        in_specs=list(specs),
        out_specs=jax.tree.map(lambda _: VM, outs),
        scratch_shapes=list(scratch),
        compiler_params=pltpu.CompilerParams(vmem_limit_bytes=LIMIT),
        cost_estimate=pl.CostEstimate(flops=cost, bytes_accessed=1 << 20, transcendentals=0),
    )(*ins)


def pack_kernel(slots_ref, noise_ref, *out_refs):
    channels, cells = noise_ref.shape[1:]
    half = cells // 2
    row = lax.broadcasted_iota(jnp.int32, (half, cells), 0)
    col = lax.broadcasted_iota(jnp.int32, (half, cells), 1)
    even = (col == 2 * row).astype(BF)
    odd = (col == 2 * row + 1).astype(BF)
    low = lax.broadcasted_iota(jnp.int32, (half, 2 * channels), 1) < channels
    per = out_refs[0].shape[0]
    for index, out_ref in enumerate(out_refs):

        def pair(j, carry, index=index, out_ref=out_ref):
            one = noise_ref[slots_ref[index * per + 2 * j]]
            two = noise_ref[slots_ref[index * per + 2 * j + 1]]
            both = jnp.concatenate([one, two], axis=0)
            first = lax.dot_general(even, both, NT_FORM, preferred_element_type=F32)
            second = lax.dot_general(odd, both, NT_FORM, preferred_element_type=F32)
            out_ref[2 * j] = jnp.where(low, first, pltpu.roll(second, channels, 1)).astype(BF)
            out_ref[2 * j + 1] = jnp.where(low, pltpu.roll(first, channels, 1), second).astype(BF)
            return carry

        lax.fori_loop(0, per // 2, pair, 0, unroll=min(4, per // 2))


def regress_kernel(above_ref, own_ref, below_ref, conv_ref, proj_ref, mean_ref, cols_ref):
    rows, channels, width = own_ref.shape
    deep = cols_ref.shape[1] // 3
    cols_ref[...] = jnp.zeros(cols_ref.shape, BF)
    lane = lax.broadcasted_iota(jnp.int32, (channels, width), 1)

    def put(at, cells):
        wide = cells.astype(F32)
        left = jnp.where(lane == 0, 0.0, pltpu.roll(wide, 1, 1)).astype(BF)
        right = jnp.where(lane == width - 1, 0.0, pltpu.roll(wide, width - 1, 1)).astype(BF)
        cols_ref[at, 0:channels] = left
        cols_ref[at, deep : deep + channels] = cells
        cols_ref[at, 2 * deep : 2 * deep + channels] = right

    put(0, above_ref[0])
    put(rows + 1, below_ref[0])

    def fill(r, carry):
        put(r + 1, own_ref[r])
        return carry

    lax.fori_loop(0, rows, fill, 0)

    def one(r, carry):
        stack = cols_ref[pl.ds(r, 3)].reshape(9 * deep, width)
        hidden = matmul(conv_ref[...], stack)
        act = (hidden * jax.nn.sigmoid(hidden)).astype(BF)
        mean_ref[r] = matmul(proj_ref[...], act).astype(BF)
        return carry

    lax.fori_loop(0, rows, one, 0, unroll=2)


def gather_kernel(
    row_ref, col_ref, mean_ref, mean_low_ref, tgt_ref, tgt_low_ref, mp_ref, tp_ref, img_m, img_t, got_m, got_t
):
    rows, channels, width = mean_ref.shape
    chunks, _, count, _ = mp_ref.shape
    pairs = rows // 2
    eye = (
        lax.broadcasted_iota(jnp.int32, (width, width), 0)
        == lax.broadcasted_iota(jnp.int32, (width, width), 1)
    ).astype(BF)

    def paint(cells, img, at):
        after = pltpu.roll(cells.astype(F32), width - 1, 1).astype(BF)
        both = jnp.concatenate([cells, after], axis=0)
        img[at] = lax.dot_general(eye, both, NT_FORM, preferred_element_type=F32)

    def own(r, carry):
        paint(mean_ref[r], img_m, r)
        paint(tgt_ref[r], img_t, r)
        return carry

    def low(r, carry):
        paint(mean_low_ref[r], img_m, rows + r)
        paint(tgt_low_ref[r], img_t, rows + r)
        return carry

    lax.fori_loop(0, rows, own, 0)
    lax.fori_loop(0, rows - 1, low, 0)
    for chunk in range(chunks):

        def patch(k, carry, chunk=chunk):
            top = row_ref[chunk * count + k]
            left = col_ref[chunk * count + k]
            for r in range(rows):
                for img, got in ((img_m, got_m), (img_t, got_t)):
                    got[pl.ds(r * pairs * count + k, pairs, stride=count), :] = img[
                        top + r, pl.ds(left, pairs, stride=2), :
                    ]
            return carry

        lax.fori_loop(0, count, patch, 0)
        mp_ref[chunk] = got_m[...].astype(BF).reshape(mp_ref.shape[1:])
        tp_ref[chunk] = got_t[...].astype(BF).reshape(tp_ref.shape[1:])


def chunk_kernel(
    chunk,
    last,
    phases,
    *refs,
):
    source_ref, phase_ref, step_ref = refs[:3]
    noise_refs = refs[3 : 3 + phases]
    refs = refs[3 + phases :]
    (mp_ref, tp_ref, fac_ref, embed_ref, w1_ref, w2_ref, v2_ref, po_ref, pg_ref) = refs[:9]
    refs = refs[9:]
    before = None
    if chunk > 0:
        before, refs = refs[0], refs[1:]
    out_ref, loss_ref = refs[:2]
    (nz, xn, xm, x2n, x2m, e1, o1, e2, o2, slope1, res, noisy, act2, gout, gt, emb) = refs[2:]
    _, cells, count, wide = mp_ref.shape
    rows = 12
    pairs = cells // rows
    total = cells * count
    group = 4
    half = wide // 2

    for ref in (xn, xm, e1, o1, e2, o2):
        ref[...] = jnp.zeros(ref.shape, BF)
    for k in range(count):
        at = source_ref[chunk * count + k]
        piece = noise_refs[0][at]
        if phases > 1:
            piece = jnp.where(phase_ref[chunk * count + k] == 0, piece, noise_refs[1][at])
        nz[pl.ds(k, cells, stride=count), :] = piece.astype(F32)
        emb[pl.ds(k, 1), :] = embed_ref[pl.ds(step_ref[chunk * count + k], 1), :]

    def spread(index):
        return fac_ref[index][None]

    scale_in, sigma, skip, scale_out, grad_scale = (spread(i) for i in range(5))
    lane = lax.broadcasted_iota(jnp.int32, (1, 1, count, wide), 3)

    mean_bf = mp_ref[0]
    mean = mean_bf.astype(F32)
    residual = tp_ref[0].astype(F32) - mean
    noised = residual + sigma * nz[...].reshape(cells, count, wide)
    res[...] = residual.reshape(total, wide)
    noisy[...] = noised.reshape(total, wide)
    xn[1 : rows + 1, 1 : pairs + 1] = (scale_in * noised).astype(BF).reshape(rows, pairs, count, wide)
    xm[1 : rows + 1, 1 : pairs + 1] = mean_bf.reshape(rows, pairs, count, wide)
    for src, dst in ((xn, x2n), (xm, x2m)):
        dst[...] = jnp.where(
            lane < half, src[:, 2 : pairs + 2].astype(F32), src[:, 0:pairs].astype(F32)
        ).astype(BF)

    def view(ref, at, many, p0):
        return ref[at : at + many, p0 : p0 + pairs].reshape(many * pairs * count, wide)

    def stack_in(at, many):
        return [view(xn, at, many, 1), view(xm, at, many, 1), view(x2n, at, many, 0), view(x2m, at, many, 0)]

    def stack_eo(even, odd, at, many):
        return [view(even, at, many, 1), view(odd, at, many, 1), view(odd, at, many, 0), view(even, at, many, 2)]

    def shape4(value, many):
        return value.reshape(many, pairs, count, value.shape[-1])

    tile = group * pairs * count
    emb_pair = jnp.concatenate([emb[...], emb[...]], axis=1)[None]
    for r in range(0, rows, group):
        left = jnp.concatenate(sum([stack_in(r + a, group) for a in range(3)], []), axis=1)
        pre = matmul(left, w1_ref[...]).reshape(group * pairs, count, 2 * wide) + emb_pair
        gate = jax.nn.sigmoid(pre)
        act = (pre * gate).astype(BF)
        slope1[r * pairs * count : r * pairs * count + tile, :] = (
            gate * (1.0 + pre * (1.0 - gate))
        ).reshape(tile, 2 * wide)
        act = shape4(act, group)
        e1[r + 1 : r + 1 + group, 1 : pairs + 1] = act[..., :wide]
        o1[r + 1 : r + 1 + group, 1 : pairs + 1] = act[..., wide:]

    loss = jnp.zeros((count, wide), F32)
    for r in range(0, rows, group):
        span = pl.ds(r * pairs * count, tile)
        left = jnp.concatenate(sum([stack_eo(e1, o1, r + a, group) for a in range(3)], []), axis=1)
        pre = matmul(left, w2_ref[...])
        gate = jax.nn.sigmoid(pre)
        act = (pre * gate).astype(BF)
        slope = gate * (1.0 + pre * (1.0 - gate))
        act2[span, :] = act
        output = matmul(act, po_ref[...]).reshape(group * pairs, count, wide)
        error = (
            skip * noisy[span, :].reshape(group * pairs, count, wide)
            + scale_out * output
            - res[span, :].reshape(group * pairs, count, wide)
        )
        loss = loss + jnp.sum(error * error, axis=0)
        grad_output = (grad_scale * error).astype(BF).reshape(tile, wide)
        gout[span, :] = grad_output
        grad_pre = (matmul(grad_output, pg_ref[...]) * slope).astype(BF)
        grad_pre = shape4(grad_pre, group)
        e2[r + 1 : r + 1 + group, 1 : pairs + 1] = grad_pre[..., :wide]
        o2[r + 1 : r + 1 + group, 1 : pairs + 1] = grad_pre[..., wide:]
    loss_ref[...] = loss

    def emit(at, size, value):
        if before is not None:
            value = value + before[at : at + size, :]
        out_ref[at : at + size, :] = value

    depth = wide
    proj = lax.dot_general(gout[...], act2[...], TN_FORM, preferred_element_type=F32)
    emit(18 * depth, half, proj[:half, :wide] + proj[half:, wide:])

    gt[0:depth, :] = jnp.transpose(view(e2, 1, rows, 1))
    gt[depth : 2 * depth, :] = jnp.transpose(view(o2, 1, rows, 1))
    for a in range(3):
        right = jnp.concatenate(stack_eo(e1, o1, a, rows), axis=1)
        got = matmul(gt[...], right)
        h0, h1 = got[:depth], got[depth:]
        base = 9 * depth + 3 * a * depth
        emit(base, depth, h1[:, 0:wide] + h0[:, 2 * wide : 3 * wide])
        emit(base + depth, depth, h0[:, 0:wide] + h1[:, wide : 2 * wide])
        emit(base + 2 * depth, depth, h0[:, wide : 2 * wide] + h1[:, 3 * wide : 4 * wide])

    sums = jnp.zeros((count, 2 * wide), F32)
    for r in range(0, rows, group):
        span = pl.ds(r * pairs * count, tile)
        left = jnp.concatenate(sum([stack_eo(e2, o2, r + a, group) for a in range(3)], []), axis=1)
        grad = (matmul(left, v2_ref[...]) * slope1[span, :]).astype(BF)
        sums = sums + jnp.sum(grad.astype(F32).reshape(group * pairs, count, 2 * wide), axis=0)
        act2[span, :] = grad
    emb[...] = sums[:, :wide] + sums[:, wide:]
    table = 18 * depth + half
    levels = embed_ref.shape[0]
    if before is not None:
        out_ref[table : table + levels, :] = before[table : table + levels, :]
    else:
        out_ref[table : table + levels, :] = jnp.zeros((levels, wide), F32)
    for k in range(count):
        at = table + step_ref[chunk * count + k]
        out_ref[pl.ds(at, 1), :] = out_ref[pl.ds(at, 1), :] + emb[pl.ds(k, 1), :]

    gt[...] = jnp.transpose(act2[...])
    low = lax.broadcasted_iota(jnp.int32, (depth, wide), 1) < half
    for a in range(3):
        right = jnp.concatenate(stack_in(a, rows), axis=1)
        got = matmul(gt[...], right)
        h0, h1 = got[:depth], got[depth:]

        def merged(first, second):
            n = first[:, 0:wide], second[:, 0:wide]
            m = first[:, wide:], second[:, wide:]
            noise_part = n[0] + pltpu.roll(n[1], half, 1)
            mean_part = pltpu.roll(m[0], half, 1) + m[1]
            return jnp.where(low, noise_part, mean_part)

        base = 3 * a * depth
        direct, rim = slice(0, 2 * wide), slice(2 * wide, 4 * wide)
        emit(base, depth, merged(h1[:, direct], h0[:, rim]))
        emit(base + depth, depth, merged(h0[:, direct], h1[:, direct]))
        emit(base + 2 * depth, depth, merged(h1[:, rim], h0[:, direct]))


def pair_weights(taps, split):
    zero = jnp.zeros_like(taps[0][0])
    blocks = []
    for a in range(3):
        low, mid, high = taps[a]

        def rows_of(first, second):
            if not split:
                return [first, second]
            half = first.shape[0] // 2
            return [first[:half], second[:half], first[half:], second[half:]]

        even = jnp.concatenate([mid, low], axis=1)
        odd = jnp.concatenate([high, mid], axis=1)
        before = jnp.concatenate([low, zero], axis=1)
        after = jnp.concatenate([zero, high], axis=1)
        blocks += rows_of(even, odd)
        blocks += rows_of(after, before) if split else rows_of(before, after)
    return jnp.concatenate(blocks, axis=0)


def forward_weights(conv, split):
    depth = conv.shape[1] // 9
    cut = [conv[:, i * depth : (i + 1) * depth].T for i in range(9)]
    return pair_weights([cut[0:3], cut[3:6], cut[6:9]], split)


def backward_weights(conv):
    depth = conv.shape[1] // 9
    cut = [conv[:, (8 - i) * depth : (9 - i) * depth] for i in range(9)]
    return pair_weights([cut[0:3], cut[3:6], cut[6:9]], False)


def by_distance(axis, distance):
    return [(i, i ^ distance) for i in range(lax.axis_size(axis))]


def rounded_to_bf16(values):
    return lax.reduce_precision(values, 8, 7)


def take(pieces, index):
    return lax.dynamic_index_in_dim(pieces, index, 0, keepdims=False)


def scatter_sum(values, axis):
    n = values.shape[0]
    me = lax.axis_index(axis)
    out = take(values, me)
    arrived = [
        lax.ppermute(take(values, me ^ d).astype(BF), axis, by_distance(axis, d)) for d in range(1, n)
    ]
    for piece in arrived:
        out = out + piece.astype(F32)
    return out


def gather_all(piece, axis):
    n = lax.axis_size(axis)
    me = lax.axis_index(axis)
    found = [piece] + [lax.ppermute(piece, axis, by_distance(axis, d)) for d in range(1, n)]
    return jnp.stack([sum_select(found, me, i) for i in range(n)])


def sum_select(found, me, index):
    out = found[0]
    for d in range(1, len(found)):
        out = jnp.where((me ^ d) == index, found[d], out)
    return out


def rows_sum(piece, axis):
    n = lax.axis_size(axis)
    if n > 4:
        return lax.psum(piece, axis)
    values = [rounded_to_bf16(piece).astype(BF)]
    for d in range(1, n):
        values.append(lax.ppermute(values[0], axis, by_distance(axis, d)))
    values = [v.astype(F32) for v in values]
    while len(values) > 1:
        values = [values[i] + values[i + 1] for i in range(0, len(values), 2)]
    return values[0]


def per_device(coarse, target, noise, regions, reg_conv, reg_out, conv_one, conv_two, out_proj, step_embed):
    strips = lax.axis_size("rows")
    me = lax.axis_index("rows")
    region = regions[0]
    per_strip = region.shape[1]
    most = noise.shape[2]
    capacity = max(2, (2 * per_strip + strips - 1) // strips)
    phases = 2
    deep = capacity // phases
    count = per_strip // phases
    exchange = strips <= 4
    channels = target.shape[1]
    height, width = target.shape[2:]
    cells = height * height
    wide = 2 * channels
    depth = conv_one.shape[0]
    levels = step_embed.shape[0]

    down = [(i + 1, i) for i in range(strips - 1)]
    up = [(i, i + 1) for i in range(strips - 1)]
    own_target = jnp.transpose(target[0], (1, 0, 2))
    own_coarse = jnp.transpose(coarse[0], (1, 0, 2))
    target_low = lax.ppermute(own_target[: height - 1], "rows", down)
    coarse_above = lax.ppermute(own_coarse[height - 1 :], "rows", up)
    coarse_below = lax.ppermute(own_coarse[:1], "rows", down)

    ids = jnp.arange(strips, dtype=jnp.int32)
    owners = region[:, :, 2]
    mine = jnp.sum((owners == me).astype(jnp.int32), axis=1)
    starts = jnp.sum(jnp.where(ids[:, None] > ids[None, :], mine[None, :], 0), axis=1)
    distances = ids
    goal = (ids ^ me) if exchange else ids
    goal_start = jnp.sum(jnp.where(goal[:, None] == ids[None, :], starts[None, :], 0), axis=1)
    rank = jnp.arange(capacity, dtype=jnp.int32).reshape(phases, 1, deep)
    slots = jnp.minimum(goal_start[None, :, None] + rank, most - 1).reshape(-1)

    own = lax.dynamic_index_in_dim(region, me, 0, keepdims=False)
    owner = own[:, 2]
    entry = jnp.arange(per_strip, dtype=jnp.int32)
    earlier = entry[None, :] < entry[:, None]
    pair_rank = jnp.sum(((owner[:, None] == owner[None, :]) & earlier).astype(jnp.int32), axis=1)
    early = pair_rank < deep
    early_before = jnp.sum((early[None, :] & earlier).astype(jnp.int32), axis=1)
    first = early & (early_before < count)
    first_before = jnp.sum((first[None, :] & earlier).astype(jnp.int32), axis=1)
    place = jnp.where(first, first_before, count + entry - first_before)
    place_hot = place[None, :] == entry[:, None]

    def ordered(field):
        return jnp.sum(jnp.where(place_hot, field[None, :], 0), axis=1)

    source = ordered(((owner ^ me) if exchange else owner) * deep + pair_rank % deep)
    phase = ordered(pair_rank // deep)
    top, left, step, owner_in_order = (ordered(own[:, i]) for i in (0, 1, 3, 2))

    sigma = 0.1 * jnp.exp(step.astype(F32) * (math.log(100.0) / (levels - 1)))
    u = sigma * sigma + 1.0
    weight = u / (sigma * sigma)
    scale_out = sigma / jnp.sqrt(u)
    grad_scale = 2.0 * weight / (channels * cells) * scale_out
    factors = jnp.stack([1.0 / jnp.sqrt(u), sigma, 1.0 / u, scale_out, grad_scale])
    factors = jnp.broadcast_to(factors[:, :, None], (5, per_strip, wide))

    slot_shape = (cells // 2, wide)
    pieces = phases * strips if exchange else phases
    packed = call(
        pack_kernel,
        [jax.ShapeDtypeStruct((phases * strips * deep // pieces,) + slot_shape, BF)] * pieces,
        (slots, noise[0, 0]),
        (SM, VM),
    )
    arrived = []
    for f in range(phases):
        if exchange:
            parts = [packed[f * strips]]
            for d in range(1, strips):
                parts.append(lax.ppermute(packed[f * strips + d], "rows", by_distance("rows", d)))
            arrived.append(jnp.concatenate(parts, axis=0))
        else:
            arrived.append(lax.all_to_all(packed[f], "rows", 0, 0, tiled=True))

    fill = -(-reg_conv.shape[1] // 9 // 16) * 16
    per_tap = reg_conv.shape[1] // 9
    reg_taps = jnp.pad(reg_conv.reshape(-1, 9, per_tap), ((0, 0), (0, 0), (0, fill - per_tap)))
    mean = call(
        regress_kernel,
        jax.ShapeDtypeStruct((height, channels, width), BF),
        (coarse_above, own_coarse, coarse_below, reg_taps.reshape(-1, 9 * fill), reg_out),
        (VM,) * 5,
        [pltpu.VMEM((height + 2, 3 * fill, width), BF)],
    )
    mean_low = lax.ppermute(mean[: height - 1], "rows", down)
    patch_shape = jax.ShapeDtypeStruct((phases, cells // 2, count, wide), BF)
    mean_p, target_p = call(
        gather_kernel,
        [patch_shape, patch_shape],
        (top, left, mean, mean_low, own_target, target_low),
        (SM, SM) + (VM,) * 4,
        [pltpu.VMEM((2 * height - 1, width, wide), F32)] * 2 + [pltpu.VMEM((cells // 2 * count, wide), F32)] * 2,
    )

    weights_one = forward_weights(conv_one, True)
    weights_two = forward_weights(conv_two, False)
    weights_back = backward_weights(conv_two)
    zero = jnp.zeros_like(out_proj)
    proj_back = jnp.concatenate(
        [jnp.concatenate([out_proj, zero], axis=1), jnp.concatenate([zero, out_proj], axis=1)], axis=0
    )
    proj_out = proj_back.T

    total = cells // 2 * count
    rows_used = 18 * depth + channels + levels
    table = None
    losses = []
    for chunk in range(phases):
        pad = pltpu.VMEM((height + 2, height // 2 + 2, count, wide), BF)
        rim = pltpu.VMEM((height + 2, height // 2, count, wide), BF)
        ins = (source, phase, step) + tuple(arrived[: chunk + 1])
        ins += (mean_p[chunk : chunk + 1], target_p[chunk : chunk + 1])
        ins += (factors[:, chunk * count : (chunk + 1) * count], step_embed)
        ins += (weights_one, weights_two, weights_back, proj_out, proj_back)
        ins += (table,) if chunk > 0 else ()
        table, loss = call(
            functools.partial(chunk_kernel, chunk, chunk == phases - 1, chunk + 1),
            [jax.ShapeDtypeStruct((rows_used, wide), F32), jax.ShapeDtypeStruct((count, wide), F32)],
            ins,
            (SM,) * 3 + (VM,) * (len(ins) - 3),
            [
                pltpu.VMEM((total, wide), F32),
                pad,
                pad,
                rim,
                rim,
                pad,
                pad,
                pad,
                pad,
                pltpu.VMEM((total, 2 * wide), F32),
                pltpu.VMEM((total, wide), F32),
                pltpu.VMEM((total, wide), F32),
                pltpu.VMEM((total, 2 * wide), BF),
                pltpu.VMEM((total, wide), BF),
                pltpu.VMEM((2 * wide, total), BF),
                pltpu.VMEM((count, wide), F32),
            ],
        )
        losses.append(loss)

    patch_loss = weight * (jnp.sum(jnp.concatenate(losses), axis=1) / (channels * cells))
    by_owner = jnp.sum(jnp.where(owner_in_order[None, :] == ids[:, None], patch_loss[None, :], 0.0), axis=1)
    samples = lax.axis_size("segment") * lax.axis_size("dp")
    sample = lax.axis_index("segment") * lax.axis_size("dp") + lax.axis_index("dp")
    spread = jnp.where(jnp.arange(samples)[:, None] == sample, by_owner[None, :], 0.0).reshape(-1)
    loss_rows = -(-samples * strips // wide)
    spread = jnp.pad(spread, (0, loss_rows * wide - samples * strips)).reshape(loss_rows, wide)
    coarse_part = rounded_to_bf16(spread)
    unit = 2 * lax.axis_size("dp") * 16
    rows_all = -(-(rows_used + 2 * loss_rows) // unit) * unit
    table = jnp.concatenate(
        [
            table,
            coarse_part,
            spread - coarse_part,
            jnp.zeros((rows_all - rows_used - 2 * loss_rows, wide), F32),
        ],
        axis=0,
    )

    cores, groups = lax.axis_size("segment"), lax.axis_size("dp")
    kept = scatter_sum(table.reshape(cores, rows_all // cores, wide), "segment")
    kept = scatter_sum(kept.reshape(groups, rows_all // cores // groups, wide), "dp")
    kept = rows_sum(kept, "rows")
    piece_rows = rows_all // cores // groups
    ending = (lax.axis_index("segment") == cores - 1) & (lax.axis_index("dp") == groups - 1)
    at = rows_used - (rows_all - piece_rows)
    exact = kept[at : at + loss_rows] + kept[at + loss_rows : at + 2 * loss_rows]
    rounded = rounded_to_bf16(exact)
    pair = jnp.concatenate([rounded, exact - rounded], axis=0)
    pair = jnp.where(ending, pair, kept[at : at + 2 * loss_rows])
    kept = rounded_to_bf16(lax.dynamic_update_slice_in_dim(kept, pair, at, 0)).astype(BF)
    kept = gather_all(kept, "dp").reshape(rows_all // cores, wide)
    table = gather_all(kept, "segment").reshape(rows_all, wide).astype(F32)

    def assembled(at):
        block = table[at : at + 9 * depth].reshape(9, depth, wide)
        return jnp.transpose(block, (1, 0, 2)).reshape(depth, 9 * wide)

    loss_table = (
        table[rows_used : rows_used + loss_rows] + table[rows_used + loss_rows : rows_used + 2 * loss_rows]
    ).reshape(-1)
    owner_loss = lax.dynamic_slice_in_dim(loss_table, sample * strips + me, 1).reshape(1, 1)
    return (
        jnp.transpose(mean, (1, 0, 2))[None],
        owner_loss,
        assembled(0),
        assembled(9 * depth),
        table[18 * depth : 18 * depth + channels],
        table[18 * depth + channels : rows_used],
    )


def solution(mesh):
    placed = (
        P(("segment", "dp"), None, "rows", None),
        P(("segment", "dp"), None, "rows", None),
        P(("segment", "dp"), "rows", None, None, None),
        P(("segment", "dp"), None, None, None),
        P(),
        P(),
        P(),
        P(),
        P(),
        P(),
    )
    return jax.shard_map(
        per_device,
        mesh=mesh,
        in_specs=placed,
        out_specs=(
            P(("segment", "dp"), None, "rows", None),
            P(("segment", "dp"), "rows"),
            P(),
            P(),
            P(),
            P(),
        ),
        check_vma=False,
    )
```

```python
import functools
import math

import jax
import jax.numpy as jnp
from jax import lax
from jax.experimental import pallas as pl
from jax.experimental.pallas import tpu as pltpu
from jax.sharding import PartitionSpec as P

BF = jnp.bfloat16
F32 = jnp.float32
TAPS = tuple((a, b) for a in (-1, 0, 1) for b in (-1, 0, 1))
NT_FORM = (((1,), (1,)), ((), ()))
TN_FORM = (((0,), (0,)), ((), ()))
MIB = 1024 * 1024


def matmul(left, right):
    return jnp.dot(left, right, preferred_element_type=F32)


VM = pl.BlockSpec(memory_space=pltpu.VMEM)
SM = pl.BlockSpec(memory_space=pltpu.SMEM)


def call(kernel, outs, ins, specs, scratch=(), cost=0, limit=32):
    return pl.pallas_call(
        kernel,
        out_shape=outs,
        in_specs=list(specs),
        out_specs=jax.tree.map(lambda _: VM, outs),
        scratch_shapes=list(scratch),
        compiler_params=pltpu.CompilerParams(vmem_limit_bytes=limit * MIB),
        cost_estimate=pl.CostEstimate(flops=cost, bytes_accessed=1 << 20, transcendentals=0),
    )(*ins)


def after(values, others):
    return lax.optimization_barrier((values, others))[0]


def pack_kernel(slots_ref, noise_ref, *out_refs):
    channels, cells = noise_ref.shape[1:]
    half = cells // 2
    row = lax.broadcasted_iota(jnp.int32, (half, cells), 0)
    col = lax.broadcasted_iota(jnp.int32, (half, cells), 1)
    even = (col == 2 * row).astype(BF)
    odd = (col == 2 * row + 1).astype(BF)
    low = lax.broadcasted_iota(jnp.int32, (half, 2 * channels), 1) < channels
    per = out_refs[0].shape[0]
    for index, out_ref in enumerate(out_refs):

        def pair(j, carry, index=index, out_ref=out_ref):
            one = noise_ref[slots_ref[index * per + 2 * j]]
            two = noise_ref[slots_ref[index * per + 2 * j + 1]]
            both = jnp.concatenate([one, two], axis=0)
            first = lax.dot_general(even, both, NT_FORM, preferred_element_type=F32)
            second = lax.dot_general(odd, both, NT_FORM, preferred_element_type=F32)
            out_ref[2 * j] = jnp.where(low, first, pltpu.roll(second, channels, 1)).astype(BF)
            out_ref[2 * j + 1] = jnp.where(low, pltpu.roll(first, channels, 1), second).astype(BF)
            return carry

        lax.fori_loop(0, per // 2, pair, 0, unroll=min(4, per // 2))


def regress_kernel(above_ref, own_ref, below_ref, conv_ref, proj_ref, mean_ref, top_ref, cols_ref, taps_ref):
    rows, channels, width = own_ref.shape
    deep = cols_ref.shape[1] // 3
    cols_ref[...] = jnp.zeros(cols_ref.shape, BF)
    taps_ref[...] = jnp.zeros(taps_ref.shape, BF)
    for tap in range(9):
        taps_ref[tap * deep : tap * deep + channels] = (
            conv_ref[tap * channels : (tap + 1) * channels].astype(F32).astype(BF)
        )
    taps = jnp.transpose(taps_ref[...])
    lane = lax.broadcasted_iota(jnp.int32, (channels, width), 1)

    def put(at, cells):
        wide = cells.astype(F32)
        left = jnp.where(lane == 0, 0.0, pltpu.roll(wide, 1, 1)).astype(BF)
        right = jnp.where(lane == width - 1, 0.0, pltpu.roll(wide, width - 1, 1)).astype(BF)
        cols_ref[at, 0:channels] = left
        cols_ref[at, deep : deep + channels] = cells
        cols_ref[at, 2 * deep : 2 * deep + channels] = right

    put(0, above_ref[0])
    put(rows + 1, below_ref[0])

    def fill(r, carry):
        put(r + 1, own_ref[r])
        return carry

    lax.fori_loop(0, rows, fill, 0)

    def one(r, carry):
        stack = cols_ref[pl.ds(r, 3)].reshape(9 * deep, width)
        hidden = matmul(taps, stack)
        act = (hidden * jax.nn.sigmoid(hidden)).astype(BF)
        mean_ref[r] = matmul(proj_ref[...], act).astype(BF)
        return carry

    lax.fori_loop(0, rows, one, 0, unroll=2)
    top_ref[...] = mean_ref[0 : rows - 1]


def painter(width):
    eye = (
        lax.broadcasted_iota(jnp.int32, (width, width), 0)
        == lax.broadcasted_iota(jnp.int32, (width, width), 1)
    ).astype(BF)

    def paint(cells):
        following = pltpu.roll(cells.astype(F32), width - 1, 1).astype(BF)
        both = jnp.concatenate([cells, following], axis=0)
        return lax.dot_general(eye, both, NT_FORM, preferred_element_type=F32)

    return paint


def paint_kernel(mean_ref, tgt_ref, img_m, img_t):
    paint = painter(mean_ref.shape[2])

    def one(r, carry):
        img_m[r] = paint(mean_ref[r]).astype(BF)
        img_t[r] = paint(tgt_ref[r]).astype(BF)
        return carry

    lax.fori_loop(0, mean_ref.shape[0], one, 0, unroll=2)


def gather_kernel(
    row_ref, col_ref, own_m, own_t, mean_low_ref, tgt_low_ref, mp_ref, tp_ref, img_m, img_t, got_m, got_t
):
    rows = own_m.shape[0]
    chunks, _, count, _ = mp_ref.shape
    pairs = rows // 2
    paint = painter(own_m.shape[1])
    img_m[0:rows] = own_m[...].astype(F32)
    img_t[0:rows] = own_t[...].astype(F32)

    def low(r, carry):
        img_m[rows + r] = paint(mean_low_ref[r])
        img_t[rows + r] = paint(tgt_low_ref[r])
        return carry

    lax.fori_loop(0, rows - 1, low, 0)
    for chunk in range(chunks):

        def patch(k, carry, chunk=chunk):
            top = row_ref[chunk * count + k]
            left = col_ref[chunk * count + k]
            for r in range(rows):
                for img, got in ((img_m, got_m), (img_t, got_t)):
                    got[pl.ds(r * pairs * count + k, pairs, stride=count), :] = img[
                        top + r, pl.ds(left, pairs, stride=2), :
                    ]
            return carry

        lax.fori_loop(0, count, patch, 0)
        mp_ref[chunk] = got_m[...].astype(BF).reshape(mp_ref.shape[1:])
        tp_ref[chunk] = got_t[...].astype(BF).reshape(tp_ref.shape[1:])


def chunk_kernel(chunk, last, pieces, *refs):
    source_ref, step_ref, place_ref = refs[:3]
    noise_refs = refs[3 : 3 + pieces]
    refs = refs[3 + pieces :]
    (mp_ref, tp_ref, fac_ref, embed_ref, w1_ref, w2_ref, v2_ref, po_ref, pg_ref) = refs[:9]
    refs = refs[9:]
    before = None
    if chunk > 0:
        before, refs = refs[0], refs[1:]
    if last:
        keep_ref, send_ref, out_ref = refs[:3]
        refs = refs[3:]
    else:
        out_ref, refs = refs[0], refs[1:]
    (stage, nz, xn, xm, x2n, x2m, e1, o1, e2, o2, slope1, res, noisy, act2, gout, gt, emb) = refs
    _, cells, count, wide = mp_ref.shape
    rows = 12
    pairs = cells // rows
    total = cells * count
    group = 4
    half = wide // 2

    for ref in (xn, xm, e1, o1, e2, o2):
        ref[...] = jnp.zeros(ref.shape, BF)
    at = 0
    for ref in noise_refs:
        stage[at : at + ref.shape[0]] = ref[...]
        at += ref.shape[0]
    for k in range(count):
        piece = stage[source_ref[chunk * count + k]]
        nz[pl.ds(k, cells, stride=count), :] = piece.astype(F32)
        emb[pl.ds(k, 1), :] = embed_ref[pl.ds(step_ref[chunk * count + k], 1), :]

    def spread(index):
        return fac_ref[index][None]

    scale_in, sigma, skip, scale_out, grad_scale = (spread(i) for i in range(5))
    lane = lax.broadcasted_iota(jnp.int32, (1, 1, count, wide), 3)

    mean_bf = mp_ref[0]
    mean = mean_bf.astype(F32)
    residual = tp_ref[0].astype(F32) - mean
    noised = residual + sigma * nz[...].reshape(cells, count, wide)
    res[...] = residual.reshape(total, wide)
    noisy[...] = noised.reshape(total, wide)
    xn[1 : rows + 1, 1 : pairs + 1] = (scale_in * noised).astype(BF).reshape(rows, pairs, count, wide)
    xm[1 : rows + 1, 1 : pairs + 1] = mean_bf.reshape(rows, pairs, count, wide)
    for src, dst in ((xn, x2n), (xm, x2m)):
        dst[...] = jnp.where(
            lane < half, src[:, 2 : pairs + 2].astype(F32), src[:, 0:pairs].astype(F32)
        ).astype(BF)

    def view(ref, at, many, p0):
        return ref[at : at + many, p0 : p0 + pairs].reshape(many * pairs * count, wide)

    def stack_in(at, many):
        return [view(xn, at, many, 1), view(xm, at, many, 1), view(x2n, at, many, 0), view(x2m, at, many, 0)]

    def stack_eo(even, odd, at, many):
        return [view(even, at, many, 1), view(odd, at, many, 1), view(odd, at, many, 0), view(even, at, many, 2)]

    def shape4(value, many):
        return value.reshape(many, pairs, count, value.shape[-1])

    tile = group * pairs * count
    emb_pair = jnp.concatenate([emb[...], emb[...]], axis=1)[None]
    for r in range(0, rows, group):
        left = jnp.concatenate(sum([stack_in(r + a, group) for a in range(3)], []), axis=1)
        pre = matmul(left, w1_ref[...]).reshape(group * pairs, count, 2 * wide) + emb_pair
        gate = jax.nn.sigmoid(pre)
        act = (pre * gate).astype(BF)
        slope1[r * pairs * count : r * pairs * count + tile, :] = (
            gate * (1.0 + pre * (1.0 - gate))
        ).reshape(tile, 2 * wide)
        act = shape4(act, group)
        e1[r + 1 : r + 1 + group, 1 : pairs + 1] = act[..., :wide]
        o1[r + 1 : r + 1 + group, 1 : pairs + 1] = act[..., wide:]

    loss = jnp.zeros((count, wide), F32)
    for r in range(0, rows, group):
        span = pl.ds(r * pairs * count, tile)
        left = jnp.concatenate(sum([stack_eo(e1, o1, r + a, group) for a in range(3)], []), axis=1)
        pre = matmul(left, w2_ref[...])
        gate = jax.nn.sigmoid(pre)
        act = (pre * gate).astype(BF)
        slope = gate * (1.0 + pre * (1.0 - gate))
        act2[span, :] = act
        output = matmul(act, po_ref[...]).reshape(group * pairs, count, wide)
        error = (
            skip * noisy[span, :].reshape(group * pairs, count, wide)
            + scale_out * output
            - res[span, :].reshape(group * pairs, count, wide)
        )
        loss = loss + jnp.sum(error * error, axis=0)
        grad_output = (grad_scale * error).astype(BF).reshape(tile, wide)
        gout[span, :] = grad_output
        grad_pre = (matmul(grad_output, pg_ref[...]) * slope).astype(BF)
        grad_pre = shape4(grad_pre, group)
        e2[r + 1 : r + 1 + group, 1 : pairs + 1] = grad_pre[..., :wide]
        o2[r + 1 : r + 1 + group, 1 : pairs + 1] = grad_pre[..., wide:]

    def emit(at, size, value):
        if before is not None:
            value = value + before[at : at + size, :]
        out_ref[at : at + size, :] = value

    depth = wide
    proj = lax.dot_general(gout[...], act2[...], TN_FORM, preferred_element_type=F32)
    emit(18 * depth, half, proj[:half, :wide] + proj[half:, wide:])

    gt[0:depth, :] = jnp.transpose(view(e2, 1, rows, 1))
    gt[depth : 2 * depth, :] = jnp.transpose(view(o2, 1, rows, 1))
    for a in range(3):
        right = jnp.concatenate(stack_eo(e1, o1, a, rows), axis=1)
        got = matmul(gt[...], right)
        h0, h1 = got[:depth], got[depth:]
        base = 9 * depth + 3 * a * depth
        emit(base, depth, h1[:, 0:wide] + h0[:, 2 * wide : 3 * wide])
        emit(base + depth, depth, h0[:, 0:wide] + h1[:, wide : 2 * wide])
        emit(base + 2 * depth, depth, h0[:, wide : 2 * wide] + h1[:, 3 * wide : 4 * wide])

    sums = jnp.zeros((count, 2 * wide), F32)
    for r in range(0, rows, group):
        span = pl.ds(r * pairs * count, tile)
        left = jnp.concatenate(sum([stack_eo(e2, o2, r + a, group) for a in range(3)], []), axis=1)
        grad = (matmul(left, v2_ref[...]) * slope1[span, :]).astype(BF)
        sums = sums + jnp.sum(grad.astype(F32).reshape(group * pairs, count, 2 * wide), axis=0)
        act2[span, :] = grad
    emb[...] = sums[:, :wide] + sums[:, wide:]
    table = 18 * depth + half
    levels = embed_ref.shape[0]
    if before is not None:
        out_ref[table : table + levels, :] = before[table : table + levels, :]
    else:
        out_ref[table : table + levels, :] = jnp.zeros((levels, wide), F32)
    for k in range(count):
        at = table + step_ref[chunk * count + k]
        out_ref[pl.ds(at, 1), :] = out_ref[pl.ds(at, 1), :] + emb[pl.ds(k, 1), :]

    levels_end = table + levels
    spots = lax.broadcasted_iota(jnp.int32, (8, wide), 0) * wide + lax.broadcasted_iota(jnp.int32, (8, wide), 1)
    sums = jnp.sum(fac_ref[5] * loss, axis=1, keepdims=True)
    owned = jnp.zeros((8, wide), F32)
    for k in range(count):
        owned = owned + jnp.where(spots == place_ref[chunk * count + k], sums[k : k + 1], 0.0)
    if before is not None:
        owned = owned + before[levels_end : levels_end + 8, :]
    out_ref[levels_end:, :] = jnp.zeros((out_ref.shape[0] - levels_end, wide), F32)
    if last:
        rounded = owned.astype(BF).astype(F32)
        out_ref[levels_end + 8 : levels_end + 16, :] = owned - rounded
        owned = rounded
    out_ref[levels_end : levels_end + 8, :] = owned

    gt[...] = jnp.transpose(act2[...])
    low = lax.broadcasted_iota(jnp.int32, (depth, wide), 1) < half
    for a in range(3):
        right = jnp.concatenate(stack_in(a, rows), axis=1)
        got = matmul(gt[...], right)
        h0, h1 = got[:depth], got[depth:]

        def merged(first, second):
            n = first[:, 0:wide], second[:, 0:wide]
            m = first[:, wide:], second[:, wide:]
            noise_part = n[0] + pltpu.roll(n[1], half, 1)
            mean_part = pltpu.roll(m[0], half, 1) + m[1]
            return jnp.where(low, noise_part, mean_part)

        base = 3 * a * depth
        direct, rim = slice(0, 2 * wide), slice(2 * wide, 4 * wide)
        emit(base, depth, merged(h1[:, direct], h0[:, rim]))
        emit(base + depth, depth, merged(h0[:, direct], h1[:, direct]))
        emit(base + 2 * depth, depth, merged(h1[:, rim], h0[:, direct]))

    if last:
        size = keep_ref.shape[0]
        core = place_ref[place_ref.shape[0] - 1]
        keep_ref[...] = out_ref[pl.ds(pl.multiple_of(core * size, 16), size), :]
        send_ref[...] = out_ref[pl.ds(pl.multiple_of((1 - core) * size, 16), size), :].astype(BF)


def unfold_kernel(index_ref, own_ref, other_ref, one_ref, two_ref, proj_ref, embed_ref, loss_ref, full):
    size, wide = own_ref.shape
    core = index_ref[0]
    full[pl.ds(pl.multiple_of(core * size, 16), size), :] = own_ref[...]
    full[pl.ds(pl.multiple_of((1 - core) * size, 16), size), :] = other_ref[...]
    depth = one_ref.shape[0]
    for tap in range(9):
        span = slice(tap * wide, (tap + 1) * wide)
        one_ref[:, span] = full[tap * depth : (tap + 1) * depth].astype(F32)
        two_ref[:, span] = full[(9 + tap) * depth : (10 + tap) * depth].astype(F32)
    at = 18 * depth
    for ref in (proj_ref, embed_ref):
        ref[...] = full[at : at + ref.shape[0]].astype(F32)
        at += ref.shape[0]
    spots = lax.broadcasted_iota(jnp.int32, (8, wide), 0) * wide + lax.broadcasted_iota(jnp.int32, (8, wide), 1)
    both = full[at : at + 16].astype(F32)
    loss = jnp.where(spots == index_ref[1], both[0:8] + both[8:16], 0.0)
    loss_ref[...] = jnp.sum(jnp.sum(loss, axis=1, keepdims=True), axis=0, keepdims=True)


def weights_kernel(one_ref, two_ref, proj_ref, w1_ref, w2_ref, v2_ref, po_ref, pg_ref):
    wide = one_ref.shape[0]
    half = wide // 2
    left, right = slice(0, wide), slice(wide, 2 * wide)
    for ref in (w1_ref, w2_ref, v2_ref, po_ref, pg_ref):
        ref[...] = jnp.zeros(ref.shape, BF)

    def place(ref, a, b, tap, split):
        base = 4 * wide * a

        def put(member, side):
            if split:
                start = {0: 0, 1: half, 3: 2 * wide, 2: 2 * wide + half}[member] + base
                ref[start : start + half, side] = tap[:half]
                ref[start + wide : start + wide + half, side] = tap[half:]
            else:
                start = base + member * wide
                ref[start : start + wide, side] = tap

        if b == 0:
            put(0, left)
            put(1, right)
        elif b == 1:
            put(1, left)
            put(3, right)
        else:
            put(0, right)
            put(2, left)

    for i, (a, b) in enumerate(TAPS):
        span = slice(i * wide, (i + 1) * wide)
        flipped = slice((8 - i) * wide, (9 - i) * wide)
        place(w1_ref, a + 1, b, jnp.transpose(one_ref[:, span]), True)
        place(w2_ref, a + 1, b, jnp.transpose(two_ref[:, span]), False)
        place(v2_ref, a + 1, b, two_ref[:, flipped], False)
    proj = proj_ref[...]
    pg_ref[0:half, left] = proj
    pg_ref[half:, right] = proj
    flat = jnp.transpose(proj.astype(F32)).astype(BF)
    zero = jnp.zeros_like(flat)
    po_ref[left, :] = jnp.concatenate([flat, zero], axis=1)
    po_ref[right, :] = jnp.concatenate([zero, flat], axis=1)


def by_distance(axis, distance):
    return [(i, i ^ distance) for i in range(lax.axis_size(axis))]


def rounded_to_bf16(values):
    return lax.reduce_precision(values, 8, 7)


def take(pieces, index):
    return lax.dynamic_index_in_dim(pieces, index, 0, keepdims=False)


def scatter_sum(values, axis):
    n = values.shape[0]
    me = lax.axis_index(axis)
    out = take(values, me)
    arrived = [
        lax.ppermute(take(values, me ^ d).astype(BF), axis, by_distance(axis, d)) for d in range(1, n)
    ]
    for piece in arrived:
        out = out + piece.astype(F32)
    return out


def gather_all(piece, axis):
    n = lax.axis_size(axis)
    me = lax.axis_index(axis)
    found = [piece] + [lax.ppermute(piece, axis, by_distance(axis, d)) for d in range(1, n)]
    return jnp.stack([sum_select(found, me, i) for i in range(n)])


def sum_select(found, me, index):
    out = found[0]
    for d in range(1, len(found)):
        out = jnp.where((me ^ d) == index, found[d], out)
    return out


def rows_sum(piece, axis):
    n = lax.axis_size(axis)
    if n > 4:
        return lax.psum(piece, axis)
    values = [rounded_to_bf16(piece).astype(BF)]
    for d in range(1, n):
        values.append(lax.ppermute(values[0], axis, by_distance(axis, d)))
    values = [v.astype(F32) for v in values]
    while len(values) > 1:
        values = [values[i] + values[i + 1] for i in range(0, len(values), 2)]
    return values[0]


def per_device(coarse, target, noise, regions, reg_conv, reg_out, conv_one, conv_two, out_proj, step_embed):
    strips = lax.axis_size("rows")
    me = lax.axis_index("rows")
    region = regions[0]
    per_strip = region.shape[1]
    most = noise.shape[2]
    capacity = max(2, (2 * per_strip + strips - 1) // strips)
    phases = 2
    deep = capacity // phases
    count = per_strip // phases
    exchange = strips <= 4
    channels = target.shape[1]
    height, width = target.shape[2:]
    cells = height * height
    wide = 2 * channels
    depth = conv_one.shape[0]
    levels = step_embed.shape[0]

    down = [(i + 1, i) for i in range(strips - 1)]
    up = [(i, i + 1) for i in range(strips - 1)]
    own_target = jnp.transpose(target[0], (1, 0, 2))
    own_coarse = jnp.transpose(coarse[0], (1, 0, 2))
    target_low = lax.ppermute(own_target[: height - 1], "rows", down)
    coarse_above = lax.ppermute(own_coarse[height - 1 :], "rows", up)
    coarse_below = lax.ppermute(own_coarse[:1], "rows", down)

    ids = jnp.arange(strips, dtype=jnp.int32)
    owners = region[:, :, 2]
    mine = jnp.sum((owners == me).astype(jnp.int32), axis=1)
    starts = jnp.sum(jnp.where(ids[:, None] > ids[None, :], mine[None, :], 0), axis=1)
    distances = ids
    goal = (ids ^ me) if exchange else ids
    goal_start = jnp.sum(jnp.where(goal[:, None] == ids[None, :], starts[None, :], 0), axis=1)
    rank = jnp.arange(capacity, dtype=jnp.int32).reshape(phases, 1, deep)
    slots = jnp.minimum(goal_start[None, :, None] + rank, most - 1).reshape(-1)

    own = lax.dynamic_index_in_dim(region, me, 0, keepdims=False)
    owner = own[:, 2]
    entry = jnp.arange(per_strip, dtype=jnp.int32)
    earlier = entry[None, :] < entry[:, None]
    pair_rank = jnp.sum(((owner[:, None] == owner[None, :]) & earlier).astype(jnp.int32), axis=1)
    early = pair_rank < deep
    early_before = jnp.sum((early[None, :] & earlier).astype(jnp.int32), axis=1)
    first = early & (early_before < count)
    first_before = jnp.sum((first[None, :] & earlier).astype(jnp.int32), axis=1)
    place = jnp.where(first, first_before, count + entry - first_before)
    place_hot = place[None, :] == entry[:, None]

    def ordered(field):
        return jnp.sum(jnp.where(place_hot, field[None, :], 0), axis=1)

    source = ordered(
        (pair_rank // deep) * (strips * deep) + ((owner ^ me) if exchange else owner) * deep + pair_rank % deep
    )
    top, left, step, owner_in_order = (ordered(own[:, i]) for i in (0, 1, 3, 2))

    sigma = 0.1 * jnp.exp(step.astype(F32) * (math.log(100.0) / (levels - 1)))
    u = sigma * sigma + 1.0
    weight = u / (sigma * sigma)
    scale_out = sigma / jnp.sqrt(u)
    grad_scale = 2.0 * weight / (channels * cells) * scale_out
    factors = [1.0 / jnp.sqrt(u), sigma, 1.0 / u, scale_out, grad_scale, weight / (channels * cells)]
    factors = jnp.broadcast_to(jnp.stack(factors)[:, :, None], (6, per_strip, wide))
    samples = lax.axis_size("segment") * lax.axis_size("dp")
    sample = lax.axis_index("segment") * lax.axis_size("dp") + lax.axis_index("dp")
    core = lax.axis_index("segment")
    place = jnp.concatenate([sample * strips + owner_in_order, core[None]]).astype(jnp.int32)

    slot_shape = (cells // 2, wide)
    pieces = phases * strips if exchange else phases
    packed = call(
        pack_kernel,
        [jax.ShapeDtypeStruct((phases * strips * deep // pieces,) + slot_shape, BF)] * pieces,
        (slots, noise[0, 0]),
        (SM, VM),
    )
    reg_channels = reg_conv.shape[1] // 9
    fill = -(-reg_channels // 16) * 16
    per_row = (channels, width)
    first_packed = packed[:strips] if exchange else packed[:1]
    coarse_above, coarse_below = after((coarse_above, coarse_below), tuple(first_packed) + (target_low,))
    mean, mean_top = call(
        regress_kernel,
        [jax.ShapeDtypeStruct((height,) + per_row, BF), jax.ShapeDtypeStruct((height - 1,) + per_row, BF)],
        (coarse_above, own_coarse, coarse_below, reg_conv.T, reg_out),
        (VM,) * 5,
        [pltpu.VMEM((height + 2, 3 * fill, width), BF), pltpu.VMEM((9 * fill, depth), BF)],
    )
    mean_low = lax.ppermute(mean_top, "rows", down)

    arrived = []
    for f in range(phases):
        sent = packed[f * strips : (f + 1) * strips] if exchange else packed[f : f + 1]
        if f > 0:
            sent = after(tuple(sent), (mean_top,))
        if exchange:
            parts = [sent[0]]
            for d in range(1, strips):
                parts.append(lax.ppermute(sent[d], "rows", by_distance("rows", d)))
        else:
            parts = [lax.all_to_all(sent[0], "rows", 0, 0, tiled=True)]
        arrived += parts

    conv_one, conv_two, out_proj = after((conv_one, conv_two, out_proj), (mean_top,))
    image = jax.ShapeDtypeStruct((height, width, wide), BF)
    image_m, image_t = call(paint_kernel, [image, image], (mean, own_target), (VM,) * 2)
    stacked = jax.ShapeDtypeStruct((12 * depth, 2 * depth), BF)
    weights = call(
        weights_kernel,
        [stacked] * 3
        + [jax.ShapeDtypeStruct((2 * depth, wide), BF), jax.ShapeDtypeStruct((wide, 2 * depth), BF)],
        (conv_one, conv_two, out_proj),
        (VM,) * 3,
    )
    patch_shape = jax.ShapeDtypeStruct((phases, cells // 2, count, wide), BF)
    mean_p, target_p = call(
        gather_kernel,
        [patch_shape, patch_shape],
        (top, left, image_m, image_t, mean_low, target_low),
        (SM, SM) + (VM,) * 4,
        [pltpu.VMEM((2 * height - 1, width, wide), F32)] * 2 + [pltpu.VMEM((cells // 2 * count, wide), F32)] * 2,
    )

    cores, groups = lax.axis_size("segment"), lax.axis_size("dp")
    total = cells // 2 * count
    rows_used = 18 * depth + channels + levels
    unit = cores * groups * 16
    rows_all = -(-(rows_used + 16) // unit) * unit
    per_core = rows_all // cores
    table = jax.ShapeDtypeStruct((rows_all, wide), F32)
    result = ()
    for chunk in range(phases):
        last = chunk == phases - 1
        pad = pltpu.VMEM((height + 2, height // 2 + 2, count, wide), BF)
        rim = pltpu.VMEM((height + 2, height // 2, count, wide), BF)
        used = arrived[: (chunk + 1) * len(parts)]
        slots_here = sum(piece.shape[0] for piece in used)
        ins = (source, step, place) + tuple(used)
        ins += (mean_p[chunk : chunk + 1], target_p[chunk : chunk + 1])
        ins += (factors[:, chunk * count : (chunk + 1) * count], step_embed)
        ins += tuple(weights) + tuple(result)
        outs = [table]
        if last:
            outs = [jax.ShapeDtypeStruct((per_core, wide), F32), jax.ShapeDtypeStruct((per_core, wide), BF)]
        result = call(
            functools.partial(chunk_kernel, chunk, last, len(used)),
            outs,
            ins,
            (SM,) * 3 + (VM,) * (len(ins) - 3),
            ([pltpu.VMEM((rows_all, wide), F32)] if last else [])
            + [
                pltpu.VMEM((slots_here, cells // 2, wide), BF),
                pltpu.VMEM((total, wide), F32),
                pad,
                pad,
                rim,
                rim,
                pad,
                pad,
                pad,
                pad,
                pltpu.VMEM((total, 2 * wide), F32),
                pltpu.VMEM((total, wide), F32),
                pltpu.VMEM((total, wide), F32),
                pltpu.VMEM((total, 2 * wide), BF),
                pltpu.VMEM((total, wide), BF),
                pltpu.VMEM((2 * wide, total), BF),
                pltpu.VMEM((count, wide), F32),
            ],
        )

    kept, sent = result
    kept = kept + lax.ppermute(sent, "segment", by_distance("segment", 1)).astype(F32)
    kept = scatter_sum(kept.reshape(groups, per_core // groups, wide), "dp")
    kept = rows_sum(kept, "rows")
    piece_rows = per_core // groups
    ending = (core == cores - 1) & (lax.axis_index("dp") == groups - 1)
    at = rows_used - (rows_all - piece_rows)
    exact = kept[at : at + 8] + kept[at + 8 : at + 16]
    rounded = rounded_to_bf16(exact)
    pair = jnp.concatenate([rounded, exact - rounded], axis=0)
    pair = jnp.where(ending, pair, kept[at : at + 16])
    kept = rounded_to_bf16(lax.dynamic_update_slice_in_dim(kept, pair, at, 0)).astype(BF)
    kept = gather_all(kept, "dp").reshape(per_core, wide)
    other = lax.ppermute(kept, "segment", by_distance("segment", 1))
    gradient = jax.ShapeDtypeStruct(conv_one.shape, F32)
    grad_one, grad_two, grad_proj, grad_embed, owner_loss = call(
        unfold_kernel,
        [
            gradient,
            gradient,
            jax.ShapeDtypeStruct(out_proj.shape, F32),
            jax.ShapeDtypeStruct(step_embed.shape, F32),
            jax.ShapeDtypeStruct((1, 1), F32),
        ],
        (jnp.stack([core, sample * strips + me]).astype(jnp.int32), kept, other),
        (SM, VM, VM),
        [pltpu.VMEM((rows_all, wide), BF)],
    )
    return jnp.transpose(mean, (1, 0, 2))[None], owner_loss, grad_one, grad_two, grad_proj, grad_embed


def solution(mesh):
    placed = (
        P(("segment", "dp"), None, "rows", None),
        P(("segment", "dp"), None, "rows", None),
        P(("segment", "dp"), "rows", None, None, None),
        P(("segment", "dp"), None, None, None),
        P(),
        P(),
        P(),
        P(),
        P(),
        P(),
    )
    return jax.shard_map(
        per_device,
        mesh=mesh,
        in_specs=placed,
        out_specs=(
            P(("segment", "dp"), None, "rows", None),
            P(("segment", "dp"), "rows"),
            P(),
            P(),
            P(),
            P(),
        ),
        check_vma=False,
    )
```

```python
import functools
import math

import jax
import jax.numpy as jnp
from jax import lax
from jax.experimental import pallas as pl
from jax.experimental.pallas import tpu as pltpu
from jax.sharding import PartitionSpec as P

BF = jnp.bfloat16
F32 = jnp.float32
TAPS = tuple((a, b) for a in (-1, 0, 1) for b in (-1, 0, 1))
NT_FORM = (((1,), (1,)), ((), ()))
TN_FORM = (((0,), (0,)), ((), ()))
MIB = 1024 * 1024
GROUP = 4


def matmul(left, right):
    return jnp.dot(left, right, preferred_element_type=F32)


VM = pl.BlockSpec(memory_space=pltpu.VMEM)
SM = pl.BlockSpec(memory_space=pltpu.SMEM)


def call(kernel, outs, ins, specs, scratch=(), limit=24):
    return pl.pallas_call(
        kernel,
        out_shape=outs,
        in_specs=list(specs),
        out_specs=jax.tree.map(lambda _: VM, outs),
        scratch_shapes=list(scratch),
        compiler_params=pltpu.CompilerParams(vmem_limit_bytes=limit * MIB),
        cost_estimate=pl.CostEstimate(flops=1000000000, bytes_accessed=1, transcendentals=0),
    )(*ins)


def after(values, others):
    return lax.optimization_barrier((values, others))[0]


def starts_kernel(region_ref, starts_ref):
    strips, _, entries = region_ref.shape
    me = lax.axis_index("rows")

    def strip(i, total):
        starts_ref[i] = total

        def entry(k, count):
            return count + jnp.where(region_ref[i, 2, k] == me, 1, 0)

        return lax.fori_loop(0, entries, entry, total, unroll=8)

    lax.fori_loop(0, strips, strip, 0)


def pack_kernel(phase, exchange, most, *refs):
    region_ref, noise_ref = refs[:2]
    out_refs, starts_ref = refs[2:-1], refs[-1]
    starts_kernel(region_ref, starts_ref)
    strips = starts_ref.shape[0]
    me = lax.axis_index("rows")
    channels, cells = noise_ref.shape[1:]
    half = cells // 2
    row = lax.broadcasted_iota(jnp.int32, (half, cells), 0)
    col = lax.broadcasted_iota(jnp.int32, (half, cells), 1)
    even = (col == 2 * row).astype(BF)
    odd = (col == 2 * row + 1).astype(BF)
    low = lax.broadcasted_iota(jnp.int32, (half, 2 * channels), 1) < channels
    deep = out_refs[0].shape[0] * len(out_refs) // strips

    def fill(goal, out_ref, base):
        first_slot = starts_ref[goal] + phase * deep

        def pair(j, carry):
            one_at, two_at = 2 * j, jnp.minimum(2 * j + 1, deep - 1)
            one = noise_ref[jnp.minimum(first_slot + one_at, most - 1)]
            two = noise_ref[jnp.minimum(first_slot + two_at, most - 1)]
            both = jnp.concatenate([one, two], axis=0)
            first = lax.dot_general(even, both, NT_FORM, preferred_element_type=F32)
            second = lax.dot_general(odd, both, NT_FORM, preferred_element_type=F32)
            out_ref[base + two_at] = jnp.where(low, pltpu.roll(first, channels, 1), second).astype(BF)
            out_ref[base + one_at] = jnp.where(low, first, pltpu.roll(second, channels, 1)).astype(BF)
            return carry

        many = (deep + 1) // 2
        lax.fori_loop(0, many, pair, 0, unroll=many)

    if exchange:
        for distance, out_ref in enumerate(out_refs):
            fill(me ^ distance, out_ref, 0)
    else:

        def goal(i, carry):
            fill(i, out_refs[0], i * deep)
            return carry

        lax.fori_loop(0, strips, goal, 0)


SOURCE, STEP, PLACE, TOP, LEFT = range(5)


def tables_kernel(exchange, deep, count, region_ref, table_ref, seen_ref):
    strips, _, entries = region_ref.shape
    me = lax.axis_index("rows")
    sample = lax.axis_index("segment") * lax.axis_size("dp") + lax.axis_index("dp")
    for i in range(strips):
        seen_ref[i] = 0

    def entry(k, carry):
        first, later = carry
        owner = region_ref[me, 2, k]
        rank = seen_ref[owner]
        seen_ref[owner] = rank + 1
        phase = rank // deep
        early = (phase == 0) & (first < count)
        at = jnp.where(early, first, later)
        sender = owner ^ me if exchange else owner
        table_ref[SOURCE, at] = (phase * strips + sender) * deep + rank - phase * deep
        table_ref[STEP, at] = region_ref[me, 3, k]
        table_ref[PLACE, at] = sample * strips + owner
        table_ref[TOP, at] = region_ref[me, 0, k]
        table_ref[LEFT, at] = region_ref[me, 1, k]
        step = jnp.where(early, 1, 0)
        return first + step, later + 1 - step

    lax.fori_loop(0, entries, entry, (0, count))


def regress_kernel(
    even_ref, inward_ref, own_ref, outward_ref, conv_ref, proj_ref, mean_ref, top_ref, last_ref, cols_ref, taps_ref
):
    rows, channels, width = own_ref.shape
    deep = cols_ref.shape[1] // 3
    cols_ref[...] = jnp.zeros(cols_ref.shape, BF)
    taps_ref[...] = jnp.zeros(taps_ref.shape, BF)
    for tap in range(9):
        taps_ref[tap * deep : tap * deep + channels] = (
            conv_ref[tap * channels : (tap + 1) * channels].astype(F32).astype(BF)
        )
    taps = jnp.transpose(taps_ref[...])
    lane = lax.broadcasted_iota(jnp.int32, (channels, width), 1)

    def put(at, cells):
        wide = cells.astype(F32)
        left = jnp.where(lane == 0, 0.0, pltpu.roll(wide, 1, 1)).astype(BF)
        right = jnp.where(lane == width - 1, 0.0, pltpu.roll(wide, width - 1, 1)).astype(BF)
        cols_ref[at, 0:channels] = left
        cols_ref[at, deep : deep + channels] = cells
        cols_ref[at, 2 * deep : 2 * deep + channels] = right

    even = even_ref[0]
    put(even * (rows + 1), inward_ref[0])
    put((1 - even) * (rows + 1), outward_ref[0])

    def fill(r, carry):
        put(r + 1, own_ref[r])
        return carry

    lax.fori_loop(0, rows, fill, 0)

    def one(r, carry):
        stack = cols_ref[pl.ds(r, 3)].reshape(9 * deep, width)
        hidden = matmul(taps, stack)
        act = (hidden * jax.nn.sigmoid(hidden)).astype(BF)
        mean_ref[r] = matmul(proj_ref[...], act).astype(BF)
        return carry

    lax.fori_loop(0, rows, one, 0, unroll=2)
    top_ref[...] = mean_ref[0 : rows - 1]
    last_ref[...] = mean_ref[rows - 1 : rows]


def painter(width):
    eye = (
        lax.broadcasted_iota(jnp.int32, (width, width), 0)
        == lax.broadcasted_iota(jnp.int32, (width, width), 1)
    ).astype(BF)

    def paint(cells):
        following = pltpu.roll(cells.astype(F32), width - 1, 1).astype(BF)
        both = jnp.concatenate([cells, following], axis=0)
        return lax.dot_general(eye, both, NT_FORM, preferred_element_type=F32)

    return paint


def gather(table_ref, image, got, out_ref):
    chunks, _, count, _ = out_ref.shape
    rows = 12
    pairs = rows // 2
    for chunk in range(chunks):

        def patch(k, carry, chunk=chunk):
            top = table_ref[TOP, chunk * count + k]
            left = table_ref[LEFT, chunk * count + k]
            for r in range(rows):
                got[pl.ds(r * pairs * count + k, pairs, stride=count), :] = image[
                    top + r, pl.ds(left, pairs, stride=2), :
                ]
            return carry

        lax.fori_loop(0, count, patch, 0, unroll=2)
        out_ref[chunk] = got[...].astype(BF).reshape(out_ref.shape[1:])


def target_kernel(
    exchange, deep, region_ref, tgt_ref, tgt_low_ref, top_ref, last_ref, table_ref, tp_ref, img_m, image, got, seen
):
    tables_kernel(exchange, deep, tp_ref.shape[2], region_ref, table_ref, seen)
    paint = painter(tgt_ref.shape[2])
    rows = tgt_ref.shape[0]

    def one(r, carry):
        img_m[r] = paint(top_ref[r]).astype(BF)
        image[r] = paint(tgt_ref[r])
        image[rows + r] = paint(tgt_low_ref[r])
        return carry

    lax.fori_loop(0, rows - 1, one, 0)
    img_m[rows - 1] = paint(last_ref[0]).astype(BF)
    image[rows - 1] = paint(tgt_ref[rows - 1])
    gather(table_ref, image, got, tp_ref)


def mean_kernel(table_ref, own, low_ref, mp_ref, image, got):
    rows = own.shape[0]
    paint = painter(own.shape[1])
    image[0:rows] = own[...].astype(F32)

    def low(r, carry):
        image[rows + r] = paint(low_ref[r])
        return carry

    lax.fori_loop(0, rows - 1, low, 0, unroll=11)
    gather(table_ref, image, got, mp_ref)


def chunk_kernel(chunk, last, pieces, *refs):
    table_ref = refs[0]
    noise_refs = refs[1 : 1 + pieces]
    refs = refs[1 + pieces :]
    (mp_ref, tp_ref, embed_ref, w1_ref, w2_ref, v2_ref, po_ref, pg_ref) = refs[:8]
    refs = refs[8:]
    before = None
    if chunk > 0:
        before, refs = refs[0], refs[1:]
    if last:
        keep_ref, send_ref, out_ref = refs[:3]
        refs = refs[3:]
    else:
        out_ref, refs = refs[0], refs[1:]
    (stage, nz, xn, xm, x2n, x2m, e1, o1, e2, o2, slope1, res, noisy, act2, gout, gt, emb, fac, by_level) = refs
    _, cells, count, wide = mp_ref.shape
    rows = 12
    pairs = cells // rows
    total = cells * count
    levels = embed_ref.shape[0]

    def entry(field, k):
        return table_ref[field, chunk * count + k]

    values = cells * wide
    level = lax.broadcasted_iota(jnp.int32, (levels, wide), 0).astype(F32)
    sig = 0.1 * jnp.exp(level * (math.log(100.0) / (levels - 1)))
    u = sig * sig + 1.0
    weight = u / (sig * sig)
    root = jnp.sqrt(u)
    scales = [1.0 / root, sig, 1.0 / u, sig / root, 2.0 * weight / values * (sig / root), weight / values]
    for i, scale in enumerate(scales):
        by_level[i] = scale
    group = GROUP
    half = wide // 2

    for ref in (xn, xm, e1, o1, e2, o2):
        ref[...] = jnp.zeros(ref.shape, BF)
    at = 0
    for ref in noise_refs:
        stage[at : at + ref.shape[0]] = ref[...]
        at += ref.shape[0]
    for k in range(count):
        piece = stage[entry(SOURCE, k)]
        nz[pl.ds(k, cells, stride=count), :] = piece.astype(F32)
        step = entry(STEP, k)
        emb[pl.ds(k, 1), :] = embed_ref[pl.ds(step, 1), :]
        for i in range(len(scales)):
            fac[i, pl.ds(k, 1), :] = by_level[i, pl.ds(step, 1), :]

    def spread(index):
        return fac[index][None]

    scale_in, sigma, skip, scale_out, grad_scale = (spread(i) for i in range(5))
    lane = lax.broadcasted_iota(jnp.int32, (1, 1, count, wide), 3)

    mean_bf = mp_ref[0]
    mean = mean_bf.astype(F32)
    residual = tp_ref[0].astype(F32) - mean
    noised = residual + sigma * nz[...].reshape(cells, count, wide)
    res[...] = residual.reshape(total, wide)
    noisy[...] = noised.reshape(total, wide)
    xn[1 : rows + 1, 1 : pairs + 1] = (scale_in * noised).astype(BF).reshape(rows, pairs, count, wide)
    xm[1 : rows + 1, 1 : pairs + 1] = mean_bf.reshape(rows, pairs, count, wide)
    for src, dst in ((xn, x2n), (xm, x2m)):
        dst[...] = jnp.where(
            lane < half, src[:, 2 : pairs + 2].astype(F32), src[:, 0:pairs].astype(F32)
        ).astype(BF)

    def view(ref, at, many, p0):
        return ref[at : at + many, p0 : p0 + pairs].reshape(many * pairs * count, wide)

    def stack_in(at, many):
        return [view(xn, at, many, 1), view(xm, at, many, 1), view(x2n, at, many, 0), view(x2m, at, many, 0)]

    def stack_eo(even, odd, at, many):
        return [view(even, at, many, 1), view(odd, at, many, 1), view(odd, at, many, 0), view(even, at, many, 2)]

    def shape4(value, many):
        return value.reshape(many, pairs, count, value.shape[-1])

    tile = group * pairs * count
    emb_pair = jnp.concatenate([emb[...], emb[...]], axis=1)[None]
    for r in range(0, rows, group):
        left = jnp.concatenate(sum([stack_in(r + a, group) for a in range(3)], []), axis=1)
        pre = matmul(left, w1_ref[...]).reshape(group * pairs, count, 2 * wide) + emb_pair
        gate = jax.nn.sigmoid(pre)
        act = (pre * gate).astype(BF)
        slope1[r * pairs * count : r * pairs * count + tile, :] = (
            gate * (1.0 + pre * (1.0 - gate))
        ).reshape(tile, 2 * wide)
        act = shape4(act, group)
        e1[r + 1 : r + 1 + group, 1 : pairs + 1] = act[..., :wide]
        o1[r + 1 : r + 1 + group, 1 : pairs + 1] = act[..., wide:]

    loss = jnp.zeros((count, wide), F32)
    for r in range(0, rows, group):
        span = pl.ds(r * pairs * count, tile)
        left = jnp.concatenate(sum([stack_eo(e1, o1, r + a, group) for a in range(3)], []), axis=1)
        pre = matmul(left, w2_ref[...])
        gate = jax.nn.sigmoid(pre)
        act = (pre * gate).astype(BF)
        slope = gate * (1.0 + pre * (1.0 - gate))
        act2[span, :] = act
        output = matmul(act, po_ref[...]).reshape(group * pairs, count, wide)
        error = (
            skip * noisy[span, :].reshape(group * pairs, count, wide)
            + scale_out * output
            - res[span, :].reshape(group * pairs, count, wide)
        )
        loss = loss + jnp.sum(error * error, axis=0)
        grad_output = (grad_scale * error).astype(BF).reshape(tile, wide)
        gout[span, :] = grad_output
        grad_pre = (matmul(grad_output, pg_ref[...]) * slope).astype(BF)
        grad_pre = shape4(grad_pre, group)
        e2[r + 1 : r + 1 + group, 1 : pairs + 1] = grad_pre[..., :wide]
        o2[r + 1 : r + 1 + group, 1 : pairs + 1] = grad_pre[..., wide:]

    def emit(at, size, value):
        if before is not None:
            value = value + before[at : at + size, :]
        out_ref[at : at + size, :] = value

    depth = wide
    proj = lax.dot_general(gout[...], act2[...], TN_FORM, preferred_element_type=F32)
    emit(18 * depth, half, proj[:half, :wide] + proj[half:, wide:])

    gt[0:depth, :] = jnp.transpose(view(e2, 1, rows, 1))
    gt[depth : 2 * depth, :] = jnp.transpose(view(o2, 1, rows, 1))
    for a in range(3):
        right = jnp.concatenate(stack_eo(e1, o1, a, rows), axis=1)
        got = matmul(gt[...], right)
        h0, h1 = got[:depth], got[depth:]
        base = 9 * depth + 3 * a * depth
        emit(base, depth, h1[:, 0:wide] + h0[:, 2 * wide : 3 * wide])
        emit(base + depth, depth, h0[:, 0:wide] + h1[:, wide : 2 * wide])
        emit(base + 2 * depth, depth, h0[:, wide : 2 * wide] + h1[:, 3 * wide : 4 * wide])

    sums = jnp.zeros((count, 2 * wide), F32)
    for r in range(0, rows, group):
        span = pl.ds(r * pairs * count, tile)
        left = jnp.concatenate(sum([stack_eo(e2, o2, r + a, group) for a in range(3)], []), axis=1)
        grad = (matmul(left, v2_ref[...]) * slope1[span, :]).astype(BF)
        sums = sums + jnp.sum(grad.astype(F32).reshape(group * pairs, count, 2 * wide), axis=0)
        act2[span, :] = grad
    emb[...] = sums[:, :wide] + sums[:, wide:]
    table = 18 * depth + half
    if before is not None:
        out_ref[table : table + levels, :] = before[table : table + levels, :]
    else:
        out_ref[table : table + levels, :] = jnp.zeros((levels, wide), F32)
    for k in range(count):
        at = table + entry(STEP, k)
        out_ref[pl.ds(at, 1), :] = out_ref[pl.ds(at, 1), :] + emb[pl.ds(k, 1), :]

    levels_end = table + levels
    spots = lax.broadcasted_iota(jnp.int32, (8, wide), 0) * wide + lax.broadcasted_iota(jnp.int32, (8, wide), 1)
    sums = jnp.sum(fac[5] * loss, axis=1, keepdims=True)
    owned = jnp.zeros((8, wide), F32)
    for k in range(count):
        owned = owned + jnp.where(spots == entry(PLACE, k), sums[k : k + 1], 0.0)
    if before is not None:
        owned = owned + before[levels_end : levels_end + 8, :]
    out_ref[levels_end:, :] = jnp.zeros((out_ref.shape[0] - levels_end, wide), F32)
    if last:
        rounded = owned.astype(BF).astype(F32)
        out_ref[levels_end + 8 : levels_end + 16, :] = owned - rounded
        owned = rounded
    out_ref[levels_end : levels_end + 8, :] = owned

    gt[...] = jnp.transpose(act2[...])
    low = lax.broadcasted_iota(jnp.int32, (depth, wide), 1) < half
    for a in range(3):
        right = jnp.concatenate(stack_in(a, rows), axis=1)
        got = matmul(gt[...], right)
        h0, h1 = got[:depth], got[depth:]

        def merged(first, second):
            n = first[:, 0:wide], second[:, 0:wide]
            m = first[:, wide:], second[:, wide:]
            noise_part = n[0] + pltpu.roll(n[1], half, 1)
            mean_part = pltpu.roll(m[0], half, 1) + m[1]
            return jnp.where(low, noise_part, mean_part)

        base = 3 * a * depth
        direct, rim = slice(0, 2 * wide), slice(2 * wide, 4 * wide)
        emit(base, depth, merged(h1[:, direct], h0[:, rim]))
        emit(base + depth, depth, merged(h0[:, direct], h1[:, direct]))
        emit(base + 2 * depth, depth, merged(h1[:, rim], h0[:, direct]))

    if last:
        size = keep_ref.shape[0]
        core = lax.axis_index("segment")
        keep_ref[...] = out_ref[pl.ds(pl.multiple_of(core * size, 16), size), :]
        send_ref[...] = out_ref[pl.ds(pl.multiple_of((1 - core) * size, 16), size), :].astype(BF)


def unfold_kernel(own_ref, other_ref, one_ref, two_ref, proj_ref, embed_ref, loss_ref, full):
    size, wide = own_ref.shape
    core = lax.axis_index("segment")
    sample = core * lax.axis_size("dp") + lax.axis_index("dp")
    place = sample * lax.axis_size("rows") + lax.axis_index("rows")
    full[pl.ds(pl.multiple_of(core * size, 16), size), :] = own_ref[...]
    full[pl.ds(pl.multiple_of((1 - core) * size, 16), size), :] = other_ref[...]
    depth = one_ref.shape[0]
    for tap in range(9):
        span = slice(tap * wide, (tap + 1) * wide)
        one_ref[:, span] = full[tap * depth : (tap + 1) * depth].astype(F32)
        two_ref[:, span] = full[(9 + tap) * depth : (10 + tap) * depth].astype(F32)
    at = 18 * depth
    for ref in (proj_ref, embed_ref):
        ref[...] = full[at : at + ref.shape[0]].astype(F32)
        at += ref.shape[0]
    spots = lax.broadcasted_iota(jnp.int32, (8, wide), 0) * wide + lax.broadcasted_iota(jnp.int32, (8, wide), 1)
    both = full[at : at + 16].astype(F32)
    loss = jnp.where(spots == place, both[0:8] + both[8:16], 0.0)
    loss_ref[...] = jnp.sum(jnp.sum(loss, axis=1, keepdims=True), axis=0, keepdims=True)


def weights_kernel(one_ref, two_ref, proj_ref, w1_ref, w2_ref, v2_ref, po_ref, pg_ref):
    wide = one_ref.shape[0]
    half = wide // 2
    left, right = slice(0, wide), slice(wide, 2 * wide)
    for ref in (w1_ref, w2_ref, v2_ref, po_ref, pg_ref):
        ref[...] = jnp.zeros(ref.shape, BF)

    def place(ref, a, b, tap, split):
        base = 4 * wide * a

        def put(member, side):
            if split:
                start = {0: 0, 1: half, 3: 2 * wide, 2: 2 * wide + half}[member] + base
                ref[start : start + half, side] = tap[:half]
                ref[start + wide : start + wide + half, side] = tap[half:]
            else:
                start = base + member * wide
                ref[start : start + wide, side] = tap

        if b == 0:
            put(0, left)
            put(1, right)
        elif b == 1:
            put(1, left)
            put(3, right)
        else:
            put(0, right)
            put(2, left)

    for i, (a, b) in enumerate(TAPS):
        span = slice(i * wide, (i + 1) * wide)
        flipped = slice((8 - i) * wide, (9 - i) * wide)
        place(w1_ref, a + 1, b, jnp.transpose(one_ref[:, span]), True)
        place(w2_ref, a + 1, b, jnp.transpose(two_ref[:, span]), False)
        place(v2_ref, a + 1, b, two_ref[:, flipped], False)
    proj = proj_ref[...]
    pg_ref[0:half, left] = proj
    pg_ref[half:, right] = proj
    flat = jnp.transpose(proj.astype(F32)).astype(BF)
    zero = jnp.zeros_like(flat)
    po_ref[left, :] = jnp.concatenate([flat, zero], axis=1)
    po_ref[right, :] = jnp.concatenate([zero, flat], axis=1)


def by_distance(axis, distance):
    return [(i, i ^ distance) for i in range(lax.axis_size(axis))]


def rounded_to_bf16(values):
    return lax.reduce_precision(values, 8, 7)


def take(pieces, index):
    return lax.dynamic_index_in_dim(pieces, index, 0, keepdims=False)


def scatter_sum(values, axis):
    n = values.shape[0]
    me = lax.axis_index(axis)
    out = take(values, me)
    arrived = [
        lax.ppermute(take(values, me ^ d).astype(BF), axis, by_distance(axis, d)) for d in range(1, n)
    ]
    for piece in arrived:
        out = out + piece.astype(F32)
    return out


def gather_all(piece, axis):
    n = lax.axis_size(axis)
    me = lax.axis_index(axis)
    found = [piece] + [lax.ppermute(piece, axis, by_distance(axis, d)) for d in range(1, n)]
    return jnp.stack([sum_select(found, me, i) for i in range(n)])


def sum_select(found, me, index):
    out = found[0]
    for d in range(1, len(found)):
        out = jnp.where((me ^ d) == index, found[d], out)
    return out


def rows_sum(piece, axis):
    n = lax.axis_size(axis)
    if n > 4:
        return lax.psum(piece, axis)
    values = [rounded_to_bf16(piece).astype(BF)]
    for d in range(1, n):
        values.append(lax.ppermute(values[0], axis, by_distance(axis, d)))
    values = [v.astype(F32) for v in values]
    while len(values) > 1:
        values = [values[i] + values[i + 1] for i in range(0, len(values), 2)]
    return values[0]


def per_device(coarse, target, noise, regions, reg_conv, reg_out, conv_one, conv_two, out_proj, step_embed):
    strips = lax.axis_size("rows")
    me = lax.axis_index("rows")
    region = regions[0]
    per_strip = region.shape[1]
    most = noise.shape[2]
    capacity = max(2, (2 * per_strip + strips - 1) // strips)
    phases = 2
    deep = capacity // phases
    count = per_strip // phases
    exchange = strips <= 4
    channels = target.shape[1]
    height, width = target.shape[2:]
    cells = height * height
    wide = 2 * channels
    depth = conv_one.shape[0]
    levels = step_embed.shape[0]

    down = [(i + 1, i) for i in range(strips - 1)]
    own_target = jnp.transpose(target[0], (1, 0, 2))
    own_coarse = jnp.transpose(coarse[0], (1, 0, 2))
    core = lax.axis_index("segment")
    region_table = jnp.transpose(region, (0, 2, 1))

    slot_shape = (cells // 2, wide)
    pieces = strips if exchange else 1

    def packed(phase, region_table, noise):
        return call(
            functools.partial(pack_kernel, phase, exchange, most),
            [jax.ShapeDtypeStruct((strips * deep // pieces,) + slot_shape, BF)] * pieces,
            (region_table, noise[0, 0]),
            (SM, VM),
            [pltpu.SMEM((strips,), jnp.int32)],
            limit=8,
        )

    def sent(packed_pieces):
        if not exchange:
            return [lax.all_to_all(packed_pieces[0], "rows", 0, 0, tiled=True)]
        moved = [lax.ppermute(packed_pieces[d], "rows", by_distance("rows", d)) for d in range(1, strips)]
        return [packed_pieces[0]] + moved

    first_packed = packed(0, region_table, noise)
    arrived = sent(first_packed)

    reg_channels = reg_conv.shape[1] // 9
    fill = -(-reg_channels // 16) * 16
    per_row = (channels, width)
    even = me % 2 == 0
    pairs = [(i, i ^ 1) for i in range(strips)]
    others = [(i, ((i + 1) ^ 1) - 1) for i in range(1, strips - 1)]
    low_edge, high_edge = own_coarse[:1], own_coarse[height - 1 :]
    inward = lax.ppermute(jnp.where(even, high_edge, low_edge), "rows", pairs)
    outward = lax.ppermute(jnp.where(even, low_edge, high_edge), "rows", others)
    target_low = lax.ppermute(own_target, "rows", down)
    inward, outward = after((inward, outward), (first_packed[0], target_low))
    mean, mean_top, mean_last = call(
        regress_kernel,
        [jax.ShapeDtypeStruct((rows,) + per_row, BF) for rows in (height, height - 1, 1)],
        (even.astype(jnp.int32)[None], inward, own_coarse, outward, reg_conv.T, reg_out),
        (SM,) + (VM,) * 5,
        [pltpu.VMEM((height + 2, 3 * fill, width), BF), pltpu.VMEM((9 * fill, depth), BF)],
        limit=12,
    )
    mean_low = lax.ppermute(mean_top, "rows", down)

    conv_one, conv_two, out_proj = after((conv_one, conv_two, out_proj), (mean_top,))
    stacked = jax.ShapeDtypeStruct((12 * depth, 2 * depth), BF)
    weights = call(
        weights_kernel,
        [stacked] * 3
        + [jax.ShapeDtypeStruct((2 * depth, wide), BF), jax.ShapeDtypeStruct((wide, 2 * depth), BF)],
        (conv_one, conv_two, out_proj),
        (VM,) * 3,
        limit=12,
    )
    patch_shape = jax.ShapeDtypeStruct((phases, cells // 2, count, wide), BF)
    image = pltpu.VMEM((2 * height - 1, width, wide), F32)
    got = pltpu.VMEM((cells // 2 * count, wide), F32)
    table, target_p, image_m = pl.pallas_call(
        functools.partial(target_kernel, exchange, deep),
        out_shape=[
            jax.ShapeDtypeStruct((5, per_strip), jnp.int32),
            patch_shape,
            jax.ShapeDtypeStruct((height, width, wide), BF),
        ],
        in_specs=[SM] + [VM] * 4,
        out_specs=[SM, VM, VM],
        scratch_shapes=[image, got, pltpu.SMEM((strips,), jnp.int32)],
        compiler_params=pltpu.CompilerParams(vmem_limit_bytes=16 * MIB),
        cost_estimate=pl.CostEstimate(flops=1000000000, bytes_accessed=1, transcendentals=0),
    )(region_table, own_target, target_low, mean_top, mean_last)
    later_region, later_noise = after((region_table, noise), (weights[0],))
    arrived += sent(packed(1, later_region, later_noise))
    mean_p = call(
        mean_kernel,
        patch_shape,
        (table, image_m, mean_low),
        (SM, VM, VM),
        [image, got],
        limit=16,
    )

    cores, groups = lax.axis_size("segment"), lax.axis_size("dp")
    total = cells // 2 * count
    rows_used = 18 * depth + channels + levels
    unit = cores * groups * 16
    rows_all = -(-(rows_used + 16) // unit) * unit
    per_core = rows_all // cores
    sums = jax.ShapeDtypeStruct((rows_all, wide), F32)
    result = ()
    for chunk in range(phases):
        last = chunk == phases - 1
        pad = pltpu.VMEM((height + 2, height // 2 + 2, count, wide), BF)
        rim = pltpu.VMEM((height + 2, height // 2, count, wide), BF)
        used = arrived[: (chunk + 1) * pieces]
        slots_here = sum(piece.shape[0] for piece in used)
        ins = (table,) + tuple(used)
        ins += (mean_p[chunk : chunk + 1], target_p[chunk : chunk + 1], step_embed)
        ins += tuple(weights) + tuple(result)
        outs = [sums]
        if last:
            outs = [jax.ShapeDtypeStruct((per_core, wide), F32), jax.ShapeDtypeStruct((per_core, wide), BF)]
        result = call(
            functools.partial(chunk_kernel, chunk, last, len(used)),
            outs,
            ins,
            (SM,) + (VM,) * (len(ins) - 1),
            ([pltpu.VMEM((rows_all, wide), F32)] if last else [])
            + [
                pltpu.VMEM((slots_here, cells // 2, wide), BF),
                pltpu.VMEM((total, wide), F32),
                pad,
                pad,
                rim,
                rim,
                pad,
                pad,
                pad,
                pad,
                pltpu.VMEM((total, 2 * wide), F32),
                pltpu.VMEM((total, wide), F32),
                pltpu.VMEM((total, wide), F32),
                pltpu.VMEM((total, 2 * wide), BF),
                pltpu.VMEM((total, wide), BF),
                pltpu.VMEM((2 * wide, total), BF),
                pltpu.VMEM((count, wide), F32),
                pltpu.VMEM((6, count, wide), F32),
                pltpu.VMEM((6, levels, wide), F32),
            ],
        )

    kept, given = result
    kept = kept + lax.ppermute(given, "segment", by_distance("segment", 1)).astype(F32)
    kept = scatter_sum(kept.reshape(groups, per_core // groups, wide), "dp")
    kept = rows_sum(kept, "rows")
    piece_rows = per_core // groups
    ending = (core == cores - 1) & (lax.axis_index("dp") == groups - 1)
    at = rows_used - (rows_all - piece_rows)
    exact = kept[at : at + 8] + kept[at + 8 : at + 16]
    rounded = rounded_to_bf16(exact)
    pair = jnp.concatenate([rounded, exact - rounded], axis=0)
    pair = jnp.where(ending, pair, kept[at : at + 16])
    kept = rounded_to_bf16(lax.dynamic_update_slice_in_dim(kept, pair, at, 0)).astype(BF)
    kept = gather_all(kept, "dp").reshape(per_core, wide)
    other = lax.ppermute(kept, "segment", by_distance("segment", 1))
    gradient = jax.ShapeDtypeStruct(conv_one.shape, F32)
    grad_one, grad_two, grad_proj, grad_embed, owner_loss = call(
        unfold_kernel,
        [
            gradient,
            gradient,
            jax.ShapeDtypeStruct(out_proj.shape, F32),
            jax.ShapeDtypeStruct(step_embed.shape, F32),
            jax.ShapeDtypeStruct((1, 1), F32),
        ],
        (kept, other),
        (VM, VM),
        [pltpu.VMEM((rows_all, wide), BF)],
        limit=12,
    )
    return jnp.transpose(mean, (1, 0, 2))[None], owner_loss, grad_one, grad_two, grad_proj, grad_embed


def solution(mesh):
    placed = (
        P(("segment", "dp"), None, "rows", None),
        P(("segment", "dp"), None, "rows", None),
        P(("segment", "dp"), "rows", None, None, None),
        P(("segment", "dp"), None, None, None),
        P(),
        P(),
        P(),
        P(),
        P(),
        P(),
    )
    return jax.shard_map(
        per_device,
        mesh=mesh,
        in_specs=placed,
        out_specs=(
            P(("segment", "dp"), None, "rows", None),
            P(("segment", "dp"), "rows"),
            P(),
            P(),
            P(),
            P(),
        ),
        check_vma=False,
    )
```

```python
import functools
import math

import jax
import jax.numpy as jnp
from jax import lax
from jax.experimental import pallas as pl
from jax.experimental.pallas import tpu as pltpu
from jax.sharding import PartitionSpec as P

BF = jnp.bfloat16
F32 = jnp.float32
TAPS = tuple((a, b) for a in (-1, 0, 1) for b in (-1, 0, 1))
NT_FORM = (((1,), (1,)), ((), ()))
TN_FORM = (((0,), (0,)), ((), ()))
MIB = 1024 * 1024
GROUP = 4
COSTS = (1000000000, 1000000000, 10000000000, 1000000000, 10000000000, 10000000000)
UNROLL = 16


def matmul(left, right):
    return jnp.dot(left, right, preferred_element_type=F32)


VM = pl.BlockSpec(memory_space=pltpu.VMEM)
SM = pl.BlockSpec(memory_space=pltpu.SMEM)


def call(kernel, outs, ins, specs, scratch=(), limit=24, cost=0):
    return pl.pallas_call(
        kernel,
        out_shape=outs,
        in_specs=list(specs),
        out_specs=jax.tree.map(lambda _: VM, outs),
        scratch_shapes=list(scratch),
        compiler_params=pltpu.CompilerParams(vmem_limit_bytes=limit * MIB),
        cost_estimate=pl.CostEstimate(flops=cost, bytes_accessed=1, transcendentals=0),
    )(*ins)


def after(values, others):
    return lax.optimization_barrier((values, others))[0]


def starts_kernel(region_ref, starts_ref):
    strips, _, entries = region_ref.shape
    me = lax.axis_index("rows")

    def strip(i, total):
        starts_ref[i] = total

        def entry(k, count):
            return count + jnp.where(region_ref[i, 2, k] == me, 1, 0)

        return lax.fori_loop(0, entries, entry, total, unroll=8)

    lax.fori_loop(0, strips, strip, 0)


def pack_kernel(phase, exchange, most, *refs):
    region_ref, noise_ref = refs[:2]
    out_refs, starts_ref = refs[2:-1], refs[-1]
    starts_kernel(region_ref, starts_ref)
    strips = starts_ref.shape[0]
    me = lax.axis_index("rows")
    channels, cells = noise_ref.shape[1:]
    half = cells // 2
    row = lax.broadcasted_iota(jnp.int32, (half, cells), 0)
    col = lax.broadcasted_iota(jnp.int32, (half, cells), 1)
    even = (col == 2 * row).astype(BF)
    odd = (col == 2 * row + 1).astype(BF)
    low = lax.broadcasted_iota(jnp.int32, (half, 2 * channels), 1) < channels
    deep = out_refs[0].shape[0] * len(out_refs) // strips

    def fill(goal, out_ref, base):
        first_slot = starts_ref[goal] + phase * deep

        def pair(j, carry):
            one_at, two_at = 2 * j, jnp.minimum(2 * j + 1, deep - 1)
            one = noise_ref[jnp.minimum(first_slot + one_at, most - 1)]
            two = noise_ref[jnp.minimum(first_slot + two_at, most - 1)]
            both = jnp.concatenate([one, two], axis=0)
            first = lax.dot_general(even, both, NT_FORM, preferred_element_type=F32)
            second = lax.dot_general(odd, both, NT_FORM, preferred_element_type=F32)
            out_ref[base + two_at] = jnp.where(low, pltpu.roll(first, channels, 1), second).astype(BF)
            out_ref[base + one_at] = jnp.where(low, first, pltpu.roll(second, channels, 1)).astype(BF)
            return carry

        many = (deep + 1) // 2
        lax.fori_loop(0, many, pair, 0, unroll=many)

    if exchange:
        for distance, out_ref in enumerate(out_refs):
            fill(me ^ distance, out_ref, 0)
    else:

        def goal(i, carry):
            fill(i, out_refs[0], i * deep)
            return carry

        lax.fori_loop(0, strips, goal, 0)


SOURCE, STEP, PLACE, TOP, LEFT = range(5)


def tables_kernel(exchange, deep, count, region_ref, table_ref, seen_ref):
    strips, _, entries = region_ref.shape
    me = lax.axis_index("rows")
    sample = lax.axis_index("segment") * lax.axis_size("dp") + lax.axis_index("dp")
    for i in range(strips):
        seen_ref[i] = 0

    def entry(k, carry):
        first, later = carry
        owner = region_ref[me, 2, k]
        rank = seen_ref[owner]
        seen_ref[owner] = rank + 1
        phase = rank // deep
        early = (phase == 0) & (first < count)
        at = jnp.where(early, first, later)
        sender = owner ^ me if exchange else owner
        table_ref[SOURCE, at] = (phase * strips + sender) * deep + rank - phase * deep
        table_ref[STEP, at] = region_ref[me, 3, k]
        table_ref[PLACE, at] = sample * strips + owner
        table_ref[TOP, at] = region_ref[me, 0, k]
        table_ref[LEFT, at] = region_ref[me, 1, k]
        step = jnp.where(early, 1, 0)
        return first + step, later + 1 - step

    lax.fori_loop(0, entries, entry, (0, count))


def regress_kernel(
    even_ref, inward_ref, own_ref, outward_ref, conv_ref, proj_ref, mean_ref, top_ref, last_ref, cols_ref, taps_ref
):
    rows, channels, width = own_ref.shape
    deep = cols_ref.shape[1] // 3
    cols_ref[...] = jnp.zeros(cols_ref.shape, BF)
    taps_ref[...] = jnp.zeros(taps_ref.shape, BF)
    for tap in range(9):
        taps_ref[tap * deep : tap * deep + channels] = (
            conv_ref[tap * channels : (tap + 1) * channels].astype(F32).astype(BF)
        )
    taps = jnp.transpose(taps_ref[...])
    lane = lax.broadcasted_iota(jnp.int32, (channels, width), 1)

    def put(at, cells):
        wide = cells.astype(F32)
        left = jnp.where(lane == 0, 0.0, pltpu.roll(wide, 1, 1)).astype(BF)
        right = jnp.where(lane == width - 1, 0.0, pltpu.roll(wide, width - 1, 1)).astype(BF)
        cols_ref[at, 0:channels] = left
        cols_ref[at, deep : deep + channels] = cells
        cols_ref[at, 2 * deep : 2 * deep + channels] = right

    even = even_ref[0]
    put(even * (rows + 1), inward_ref[0])
    put((1 - even) * (rows + 1), outward_ref[0])

    def fill(r, carry):
        put(r + 1, own_ref[r])
        return carry

    lax.fori_loop(0, rows, fill, 0, unroll=12)

    def one(r, carry):
        stack = cols_ref[pl.ds(r, 3)].reshape(9 * deep, width)
        hidden = matmul(taps, stack)
        act = (hidden * jax.nn.sigmoid(hidden)).astype(BF)
        mean_ref[r] = matmul(proj_ref[...], act).astype(BF)
        return carry

    lax.fori_loop(0, rows, one, 0, unroll=12)
    top_ref[...] = mean_ref[0 : rows - 1]
    last_ref[...] = mean_ref[rows - 1 : rows]


def identity(width):
    return (
        lax.broadcasted_iota(jnp.int32, (width, width), 0)
        == lax.broadcasted_iota(jnp.int32, (width, width), 1)
    ).astype(BF)


def paint(eye, pieces):
    return lax.dot_general(eye, jnp.concatenate(pieces, axis=0), NT_FORM, preferred_element_type=F32)


def own_kernel(exchange, deep, count, region_ref, tgt_ref, top_ref, last_ref, table_ref, image, seen):
    tables_kernel(exchange, deep, count, region_ref, table_ref, seen)
    rows, width, wide = image.shape
    eye = identity(width)
    means = [top_ref[r] for r in range(rows - 1)] + [last_ref[0]]
    for r in range(0, rows, 2):
        both = paint(eye, [means[r], tgt_ref[r], means[r + 1], tgt_ref[r + 1]])
        image[r] = both[:, :wide].astype(BF)
        image[r + 1] = both[:, wide:].astype(BF)


def gather_kernel(table_ref, own, mean_ref, tgt_ref, mp_ref, tp_ref, image, evens, odds):
    rows, width, wide = own.shape
    chunks, _, count, _ = mp_ref.shape
    pairs = rows // 2
    eye = identity(width)
    image[0:rows] = own[...].astype(F32)
    for r in range(0, rows - 1, 2):
        many = min(2, rows - 1 - r)
        both = paint(eye, sum([[mean_ref[r + i], tgt_ref[r + i]] for i in range(many)], []))
        for i in range(many):
            image[rows + r + i] = both[:, i * wide : (i + 1) * wide]
    half = wide // 2
    low = lax.broadcasted_iota(jnp.int32, evens.shape, 1) < half
    for chunk in range(chunks):

        def patch(k, carry, chunk=chunk):
            top = table_ref[TOP, chunk * count + k]
            left = table_ref[LEFT, chunk * count + k]
            for r in range(rows):
                span = pl.ds(r * pairs * count + k, pairs, stride=count)
                evens[span, :] = image[top + r, pl.ds(left, pairs, stride=2), :]
                odds[span, :] = image[top + r, pl.ds(left + 1, pairs, stride=2), :]
            return carry

        lax.fori_loop(0, count, patch, 0, unroll=min(UNROLL, count))
        even, odd = evens[...], odds[...]
        mean = jnp.where(low, even, pltpu.roll(odd, half, 1))
        goal = jnp.where(low, pltpu.roll(even, half, 1), odd)
        mp_ref[chunk] = mean.astype(BF).reshape(mp_ref.shape[1:])
        tp_ref[chunk] = goal.astype(BF).reshape(tp_ref.shape[1:])


def chunk_kernel(chunk, last, pieces, *refs):
    table_ref = refs[0]
    noise_refs = refs[1 : 1 + pieces]
    refs = refs[1 + pieces :]
    (mp_ref, tp_ref, embed_ref, w1_ref, w2_ref, v2_ref, po_ref, pg_ref) = refs[:8]
    refs = refs[8:]
    before = None
    if chunk > 0:
        before, refs = refs[0], refs[1:]
    if last:
        keep_ref, send_ref, out_ref = refs[:3]
        refs = refs[3:]
    else:
        out_ref, refs = refs[0], refs[1:]
    (stage, nz, xn, xm, x2n, x2m, e1, o1, e2, o2, slope1, res, noisy, act2, back, gout, gt, emb, fac, by_level) = refs
    _, cells, count, wide = mp_ref.shape
    rows = 12
    pairs = cells // rows
    total = cells * count
    levels = embed_ref.shape[0]

    def entry(field, k):
        return table_ref[field, chunk * count + k]

    values = cells * wide
    level = lax.broadcasted_iota(jnp.int32, (levels, wide), 0).astype(F32)
    sig = 0.1 * jnp.exp(level * (math.log(100.0) / (levels - 1)))
    u = sig * sig + 1.0
    weight = u / (sig * sig)
    root = jnp.sqrt(u)
    scales = [1.0 / root, sig, 1.0 / u, sig / root, 2.0 * weight / values * (sig / root), weight / values]
    for i, scale in enumerate(scales):
        by_level[i] = scale
    group = GROUP
    half = wide // 2

    for ref in (xn, xm, e1, o1, e2, o2):
        for at in (0, rows + 1):
            ref[at] = jnp.zeros(ref.shape[1:], BF)
        for at in (0, pairs + 1):
            ref[1 : rows + 1, at] = jnp.zeros((rows,) + ref.shape[2:], BF)
    at = 0
    for ref in noise_refs:
        stage[at : at + ref.shape[0]] = ref[...]
        at += ref.shape[0]
    for k in range(count):
        piece = stage[entry(SOURCE, k)]
        nz[pl.ds(k, cells, stride=count), :] = piece.astype(F32)
        step = entry(STEP, k)
        emb[pl.ds(k, 1), :] = embed_ref[pl.ds(step, 1), :]
        for i in range(len(scales)):
            fac[i, pl.ds(k, 1), :] = by_level[i, pl.ds(step, 1), :]

    def spread(index):
        return fac[index][None]

    scale_in, sigma, skip, scale_out, grad_scale = (spread(i) for i in range(5))
    lane = lax.broadcasted_iota(jnp.int32, (1, 1, count, wide), 3)

    mean_bf = mp_ref[chunk]
    mean = mean_bf.astype(F32)
    residual = tp_ref[chunk].astype(F32) - mean
    noised = residual + sigma * nz[...].reshape(cells, count, wide)
    res[...] = residual.reshape(total, wide)
    noisy[...] = noised.reshape(total, wide)
    xn[1 : rows + 1, 1 : pairs + 1] = (scale_in * noised).astype(BF).reshape(rows, pairs, count, wide)
    xm[1 : rows + 1, 1 : pairs + 1] = mean_bf.reshape(rows, pairs, count, wide)
    for src, dst in ((xn, x2n), (xm, x2m)):
        dst[...] = jnp.where(
            lane < half, src[:, 2 : pairs + 2].astype(F32), src[:, 0:pairs].astype(F32)
        ).astype(BF)

    def view(ref, at, many, p0):
        return ref[at : at + many, p0 : p0 + pairs].reshape(many * pairs * count, wide)

    def stack_in(at, many):
        return [view(xn, at, many, 1), view(xm, at, many, 1), view(x2n, at, many, 0), view(x2m, at, many, 0)]

    def stack_eo(even, odd, at, many):
        return [view(even, at, many, 1), view(odd, at, many, 1), view(odd, at, many, 0), view(even, at, many, 2)]

    def shape4(value, many):
        return value.reshape(many, pairs, count, value.shape[-1])

    tile = group * pairs * count
    emb_pair = jnp.concatenate([emb[...], emb[...]], axis=1)[None]
    def span_of(g):
        return pl.ds(g * tile, tile)

    def conv(stack, weight_ref, g):
        left = jnp.concatenate(sum([stack(g * group + a, group) for a in range(3)], []), axis=1)
        return matmul(left, weight_ref[...])

    def inner(ref, g):
        return ref.at[g * group + 1 : g * group + 1 + group, 1 : pairs + 1]

    def first(g, pre):
        pre = pre.reshape(group * pairs, count, 2 * wide) + emb_pair
        gate = jax.nn.sigmoid(pre)
        act = shape4((pre * gate).astype(BF), group)
        slope1[span_of(g), :] = (gate * (1.0 + pre * (1.0 - gate))).reshape(tile, 2 * wide)
        inner(e1, g)[...] = act[..., :wide]
        inner(o1, g)[...] = act[..., wide:]

    losses = []

    def second(g, pre):
        span = span_of(g)
        gate = jax.nn.sigmoid(pre)
        act = (pre * gate).astype(BF)
        slope = gate * (1.0 + pre * (1.0 - gate))
        act2[span, :] = act
        output = matmul(act, po_ref[...]).reshape(group * pairs, count, wide)
        error = (
            skip * noisy[span, :].reshape(group * pairs, count, wide)
            + scale_out * output
            - res[span, :].reshape(group * pairs, count, wide)
        )
        losses.append(jnp.sum(error * error, axis=0))
        grad_output = (grad_scale * error).astype(BF).reshape(tile, wide)
        gout[span, :] = grad_output
        grad_pre = shape4((matmul(grad_output, pg_ref[...]) * slope).astype(BF), group)
        inner(e2, g)[...] = grad_pre[..., :wide]
        inner(o2, g)[...] = grad_pre[..., wide:]

    partial = []

    def third(g, pre):
        span = span_of(g)
        grad = (pre * slope1[span, :]).astype(BF)
        back[span, :] = grad
        partial.append(jnp.sum(grad.astype(F32).reshape(group * pairs, count, 2 * wide), axis=0))

    stages = (
        (lambda g: conv(stack_in, w1_ref, g), first),
        (lambda g: conv(lambda at, many: stack_eo(e1, o1, at, many), w2_ref, g), second),
        (lambda g: conv(lambda at, many: stack_eo(e2, o2, at, many), v2_ref, g), third),
    )
    groups = rows // group
    depth = wide
    pending = None
    for index, (product, finish) in enumerate(stages):
        for g in range(groups):
            pre = product(g)
            if pending is not None:
                pending()
            pending = functools.partial(finish, g, pre)
        if groups < 3:
            pending()
            pending = None
    proj = lax.dot_general(gout[...], act2[...], TN_FORM, preferred_element_type=F32)
    gt[0:depth, :] = jnp.transpose(view(e2, 1, rows, 1))
    gt[depth : 2 * depth, :] = jnp.transpose(view(o2, 1, rows, 1))
    if pending is not None:
        pending()
    loss = sum(losses[1:], losses[0])
    sums = sum(partial[1:], partial[0])

    def emit(at, size, value):
        if before is not None:
            value = value + before[at : at + size, :]
        out_ref[at : at + size, :] = value

    emit(18 * depth, half, proj[:half, :wide] + proj[half:, wide:])
    for a in range(3):
        right = jnp.concatenate(stack_eo(e1, o1, a, rows), axis=1)
        got = matmul(gt[...], right)
        h0, h1 = got[:depth], got[depth:]
        base = 9 * depth + 3 * a * depth
        emit(base, depth, h1[:, 0:wide] + h0[:, 2 * wide : 3 * wide])
        emit(base + depth, depth, h0[:, 0:wide] + h1[:, wide : 2 * wide])
        emit(base + 2 * depth, depth, h0[:, wide : 2 * wide] + h1[:, 3 * wide : 4 * wide])

    emb[...] = sums[:, :wide] + sums[:, wide:]
    table = 18 * depth + half
    if before is not None:
        out_ref[table : table + levels, :] = before[table : table + levels, :]
    else:
        out_ref[table : table + levels, :] = jnp.zeros((levels, wide), F32)
    for k in range(count):
        at = table + entry(STEP, k)
        out_ref[pl.ds(at, 1), :] = out_ref[pl.ds(at, 1), :] + emb[pl.ds(k, 1), :]

    levels_end = table + levels
    spots = lax.broadcasted_iota(jnp.int32, (8, wide), 0) * wide + lax.broadcasted_iota(jnp.int32, (8, wide), 1)
    sums = jnp.sum(fac[5] * loss, axis=1, keepdims=True)
    owned = jnp.zeros((8, wide), F32)
    for k in range(count):
        owned = owned + jnp.where(spots == entry(PLACE, k), sums[k : k + 1], 0.0)
    if before is not None:
        owned = owned + before[levels_end : levels_end + 8, :]
    out_ref[levels_end:, :] = jnp.zeros((out_ref.shape[0] - levels_end, wide), F32)
    if last:
        rounded = owned.astype(BF).astype(F32)
        out_ref[levels_end + 8 : levels_end + 16, :] = owned - rounded
        owned = rounded
    out_ref[levels_end : levels_end + 8, :] = owned

    gt[...] = jnp.transpose(back[...])
    low = lax.broadcasted_iota(jnp.int32, (depth, wide), 1) < half
    for a in range(3):
        right = jnp.concatenate(stack_in(a, rows), axis=1)
        got = matmul(gt[...], right)
        h0, h1 = got[:depth], got[depth:]

        def merged(first, second):
            n = first[:, 0:wide], second[:, 0:wide]
            m = first[:, wide:], second[:, wide:]
            noise_part = n[0] + pltpu.roll(n[1], half, 1)
            mean_part = pltpu.roll(m[0], half, 1) + m[1]
            return jnp.where(low, noise_part, mean_part)

        base = 3 * a * depth
        direct, rim = slice(0, 2 * wide), slice(2 * wide, 4 * wide)
        emit(base, depth, merged(h1[:, direct], h0[:, rim]))
        emit(base + depth, depth, merged(h0[:, direct], h1[:, direct]))
        emit(base + 2 * depth, depth, merged(h1[:, rim], h0[:, direct]))

    if last:
        size = keep_ref.shape[0]
        core = lax.axis_index("segment")
        keep_ref[...] = out_ref[pl.ds(pl.multiple_of(core * size, 16), size), :]
        send_ref[...] = out_ref[pl.ds(pl.multiple_of((1 - core) * size, 16), size), :].astype(BF)


def unfold_kernel(own_ref, other_ref, one_ref, two_ref, proj_ref, embed_ref, loss_ref, full):
    size, wide = own_ref.shape
    core = lax.axis_index("segment")
    sample = core * lax.axis_size("dp") + lax.axis_index("dp")
    place = sample * lax.axis_size("rows") + lax.axis_index("rows")
    full[pl.ds(pl.multiple_of(core * size, 16), size), :] = own_ref[...]
    full[pl.ds(pl.multiple_of((1 - core) * size, 16), size), :] = other_ref[...]
    depth = one_ref.shape[0]
    for tap in range(9):
        span = slice(tap * wide, (tap + 1) * wide)
        one_ref[:, span] = full[tap * depth : (tap + 1) * depth].astype(F32)
        two_ref[:, span] = full[(9 + tap) * depth : (10 + tap) * depth].astype(F32)
    at = 18 * depth
    for ref in (proj_ref, embed_ref):
        ref[...] = full[at : at + ref.shape[0]].astype(F32)
        at += ref.shape[0]
    spots = lax.broadcasted_iota(jnp.int32, (8, wide), 0) * wide + lax.broadcasted_iota(jnp.int32, (8, wide), 1)
    both = full[at : at + 16].astype(F32)
    loss = jnp.where(spots == place, both[0:8] + both[8:16], 0.0)
    loss_ref[...] = jnp.sum(jnp.sum(loss, axis=1, keepdims=True), axis=0, keepdims=True)


def weights_kernel(one_ref, two_ref, proj_ref, w1_ref, w2_ref, v2_ref, po_ref, pg_ref):
    wide = one_ref.shape[0]
    half = wide // 2
    left, right = slice(0, wide), slice(wide, 2 * wide)
    for ref in (w1_ref, w2_ref, v2_ref, po_ref, pg_ref):
        ref[...] = jnp.zeros(ref.shape, BF)

    def place(ref, a, b, tap, split):
        base = 4 * wide * a

        def put(member, side):
            if split:
                start = {0: 0, 1: half, 3: 2 * wide, 2: 2 * wide + half}[member] + base
                ref[start : start + half, side] = tap[:half]
                ref[start + wide : start + wide + half, side] = tap[half:]
            else:
                start = base + member * wide
                ref[start : start + wide, side] = tap

        if b == 0:
            put(0, left)
            put(1, right)
        elif b == 1:
            put(1, left)
            put(3, right)
        else:
            put(0, right)
            put(2, left)

    for i, (a, b) in enumerate(TAPS):
        span = slice(i * wide, (i + 1) * wide)
        flipped = slice((8 - i) * wide, (9 - i) * wide)
        place(w1_ref, a + 1, b, jnp.transpose(one_ref[:, span]), True)
        place(w2_ref, a + 1, b, jnp.transpose(two_ref[:, span]), False)
        place(v2_ref, a + 1, b, two_ref[:, flipped], False)
    proj = proj_ref[...]
    pg_ref[0:half, left] = proj
    pg_ref[half:, right] = proj
    flat = jnp.transpose(proj.astype(F32)).astype(BF)
    zero = jnp.zeros_like(flat)
    po_ref[left, :] = jnp.concatenate([flat, zero], axis=1)
    po_ref[right, :] = jnp.concatenate([zero, flat], axis=1)


def by_distance(axis, distance):
    return [(i, i ^ distance) for i in range(lax.axis_size(axis))]


def rounded_to_bf16(values):
    return lax.reduce_precision(values, 8, 7)


def take(pieces, index):
    return lax.dynamic_index_in_dim(pieces, index, 0, keepdims=False)


def scatter_sum(values, axis):
    n = values.shape[0]
    me = lax.axis_index(axis)
    out = take(values, me)
    arrived = [
        lax.ppermute(take(values, me ^ d).astype(BF), axis, by_distance(axis, d)) for d in range(1, n)
    ]
    for piece in arrived:
        out = out + piece.astype(F32)
    return out


def gather_all(piece, axis):
    n = lax.axis_size(axis)
    me = lax.axis_index(axis)
    found = [piece] + [lax.ppermute(piece, axis, by_distance(axis, d)) for d in range(1, n)]
    return jnp.stack([sum_select(found, me, i) for i in range(n)])


def sum_select(found, me, index):
    out = found[0]
    for d in range(1, len(found)):
        out = jnp.where((me ^ d) == index, found[d], out)
    return out


def rows_sum(piece, axis):
    n = lax.axis_size(axis)
    if n > 4:
        return lax.psum(piece, axis)
    values = [rounded_to_bf16(piece).astype(BF)]
    for d in range(1, n):
        values.append(lax.ppermute(values[0], axis, by_distance(axis, d)))
    values = [v.astype(F32) for v in values]
    while len(values) > 1:
        values = [values[i] + values[i + 1] for i in range(0, len(values), 2)]
    return values[0]


def per_device(coarse, target, noise, regions, reg_conv, reg_out, conv_one, conv_two, out_proj, step_embed):
    strips = lax.axis_size("rows")
    me = lax.axis_index("rows")
    region = regions[0]
    per_strip = region.shape[1]
    most = noise.shape[2]
    capacity = max(2, (2 * per_strip + strips - 1) // strips)
    phases = 2
    deep = capacity // phases
    count = per_strip // phases
    exchange = strips <= 4
    channels = target.shape[1]
    height, width = target.shape[2:]
    cells = height * height
    wide = 2 * channels
    depth = conv_one.shape[0]
    levels = step_embed.shape[0]

    down = [(i + 1, i) for i in range(strips - 1)]
    own_target = jnp.transpose(target[0], (1, 0, 2))
    own_coarse = jnp.transpose(coarse[0], (1, 0, 2))
    core = lax.axis_index("segment")
    region_table = jnp.transpose(region, (0, 2, 1))

    slot_shape = (cells // 2, wide)
    pieces = strips if exchange else 1

    def packed(phase, region_table, noise):
        return call(
            functools.partial(pack_kernel, phase, exchange, most),
            [jax.ShapeDtypeStruct((strips * deep // pieces,) + slot_shape, BF)] * pieces,
            (region_table, noise[0, 0]),
            (SM, VM),
            [pltpu.SMEM((strips,), jnp.int32)],
            limit=8,
            cost=COSTS[0],
        )

    def sent(packed_pieces):
        if not exchange:
            return [lax.all_to_all(packed_pieces[0], "rows", 0, 0, tiled=True)]
        moved = [lax.ppermute(packed_pieces[d], "rows", by_distance("rows", d)) for d in range(1, strips)]
        return [packed_pieces[0]] + moved

    first_packed = packed(0, region_table, noise)
    arrived = sent(first_packed)

    reg_channels = reg_conv.shape[1] // 9
    fill = -(-reg_channels // 16) * 16
    per_row = (channels, width)
    even = me % 2 == 0
    pairs = [(i, i ^ 1) for i in range(strips)]
    others = [(i, ((i + 1) ^ 1) - 1) for i in range(1, strips - 1)]
    low_edge, high_edge = own_coarse[:1], own_coarse[height - 1 :]
    inward = lax.ppermute(jnp.where(even, high_edge, low_edge), "rows", pairs)
    outward = lax.ppermute(jnp.where(even, low_edge, high_edge), "rows", others)
    target_low = lax.ppermute(own_target, "rows", down)
    inward, outward = after((inward, outward), (first_packed[0],))
    mean, mean_top, mean_last = call(
        regress_kernel,
        [jax.ShapeDtypeStruct((rows,) + per_row, BF) for rows in (height, height - 1, 1)],
        (even.astype(jnp.int32)[None], inward, own_coarse, outward, reg_conv.T, reg_out),
        (SM,) + (VM,) * 5,
        [pltpu.VMEM((height + 2, 3 * fill, width), BF), pltpu.VMEM((9 * fill, depth), BF)],
        limit=12,
        cost=COSTS[1],
    )
    mean_low = lax.ppermute(mean_top, "rows", down)

    conv_one, conv_two, out_proj = after((conv_one, conv_two, out_proj), (mean_top,))
    stacked = jax.ShapeDtypeStruct((12 * depth, 2 * depth), BF)
    weights = call(
        weights_kernel,
        [stacked] * 3
        + [jax.ShapeDtypeStruct((2 * depth, wide), BF), jax.ShapeDtypeStruct((wide, 2 * depth), BF)],
        (conv_one, conv_two, out_proj),
        (VM,) * 3,
        limit=12,
        cost=COSTS[3],
    )
    patch_shape = jax.ShapeDtypeStruct((phases, cells // 2, count, wide), BF)
    got = pltpu.VMEM((cells // 2 * count, wide), F32)
    table, image = pl.pallas_call(
        functools.partial(own_kernel, exchange, deep, count),
        out_shape=[
            jax.ShapeDtypeStruct((5, per_strip), jnp.int32),
            jax.ShapeDtypeStruct((height, width, wide), BF),
        ],
        in_specs=[SM] + [VM] * 3,
        out_specs=[SM, VM],
        scratch_shapes=[pltpu.SMEM((strips,), jnp.int32)],
        compiler_params=pltpu.CompilerParams(vmem_limit_bytes=16 * MIB),
        cost_estimate=pl.CostEstimate(flops=COSTS[2], bytes_accessed=1, transcendentals=0),
    )(region_table, own_target, mean_top, after((mean_last,), (target_low,))[0])
    later_region, later_noise = after((region_table, noise), (weights[0], image))
    arrived += sent(packed(1, later_region, later_noise))
    mean_p, target_p = call(
        gather_kernel,
        [patch_shape, patch_shape],
        (table, image, mean_low, target_low),
        (SM, VM, VM, VM),
        [pltpu.VMEM((2 * height - 1, width, wide), F32), got, got],
        limit=16,
        cost=COSTS[4],
    )

    cores, groups = lax.axis_size("segment"), lax.axis_size("dp")
    total = cells // 2 * count
    rows_used = 18 * depth + channels + levels
    unit = cores * groups * 16
    rows_all = -(-(rows_used + 16) // unit) * unit
    per_core = rows_all // cores
    sums = jax.ShapeDtypeStruct((rows_all, wide), F32)
    result = ()
    for chunk in range(phases):
        last = chunk == phases - 1
        pad = pltpu.VMEM((height + 2, height // 2 + 2, count, wide), BF)
        rim = pltpu.VMEM((height + 2, height // 2, count, wide), BF)
        used = arrived[: (chunk + 1) * pieces]
        slots_here = sum(piece.shape[0] for piece in used)
        ins = (table,) + tuple(used)
        ins += (mean_p, target_p, step_embed)
        ins += tuple(weights) + tuple(result)
        outs = [sums]
        if last:
            outs = [jax.ShapeDtypeStruct((per_core, wide), F32), jax.ShapeDtypeStruct((per_core, wide), BF)]
        result = call(
            functools.partial(chunk_kernel, chunk, last, len(used)),
            outs,
            ins,
            (SM,) + (VM,) * (len(ins) - 1),
            ([pltpu.VMEM((rows_all, wide), F32)] if last else [])
            + [
                pltpu.VMEM((slots_here, cells // 2, wide), BF),
                pltpu.VMEM((total, wide), F32),
                pad,
                pad,
                rim,
                rim,
                pad,
                pad,
                pad,
                pad,
                pltpu.VMEM((total, 2 * wide), F32),
                pltpu.VMEM((total, wide), F32),
                pltpu.VMEM((total, wide), F32),
                pltpu.VMEM((total, 2 * wide), BF),
                pltpu.VMEM((total, 2 * wide), BF),
                pltpu.VMEM((total, wide), BF),
                pltpu.VMEM((2 * wide, total), BF),
                pltpu.VMEM((count, wide), F32),
                pltpu.VMEM((6, count, wide), F32),
                pltpu.VMEM((6, levels, wide), F32),
            ],
            cost=COSTS[5],
        )

    kept, given = result
    kept = kept + lax.ppermute(given, "segment", by_distance("segment", 1)).astype(F32)
    kept = scatter_sum(kept.reshape(groups, per_core // groups, wide), "dp")
    kept = rows_sum(kept, "rows")
    piece_rows = per_core // groups
    ending = (core == cores - 1) & (lax.axis_index("dp") == groups - 1)
    at = rows_used - (rows_all - piece_rows)
    exact = kept[at : at + 8] + kept[at + 8 : at + 16]
    rounded = rounded_to_bf16(exact)
    pair = jnp.concatenate([rounded, exact - rounded], axis=0)
    pair = jnp.where(ending, pair, kept[at : at + 16])
    kept = rounded_to_bf16(lax.dynamic_update_slice_in_dim(kept, pair, at, 0)).astype(BF)
    kept = gather_all(kept, "dp").reshape(per_core, wide)
    other = lax.ppermute(kept, "segment", by_distance("segment", 1))
    gradient = jax.ShapeDtypeStruct(conv_one.shape, F32)
    grad_one, grad_two, grad_proj, grad_embed, owner_loss = call(
        unfold_kernel,
        [
            gradient,
            gradient,
            jax.ShapeDtypeStruct(out_proj.shape, F32),
            jax.ShapeDtypeStruct(step_embed.shape, F32),
            jax.ShapeDtypeStruct((1, 1), F32),
        ],
        (kept, other),
        (VM, VM),
        [pltpu.VMEM((rows_all, wide), BF)],
        limit=12,
    )
    return jnp.transpose(mean, (1, 0, 2))[None], owner_loss, grad_one, grad_two, grad_proj, grad_embed


def solution(mesh):
    placed = (
        P(("segment", "dp"), None, "rows", None),
        P(("segment", "dp"), None, "rows", None),
        P(("segment", "dp"), "rows", None, None, None),
        P(("segment", "dp"), None, None, None),
        P(),
        P(),
        P(),
        P(),
        P(),
        P(),
    )
    return jax.shard_map(
        per_device,
        mesh=mesh,
        in_specs=placed,
        out_specs=(
            P(("segment", "dp"), None, "rows", None),
            P(("segment", "dp"), "rows"),
            P(),
            P(),
            P(),
            P(),
        ),
        check_vma=False,
    )
```

```python
import functools
import math

import jax
import jax.numpy as jnp
from jax import lax
from jax.experimental import pallas as pl
from jax.experimental.pallas import tpu as pltpu
from jax.sharding import PartitionSpec as P

BF = jnp.bfloat16
F32 = jnp.float32
TAPS = tuple((a, b) for a in (-1, 0, 1) for b in (-1, 0, 1))
NT_FORM = (((1,), (1,)), ((), ()))
TN_FORM = (((0,), (0,)), ((), ()))
MIB = 1024 * 1024
GROUP = 4
COSTS = (1000000000, 1000000000, 10000000000, 1000000000, 10000000000, 10000000000)
UNROLL = 16


def matmul(left, right):
    return jnp.dot(left, right, preferred_element_type=F32)


VM = pl.BlockSpec(memory_space=pltpu.VMEM)
SM = pl.BlockSpec(memory_space=pltpu.SMEM)


def call(kernel, outs, ins, specs, scratch=(), limit=24, cost=0):
    return pl.pallas_call(
        kernel,
        out_shape=outs,
        in_specs=list(specs),
        out_specs=jax.tree.map(lambda _: VM, outs),
        scratch_shapes=list(scratch),
        compiler_params=pltpu.CompilerParams(vmem_limit_bytes=limit * MIB),
        cost_estimate=pl.CostEstimate(flops=cost, bytes_accessed=1, transcendentals=0),
    )(*ins)


def after(values, others):
    return lax.optimization_barrier((values, others))[0]


def starts_kernel(region_ref, starts_ref):
    strips, _, entries = region_ref.shape
    me = lax.axis_index("rows")

    def strip(i, total):
        starts_ref[i] = total

        def entry(k, count):
            return count + jnp.where(region_ref[i, 2, k] == me, 1, 0)

        return lax.fori_loop(0, entries, entry, total, unroll=8)

    lax.fori_loop(0, strips, strip, 0)


def pack_kernel(phase, exchange, most, *refs):
    region_ref, noise_ref = refs[:2]
    out_refs, starts_ref = refs[2:-1], refs[-1]
    starts_kernel(region_ref, starts_ref)
    strips = starts_ref.shape[0]
    me = lax.axis_index("rows")
    channels, cells = noise_ref.shape[1:]
    half = cells // 2
    row = lax.broadcasted_iota(jnp.int32, (half, cells), 0)
    col = lax.broadcasted_iota(jnp.int32, (half, cells), 1)
    even = (col == 2 * row).astype(BF)
    odd = (col == 2 * row + 1).astype(BF)
    low = lax.broadcasted_iota(jnp.int32, (half, 2 * channels), 1) < channels
    deep = out_refs[0].shape[0] * len(out_refs) // strips

    def fill(goal, out_ref, base):
        first_slot = starts_ref[goal] + phase * deep

        def pair(j, carry):
            one_at, two_at = 2 * j, jnp.minimum(2 * j + 1, deep - 1)
            one = noise_ref[jnp.minimum(first_slot + one_at, most - 1)]
            two = noise_ref[jnp.minimum(first_slot + two_at, most - 1)]
            both = jnp.concatenate([one, two], axis=0)
            first = lax.dot_general(even, both, NT_FORM, preferred_element_type=F32)
            second = lax.dot_general(odd, both, NT_FORM, preferred_element_type=F32)
            out_ref[base + two_at] = jnp.where(low, pltpu.roll(first, channels, 1), second).astype(BF)
            out_ref[base + one_at] = jnp.where(low, first, pltpu.roll(second, channels, 1)).astype(BF)
            return carry

        many = (deep + 1) // 2
        lax.fori_loop(0, many, pair, 0, unroll=many)

    if exchange:
        for distance, out_ref in enumerate(out_refs):
            fill(me ^ distance, out_ref, 0)
    else:

        def goal(i, carry):
            fill(i, out_refs[0], i * deep)
            return carry

        lax.fori_loop(0, strips, goal, 0)


SOURCE, STEP, PLACE, TOP, LEFT = range(5)


def tables_kernel(exchange, deep, count, region_ref, table_ref, seen_ref):
    strips, _, entries = region_ref.shape
    me = lax.axis_index("rows")
    sample = lax.axis_index("segment") * lax.axis_size("dp") + lax.axis_index("dp")
    for i in range(strips):
        seen_ref[i] = 0

    def entry(k, carry):
        first, later = carry
        owner = region_ref[me, 2, k]
        rank = seen_ref[owner]
        seen_ref[owner] = rank + 1
        phase = rank // deep
        early = (phase == 0) & (first < count)
        at = jnp.where(early, first, later)
        sender = owner ^ me if exchange else owner
        table_ref[SOURCE, at] = (phase * strips + sender) * deep + rank - phase * deep
        table_ref[STEP, at] = region_ref[me, 3, k]
        table_ref[PLACE, at] = sample * strips + owner
        table_ref[TOP, at] = region_ref[me, 0, k]
        table_ref[LEFT, at] = region_ref[me, 1, k]
        step = jnp.where(early, 1, 0)
        return first + step, later + 1 - step

    lax.fori_loop(0, entries, entry, (0, count))


def regress_kernel(
    even_ref, inward_ref, own_ref, outward_ref, conv_ref, proj_ref, mean_ref, top_ref, last_ref, cols_ref, taps_ref
):
    rows, channels, width = own_ref.shape
    deep = cols_ref.shape[1] // 3
    cols_ref[...] = jnp.zeros(cols_ref.shape, BF)
    taps_ref[...] = jnp.zeros(taps_ref.shape, BF)
    for tap in range(9):
        taps_ref[tap * deep : tap * deep + channels] = (
            conv_ref[tap * channels : (tap + 1) * channels].astype(F32).astype(BF)
        )
    taps = jnp.transpose(taps_ref[...])
    lane = lax.broadcasted_iota(jnp.int32, (channels, width), 1)

    def put(at, cells):
        wide = cells.astype(F32)
        left = jnp.where(lane == 0, 0.0, pltpu.roll(wide, 1, 1)).astype(BF)
        right = jnp.where(lane == width - 1, 0.0, pltpu.roll(wide, width - 1, 1)).astype(BF)
        cols_ref[at, 0:channels] = left
        cols_ref[at, deep : deep + channels] = cells
        cols_ref[at, 2 * deep : 2 * deep + channels] = right

    even = even_ref[0]
    put(even * (rows + 1), inward_ref[0])
    put((1 - even) * (rows + 1), outward_ref[0])

    def fill(r, carry):
        put(r + 1, own_ref[r])
        return carry

    lax.fori_loop(0, rows, fill, 0, unroll=12)

    def one(r, carry):
        stack = cols_ref[pl.ds(r, 3)].reshape(9 * deep, width)
        hidden = matmul(taps, stack)
        act = (hidden * jax.nn.sigmoid(hidden)).astype(BF)
        mean_ref[r] = matmul(proj_ref[...], act).astype(BF)
        return carry

    lax.fori_loop(0, rows, one, 0, unroll=12)
    top_ref[...] = mean_ref[0 : rows - 1]
    last_ref[...] = mean_ref[rows - 1 : rows]


def identity(width):
    return (
        lax.broadcasted_iota(jnp.int32, (width, width), 0)
        == lax.broadcasted_iota(jnp.int32, (width, width), 1)
    ).astype(BF)


def paint(eye, pieces):
    return lax.dot_general(eye, jnp.concatenate(pieces, axis=0), NT_FORM, preferred_element_type=F32)


def own_kernel(exchange, deep, count, region_ref, tgt_ref, top_ref, last_ref, table_ref, image, seen):
    tables_kernel(exchange, deep, count, region_ref, table_ref, seen)
    rows, width, wide = image.shape
    eye = identity(width)
    means = [top_ref[r] for r in range(rows - 1)] + [last_ref[0]]
    for r in range(0, rows, 2):
        both = paint(eye, [means[r], tgt_ref[r], means[r + 1], tgt_ref[r + 1]])
        image[r] = both[:, :wide].astype(BF)
        image[r + 1] = both[:, wide:].astype(BF)


def gather_kernel(table_ref, own, mean_ref, tgt_ref, mp_ref, tp_ref, image, evens, odds):
    rows, width, wide = own.shape
    chunks, _, count, _ = mp_ref.shape
    pairs = rows // 2
    eye = identity(width)
    image[0:rows] = own[...].astype(F32)
    for r in range(0, rows - 1, 2):
        many = min(2, rows - 1 - r)
        both = paint(eye, sum([[mean_ref[r + i], tgt_ref[r + i]] for i in range(many)], []))
        for i in range(many):
            image[rows + r + i] = both[:, i * wide : (i + 1) * wide]
    half = wide // 2
    low = lax.broadcasted_iota(jnp.int32, evens.shape, 1) < half
    for chunk in range(chunks):

        def patch(k, carry, chunk=chunk):
            top = table_ref[TOP, chunk * count + k]
            left = table_ref[LEFT, chunk * count + k]
            for r in range(rows):
                span = pl.ds(r * pairs * count + k, pairs, stride=count)
                evens[span, :] = image[top + r, pl.ds(left, pairs, stride=2), :]
                odds[span, :] = image[top + r, pl.ds(left + 1, pairs, stride=2), :]
            return carry

        lax.fori_loop(0, count, patch, 0, unroll=min(UNROLL, count))
        even, odd = evens[...], odds[...]
        mean = jnp.where(low, even, pltpu.roll(odd, half, 1))
        goal = jnp.where(low, pltpu.roll(even, half, 1), odd)
        mp_ref[chunk] = mean.astype(BF).reshape(mp_ref.shape[1:])
        tp_ref[chunk] = goal.astype(BF).reshape(tp_ref.shape[1:])


def chunk_kernel(chunk, last, pieces, *refs):
    table_ref = refs[0]
    noise_refs = refs[1 : 1 + pieces]
    refs = refs[1 + pieces :]
    (mp_ref, tp_ref, embed_ref, w1_ref, w2_ref, v2_ref, po_ref, pg_ref) = refs[:8]
    refs = refs[8:]
    before = None
    if chunk > 0:
        before, refs = refs[0], refs[1:]
    if last:
        keep_ref, send_ref, out_ref = refs[:3]
        refs = refs[3:]
    else:
        out_ref, refs = refs[0], refs[1:]
    (stage, nz, xn, xm, x2n, x2m, e1, o1, e2, o2, slope1, res, noisy, act2, back, gout, gt, emb, fac, by_level) = refs
    _, cells, count, wide = mp_ref.shape
    rows = 12
    pairs = cells // rows
    total = cells * count
    levels = embed_ref.shape[0]

    def entry(field, k):
        return table_ref[field, chunk * count + k]

    values = cells * wide
    level = lax.broadcasted_iota(jnp.int32, (levels, wide), 0).astype(F32)
    sig = 0.1 * jnp.exp(level * (math.log(100.0) / (levels - 1)))
    u = sig * sig + 1.0
    weight = u / (sig * sig)
    root = jnp.sqrt(u)
    scales = [1.0 / root, sig, 1.0 / u, sig / root, 2.0 * weight / values * (sig / root), weight / values]
    for i, scale in enumerate(scales):
        by_level[i] = scale
    group = GROUP
    half = wide // 2

    for ref in (xn, xm, e1, o1, e2, o2):
        for at in (0, rows + 1):
            ref[at] = jnp.zeros(ref.shape[1:], BF)
        for at in (0, pairs + 1):
            ref[1 : rows + 1, at] = jnp.zeros((rows,) + ref.shape[2:], BF)
    at = 0
    for ref in noise_refs:
        stage[at : at + ref.shape[0]] = ref[...]
        at += ref.shape[0]
    for k in range(count):
        piece = stage[entry(SOURCE, k)]
        nz[pl.ds(k, cells, stride=count), :] = piece.astype(F32)
        step = entry(STEP, k)
        emb[pl.ds(k, 1), :] = embed_ref[pl.ds(step, 1), :]
        for i in range(len(scales)):
            fac[i, pl.ds(k, 1), :] = by_level[i, pl.ds(step, 1), :]

    def spread(index):
        return fac[index][None]

    scale_in, sigma, skip, scale_out, grad_scale = (spread(i) for i in range(5))
    lane = lax.broadcasted_iota(jnp.int32, (1, 1, count, wide), 3)

    mean_bf = mp_ref[chunk]
    mean = mean_bf.astype(F32)
    residual = tp_ref[chunk].astype(F32) - mean
    noised = residual + sigma * nz[...].reshape(cells, count, wide)
    res[...] = residual.reshape(total, wide)
    noisy[...] = noised.reshape(total, wide)
    xn[1 : rows + 1, 1 : pairs + 1] = (scale_in * noised).astype(BF).reshape(rows, pairs, count, wide)
    xm[1 : rows + 1, 1 : pairs + 1] = mean_bf.reshape(rows, pairs, count, wide)
    for src, dst in ((xn, x2n), (xm, x2m)):
        dst[...] = jnp.where(
            lane < half, src[:, 2 : pairs + 2].astype(F32), src[:, 0:pairs].astype(F32)
        ).astype(BF)

    def view(ref, at, many, p0):
        return ref[at : at + many, p0 : p0 + pairs].reshape(many * pairs * count, wide)

    def stack_in(at, many):
        return [view(xn, at, many, 1), view(xm, at, many, 1), view(x2n, at, many, 0), view(x2m, at, many, 0)]

    def stack_eo(even, odd, at, many):
        return [view(even, at, many, 1), view(odd, at, many, 1), view(odd, at, many, 0), view(even, at, many, 2)]

    def shape4(value, many):
        return value.reshape(many, pairs, count, value.shape[-1])

    tile = group * pairs * count
    emb_pair = jnp.concatenate([emb[...], emb[...]], axis=1)[None]
    def span_of(g):
        return pl.ds(g * tile, tile)

    def conv(stack, weight_ref, g):
        left = jnp.concatenate(sum([stack(g * group + a, group) for a in range(3)], []), axis=1)
        return matmul(left, weight_ref[...])

    def inner(ref, g):
        return ref.at[g * group + 1 : g * group + 1 + group, 1 : pairs + 1]

    def first(g, pre):
        pre = pre.reshape(group * pairs, count, 2 * wide) + emb_pair
        gate = jax.nn.sigmoid(pre)
        act = shape4((pre * gate).astype(BF), group)
        slope1[span_of(g), :] = (gate * (1.0 + pre * (1.0 - gate))).reshape(tile, 2 * wide)
        inner(e1, g)[...] = act[..., :wide]
        inner(o1, g)[...] = act[..., wide:]

    losses = []

    def second(g, pre):
        span = span_of(g)
        gate = jax.nn.sigmoid(pre)
        act = (pre * gate).astype(BF)
        slope = gate * (1.0 + pre * (1.0 - gate))
        act2[span, :] = act
        output = matmul(act, po_ref[...]).reshape(group * pairs, count, wide)
        error = (
            skip * noisy[span, :].reshape(group * pairs, count, wide)
            + scale_out * output
            - res[span, :].reshape(group * pairs, count, wide)
        )
        losses.append(jnp.sum(error * error, axis=0))
        grad_output = (grad_scale * error).astype(BF).reshape(tile, wide)
        gout[span, :] = grad_output
        grad_pre = shape4((matmul(grad_output, pg_ref[...]) * slope).astype(BF), group)
        inner(e2, g)[...] = grad_pre[..., :wide]
        inner(o2, g)[...] = grad_pre[..., wide:]

    partial = []

    def third(g, pre):
        span = span_of(g)
        grad = (pre * slope1[span, :]).astype(BF)
        back[span, :] = grad
        partial.append(jnp.sum(grad.astype(F32).reshape(group * pairs, count, 2 * wide), axis=0))

    stages = (
        (lambda g: conv(stack_in, w1_ref, g), first),
        (lambda g: conv(lambda at, many: stack_eo(e1, o1, at, many), w2_ref, g), second),
        (lambda g: conv(lambda at, many: stack_eo(e2, o2, at, many), v2_ref, g), third),
    )
    groups = rows // group
    depth = wide
    pending = None
    for index, (product, finish) in enumerate(stages):
        for g in range(groups):
            pre = product(g)
            if pending is not None:
                pending()
            pending = functools.partial(finish, g, pre)
        if groups < 3:
            pending()
            pending = None
    proj = lax.dot_general(gout[...], act2[...], TN_FORM, preferred_element_type=F32)
    gt[0:depth, :] = jnp.transpose(view(e2, 1, rows, 1))
    gt[depth : 2 * depth, :] = jnp.transpose(view(o2, 1, rows, 1))
    if pending is not None:
        pending()
    loss = sum(losses[1:], losses[0])
    sums = sum(partial[1:], partial[0])

    def emit(at, size, value):
        if before is not None:
            value = value + before[at : at + size, :]
        out_ref[at : at + size, :] = value

    emit(18 * depth, half, proj[:half, :wide] + proj[half:, wide:])
    for a in range(3):
        right = jnp.concatenate(stack_eo(e1, o1, a, rows), axis=1)
        got = matmul(gt[...], right)
        h0, h1 = got[:depth], got[depth:]
        base = 9 * depth + 3 * a * depth
        emit(base, depth, h1[:, 0:wide] + h0[:, 2 * wide : 3 * wide])
        emit(base + depth, depth, h0[:, 0:wide] + h1[:, wide : 2 * wide])
        emit(base + 2 * depth, depth, h0[:, wide : 2 * wide] + h1[:, 3 * wide : 4 * wide])

    emb[...] = sums[:, :wide] + sums[:, wide:]
    table = 18 * depth + half
    if before is not None:
        out_ref[table : table + levels, :] = before[table : table + levels, :]
    else:
        out_ref[table : table + levels, :] = jnp.zeros((levels, wide), F32)
    for k in range(count):
        at = table + entry(STEP, k)
        out_ref[pl.ds(at, 1), :] = out_ref[pl.ds(at, 1), :] + emb[pl.ds(k, 1), :]

    levels_end = table + levels
    spots = lax.broadcasted_iota(jnp.int32, (8, wide), 0) * wide + lax.broadcasted_iota(jnp.int32, (8, wide), 1)
    sums = jnp.sum(fac[5] * loss, axis=1, keepdims=True)
    owned = jnp.zeros((8, wide), F32)
    for k in range(count):
        owned = owned + jnp.where(spots == entry(PLACE, k), sums[k : k + 1], 0.0)
    if before is not None:
        owned = owned + before[levels_end : levels_end + 8, :]
    out_ref[levels_end:, :] = jnp.zeros((out_ref.shape[0] - levels_end, wide), F32)
    if last:
        rounded = owned.astype(BF).astype(F32)
        out_ref[levels_end + 8 : levels_end + 16, :] = owned - rounded
        owned = rounded
    out_ref[levels_end : levels_end + 8, :] = owned

    gt[...] = jnp.transpose(back[...])
    low = lax.broadcasted_iota(jnp.int32, (depth, wide), 1) < half
    for a in range(3):
        right = jnp.concatenate(stack_in(a, rows), axis=1)
        got = matmul(gt[...], right)
        h0, h1 = got[:depth], got[depth:]

        def merged(first, second):
            n = first[:, 0:wide], second[:, 0:wide]
            m = first[:, wide:], second[:, wide:]
            noise_part = n[0] + pltpu.roll(n[1], half, 1)
            mean_part = pltpu.roll(m[0], half, 1) + m[1]
            return jnp.where(low, noise_part, mean_part)

        base = 3 * a * depth
        direct, rim = slice(0, 2 * wide), slice(2 * wide, 4 * wide)
        emit(base, depth, merged(h1[:, direct], h0[:, rim]))
        emit(base + depth, depth, merged(h0[:, direct], h1[:, direct]))
        emit(base + 2 * depth, depth, merged(h1[:, rim], h0[:, direct]))

    if last:
        size = keep_ref.shape[0]
        core = lax.axis_index("segment")
        keep_ref[...] = out_ref[pl.ds(pl.multiple_of(core * size, 16), size), :]
        send_ref[...] = out_ref[pl.ds(pl.multiple_of((1 - core) * size, 16), size), :].astype(BF)


def unfold_kernel(own_ref, other_ref, one_ref, two_ref, proj_ref, embed_ref, loss_ref, full):
    size, wide = own_ref.shape
    core = lax.axis_index("segment")
    sample = core * lax.axis_size("dp") + lax.axis_index("dp")
    place = sample * lax.axis_size("rows") + lax.axis_index("rows")
    full[pl.ds(pl.multiple_of(core * size, 16), size), :] = own_ref[...]
    full[pl.ds(pl.multiple_of((1 - core) * size, 16), size), :] = other_ref[...]
    depth = one_ref.shape[0]
    for tap in range(9):
        span = slice(tap * wide, (tap + 1) * wide)
        one_ref[:, span] = full[tap * depth : (tap + 1) * depth].astype(F32)
        two_ref[:, span] = full[(9 + tap) * depth : (10 + tap) * depth].astype(F32)
    at = 18 * depth
    for ref in (proj_ref, embed_ref):
        ref[...] = full[at : at + ref.shape[0]].astype(F32)
        at += ref.shape[0]
    spots = lax.broadcasted_iota(jnp.int32, (8, wide), 0) * wide + lax.broadcasted_iota(jnp.int32, (8, wide), 1)
    both = full[at : at + 16].astype(F32)
    loss = jnp.where(spots == place, both[0:8] + both[8:16], 0.0)
    loss_ref[...] = jnp.sum(jnp.sum(loss, axis=1, keepdims=True), axis=0, keepdims=True)


def weights_kernel(one_ref, two_ref, proj_ref, w1_ref, w2_ref, v2_ref, po_ref, pg_ref):
    wide = one_ref.shape[0]
    half = wide // 2
    left, right = slice(0, wide), slice(wide, 2 * wide)
    for ref in (w1_ref, w2_ref, v2_ref, po_ref, pg_ref):
        ref[...] = jnp.zeros(ref.shape, BF)

    def place(ref, a, b, tap, split):
        base = 4 * wide * a

        def put(member, side):
            if split:
                start = {0: 0, 1: half, 3: 2 * wide, 2: 2 * wide + half}[member] + base
                ref[start : start + half, side] = tap[:half]
                ref[start + wide : start + wide + half, side] = tap[half:]
            else:
                start = base + member * wide
                ref[start : start + wide, side] = tap

        if b == 0:
            put(0, left)
            put(1, right)
        elif b == 1:
            put(1, left)
            put(3, right)
        else:
            put(0, right)
            put(2, left)

    for i, (a, b) in enumerate(TAPS):
        span = slice(i * wide, (i + 1) * wide)
        flipped = slice((8 - i) * wide, (9 - i) * wide)
        place(w1_ref, a + 1, b, jnp.transpose(one_ref[:, span]), True)
        place(w2_ref, a + 1, b, jnp.transpose(two_ref[:, span]), False)
        place(v2_ref, a + 1, b, two_ref[:, flipped], False)
    proj = proj_ref[...]
    pg_ref[0:half, left] = proj
    pg_ref[half:, right] = proj
    flat = jnp.transpose(proj.astype(F32)).astype(BF)
    zero = jnp.zeros_like(flat)
    po_ref[left, :] = jnp.concatenate([flat, zero], axis=1)
    po_ref[right, :] = jnp.concatenate([zero, flat], axis=1)


def by_distance(axis, distance):
    return [(i, i ^ distance) for i in range(lax.axis_size(axis))]


def rounded_to_bf16(values):
    return lax.reduce_precision(values, 8, 7)


def take(pieces, index):
    return lax.dynamic_index_in_dim(pieces, index, 0, keepdims=False)


def scatter_sum(values, axis):
    n = values.shape[0]
    me = lax.axis_index(axis)
    out = take(values, me)
    arrived = [
        lax.ppermute(take(values, me ^ d).astype(BF), axis, by_distance(axis, d)) for d in range(1, n)
    ]
    for piece in arrived:
        out = out + piece.astype(F32)
    return out


def gather_all(piece, axis):
    n = lax.axis_size(axis)
    me = lax.axis_index(axis)
    found = [piece] + [lax.ppermute(piece, axis, by_distance(axis, d)) for d in range(1, n)]
    return jnp.stack([sum_select(found, me, i) for i in range(n)])


def sum_select(found, me, index):
    out = found[0]
    for d in range(1, len(found)):
        out = jnp.where((me ^ d) == index, found[d], out)
    return out


def rows_sum(piece, axis):
    n = lax.axis_size(axis)
    if n > 4:
        return lax.psum(piece, axis)
    values = [rounded_to_bf16(piece).astype(BF)]
    for d in range(1, n):
        values.append(lax.ppermute(values[0], axis, by_distance(axis, d)))
    values = [v.astype(F32) for v in values]
    while len(values) > 1:
        values = [values[i] + values[i + 1] for i in range(0, len(values), 2)]
    return values[0]


def per_device(coarse, target, noise, regions, reg_conv, reg_out, conv_one, conv_two, out_proj, step_embed):
    strips = lax.axis_size("rows")
    me = lax.axis_index("rows")
    region = regions[0]
    per_strip = region.shape[1]
    most = noise.shape[2]
    capacity = max(2, (2 * per_strip + strips - 1) // strips)
    phases = 2
    deep = capacity // phases
    count = per_strip // phases
    exchange = strips <= 4
    channels = target.shape[1]
    height, width = target.shape[2:]
    cells = height * height
    wide = 2 * channels
    depth = conv_one.shape[0]
    levels = step_embed.shape[0]

    down = [(i + 1, i) for i in range(strips - 1)]
    own_target = jnp.transpose(target[0], (1, 0, 2))
    own_coarse = jnp.transpose(coarse[0], (1, 0, 2))
    core = lax.axis_index("segment")
    region_table = jnp.transpose(region, (0, 2, 1))

    slot_shape = (cells // 2, wide)
    pieces = strips if exchange else 1

    def packed(phase, region_table, noise):
        return call(
            functools.partial(pack_kernel, phase, exchange, most),
            [jax.ShapeDtypeStruct((strips * deep // pieces,) + slot_shape, BF)] * pieces,
            (region_table, noise[0, 0]),
            (SM, VM),
            [pltpu.SMEM((strips,), jnp.int32)],
            limit=8,
            cost=COSTS[0],
        )

    def sent(packed_pieces):
        if not exchange:
            return [lax.all_to_all(packed_pieces[0], "rows", 0, 0, tiled=True)]
        moved = {d: lax.ppermute(packed_pieces[d], "rows", by_distance("rows", d)) for d in (3, 2, 1) if d < strips}
        return [packed_pieces[0]] + [moved[d] for d in range(1, strips)]

    first_packed = packed(0, region_table, noise)

    reg_channels = reg_conv.shape[1] // 9
    fill = -(-reg_channels // 16) * 16
    per_row = (channels, width)
    even = me % 2 == 0
    pairs = [(i, i ^ 1) for i in range(strips)]
    others = [(i, ((i + 1) ^ 1) - 1) for i in range(1, strips - 1)]
    low_edge, high_edge = own_coarse[:1], own_coarse[height - 1 :]
    inward = lax.ppermute(jnp.where(even, high_edge, low_edge), "rows", pairs)
    outward = lax.ppermute(jnp.where(even, low_edge, high_edge), "rows", others)
    target_low = lax.ppermute(own_target, "rows", down)
    inward, outward = after((inward, outward), (first_packed[0],))
    mean, mean_top, mean_last = call(
        regress_kernel,
        [jax.ShapeDtypeStruct((rows,) + per_row, BF) for rows in (height, height - 1, 1)],
        (even.astype(jnp.int32)[None], inward, own_coarse, outward, reg_conv.T, reg_out),
        (SM,) + (VM,) * 5,
        [pltpu.VMEM((height + 2, 3 * fill, width), BF), pltpu.VMEM((9 * fill, depth), BF)],
        limit=12,
        cost=COSTS[1],
    )
    mean_low = lax.ppermute(mean_top, "rows", down)

    arrived = sent([p if d != 1 else after((p,), (mean_top,))[0] for d, p in enumerate(first_packed)])

    conv_one, conv_two, out_proj = after((conv_one, conv_two, out_proj), (mean_top,))
    stacked = jax.ShapeDtypeStruct((12 * depth, 2 * depth), BF)
    weights = call(
        weights_kernel,
        [stacked] * 3
        + [jax.ShapeDtypeStruct((2 * depth, wide), BF), jax.ShapeDtypeStruct((wide, 2 * depth), BF)],
        (conv_one, conv_two, out_proj),
        (VM,) * 3,
        limit=12,
        cost=COSTS[3],
    )
    patch_shape = jax.ShapeDtypeStruct((phases, cells // 2, count, wide), BF)
    got = pltpu.VMEM((cells // 2 * count, wide), F32)
    table, image = pl.pallas_call(
        functools.partial(own_kernel, exchange, deep, count),
        out_shape=[
            jax.ShapeDtypeStruct((5, per_strip), jnp.int32),
            jax.ShapeDtypeStruct((height, width, wide), BF),
        ],
        in_specs=[SM] + [VM] * 3,
        out_specs=[SM, VM],
        scratch_shapes=[pltpu.SMEM((strips,), jnp.int32)],
        compiler_params=pltpu.CompilerParams(vmem_limit_bytes=16 * MIB),
        cost_estimate=pl.CostEstimate(flops=COSTS[2], bytes_accessed=1, transcendentals=0),
    )(region_table, own_target, mean_top, after((mean_last,), (target_low,))[0])
    later_region, later_noise = after((region_table, noise), (weights[0], image))
    arrived += sent(packed(1, later_region, later_noise))
    mean_p, target_p = call(
        gather_kernel,
        [patch_shape, patch_shape],
        (table, image, mean_low, target_low),
        (SM, VM, VM, VM),
        [pltpu.VMEM((2 * height - 1, width, wide), F32), got, got],
        limit=16,
        cost=COSTS[4],
    )

    cores, groups = lax.axis_size("segment"), lax.axis_size("dp")
    total = cells // 2 * count
    rows_used = 18 * depth + channels + levels
    unit = cores * groups * 16
    rows_all = -(-(rows_used + 16) // unit) * unit
    per_core = rows_all // cores
    sums = jax.ShapeDtypeStruct((rows_all, wide), F32)
    result = ()
    for chunk in range(phases):
        last = chunk == phases - 1
        pad = pltpu.VMEM((height + 2, height // 2 + 2, count, wide), BF)
        rim = pltpu.VMEM((height + 2, height // 2, count, wide), BF)
        used = arrived[: (chunk + 1) * pieces]
        slots_here = sum(piece.shape[0] for piece in used)
        ins = (table,) + tuple(used)
        ins += (mean_p, target_p, step_embed)
        ins += tuple(weights) + tuple(result)
        outs = [sums]
        if last:
            outs = [jax.ShapeDtypeStruct((per_core, wide), F32), jax.ShapeDtypeStruct((per_core, wide), BF)]
        result = call(
            functools.partial(chunk_kernel, chunk, last, len(used)),
            outs,
            ins,
            (SM,) + (VM,) * (len(ins) - 1),
            ([pltpu.VMEM((rows_all, wide), F32)] if last else [])
            + [
                pltpu.VMEM((slots_here, cells // 2, wide), BF),
                pltpu.VMEM((total, wide), F32),
                pad,
                pad,
                rim,
                rim,
                pad,
                pad,
                pad,
                pad,
                pltpu.VMEM((total, 2 * wide), F32),
                pltpu.VMEM((total, wide), F32),
                pltpu.VMEM((total, wide), F32),
                pltpu.VMEM((total, 2 * wide), BF),
                pltpu.VMEM((total, 2 * wide), BF),
                pltpu.VMEM((total, wide), BF),
                pltpu.VMEM((2 * wide, total), BF),
                pltpu.VMEM((count, wide), F32),
                pltpu.VMEM((6, count, wide), F32),
                pltpu.VMEM((6, levels, wide), F32),
            ],
            cost=COSTS[5],
        )

    kept, given = result
    kept = kept + lax.ppermute(given, "segment", by_distance("segment", 1)).astype(F32)
    kept = scatter_sum(kept.reshape(groups, per_core // groups, wide), "dp")
    kept = rows_sum(kept, "rows")
    piece_rows = per_core // groups
    ending = (core == cores - 1) & (lax.axis_index("dp") == groups - 1)
    at = rows_used - (rows_all - piece_rows)
    exact = kept[at : at + 8] + kept[at + 8 : at + 16]
    rounded = rounded_to_bf16(exact)
    pair = jnp.concatenate([rounded, exact - rounded], axis=0)
    pair = jnp.where(ending, pair, kept[at : at + 16])
    kept = rounded_to_bf16(lax.dynamic_update_slice_in_dim(kept, pair, at, 0)).astype(BF)
    kept = gather_all(kept, "dp").reshape(per_core, wide)
    other = lax.ppermute(kept, "segment", by_distance("segment", 1))
    gradient = jax.ShapeDtypeStruct(conv_one.shape, F32)
    grad_one, grad_two, grad_proj, grad_embed, owner_loss = call(
        unfold_kernel,
        [
            gradient,
            gradient,
            jax.ShapeDtypeStruct(out_proj.shape, F32),
            jax.ShapeDtypeStruct(step_embed.shape, F32),
            jax.ShapeDtypeStruct((1, 1), F32),
        ],
        (kept, other),
        (VM, VM),
        [pltpu.VMEM((rows_all, wide), BF)],
        limit=12,
    )
    return jnp.transpose(mean, (1, 0, 2))[None], owner_loss, grad_one, grad_two, grad_proj, grad_embed


def solution(mesh):
    placed = (
        P(("segment", "dp"), None, "rows", None),
        P(("segment", "dp"), None, "rows", None),
        P(("segment", "dp"), "rows", None, None, None),
        P(("segment", "dp"), None, None, None),
        P(),
        P(),
        P(),
        P(),
        P(),
        P(),
    )
    return jax.shard_map(
        per_device,
        mesh=mesh,
        in_specs=placed,
        out_specs=(
            P(("segment", "dp"), None, "rows", None),
            P(("segment", "dp"), "rows"),
            P(),
            P(),
            P(),
            P(),
        ),
        check_vma=False,
    )
```

```python
import functools
import math

import jax
import jax.numpy as jnp
from jax import lax
from jax.experimental import pallas as pl
from jax.experimental.pallas import tpu as pltpu
from jax.sharding import PartitionSpec as P

BF = jnp.bfloat16
F32 = jnp.float32
TAPS = tuple((a, b) for a in (-1, 0, 1) for b in (-1, 0, 1))
NT_FORM = (((1,), (1,)), ((), ()))
TN_FORM = (((0,), (0,)), ((), ()))
MIB = 1024 * 1024
GROUP = 4
COSTS = (1000000000, 1000000000, 10000000000, 1000000000, 10000000000, 10000000000)
UNROLL = 16


def matmul(left, right):
    return jnp.dot(left, right, preferred_element_type=F32)


VM = pl.BlockSpec(memory_space=pltpu.VMEM)
SM = pl.BlockSpec(memory_space=pltpu.SMEM)


def call(kernel, outs, ins, specs, scratch=(), limit=24, cost=0):
    return pl.pallas_call(
        kernel,
        out_shape=outs,
        in_specs=list(specs),
        out_specs=jax.tree.map(lambda _: VM, outs),
        scratch_shapes=list(scratch),
        compiler_params=pltpu.CompilerParams(vmem_limit_bytes=limit * MIB),
        cost_estimate=pl.CostEstimate(flops=cost, bytes_accessed=1, transcendentals=0),
    )(*ins)


def after(values, others):
    return lax.optimization_barrier((values, others))[0]


def starts_kernel(region_ref, starts_ref):
    strips, _, entries = region_ref.shape
    me = lax.axis_index("rows")

    def strip(i, total):
        starts_ref[i] = total

        def entry(k, count):
            return count + jnp.where(region_ref[i, 2, k] == me, 1, 0)

        return lax.fori_loop(0, entries, entry, total, unroll=8)

    lax.fori_loop(0, strips, strip, 0)


def pack_kernel(phase, exchange, most, *refs):
    region_ref, noise_ref = refs[:2]
    out_refs, starts_ref = refs[2:-1], refs[-1]
    starts_kernel(region_ref, starts_ref)
    strips = starts_ref.shape[0]
    me = lax.axis_index("rows")
    channels, cells = noise_ref.shape[1:]
    half = cells // 2
    row = lax.broadcasted_iota(jnp.int32, (half, cells), 0)
    col = lax.broadcasted_iota(jnp.int32, (half, cells), 1)
    even = (col == 2 * row).astype(BF)
    odd = (col == 2 * row + 1).astype(BF)
    low = lax.broadcasted_iota(jnp.int32, (half, 2 * channels), 1) < channels
    deep = out_refs[0].shape[0] * len(out_refs) // strips

    def fill(goal, out_ref, base):
        first_slot = starts_ref[goal] + phase * deep

        def pair(j, carry):
            one_at, two_at = 2 * j, jnp.minimum(2 * j + 1, deep - 1)
            one = noise_ref[jnp.minimum(first_slot + one_at, most - 1)]
            two = noise_ref[jnp.minimum(first_slot + two_at, most - 1)]
            both = jnp.concatenate([one, two], axis=0)
            first = lax.dot_general(even, both, NT_FORM, preferred_element_type=F32)
            second = lax.dot_general(odd, both, NT_FORM, preferred_element_type=F32)
            out_ref[base + two_at] = jnp.where(low, pltpu.roll(first, channels, 1), second).astype(BF)
            out_ref[base + one_at] = jnp.where(low, first, pltpu.roll(second, channels, 1)).astype(BF)
            return carry

        many = (deep + 1) // 2
        lax.fori_loop(0, many, pair, 0, unroll=many)

    if exchange:
        for distance, out_ref in enumerate(out_refs):
            fill(me ^ distance, out_ref, 0)
    else:

        def goal(i, carry):
            fill(i, out_refs[0], i * deep)
            return carry

        lax.fori_loop(0, strips, goal, 0)


SOURCE, STEP, PLACE, TOP, LEFT = range(5)


def tables_kernel(exchange, deep, count, region_ref, table_ref, seen_ref):
    strips, _, entries = region_ref.shape
    me = lax.axis_index("rows")
    sample = lax.axis_index("segment") * lax.axis_size("dp") + lax.axis_index("dp")
    for i in range(strips):
        seen_ref[i] = 0

    def entry(k, carry):
        first, later = carry
        owner = region_ref[me, 2, k]
        rank = seen_ref[owner]
        seen_ref[owner] = rank + 1
        phase = rank // deep
        early = (phase == 0) & (first < count)
        at = jnp.where(early, first, later)
        sender = owner ^ me if exchange else owner
        table_ref[SOURCE, at] = (phase * strips + sender) * deep + rank - phase * deep
        table_ref[STEP, at] = region_ref[me, 3, k]
        table_ref[PLACE, at] = sample * strips + owner
        table_ref[TOP, at] = region_ref[me, 0, k]
        table_ref[LEFT, at] = region_ref[me, 1, k]
        step = jnp.where(early, 1, 0)
        return first + step, later + 1 - step

    lax.fori_loop(0, entries, entry, (0, count))


def regress_kernel(
    even_ref, inward_ref, own_ref, outward_ref, conv_ref, proj_ref, mean_ref, top_ref, last_ref, cols_ref, taps_ref
):
    rows, channels, width = own_ref.shape
    deep = cols_ref.shape[1] // 3
    cols_ref[...] = jnp.zeros(cols_ref.shape, BF)
    taps_ref[...] = jnp.zeros(taps_ref.shape, BF)
    for tap in range(9):
        taps_ref[tap * deep : tap * deep + channels] = (
            conv_ref[tap * channels : (tap + 1) * channels].astype(F32).astype(BF)
        )
    taps = jnp.transpose(taps_ref[...])
    lane = lax.broadcasted_iota(jnp.int32, (channels, width), 1)

    def put(at, cells):
        wide = cells.astype(F32)
        left = jnp.where(lane == 0, 0.0, pltpu.roll(wide, 1, 1)).astype(BF)
        right = jnp.where(lane == width - 1, 0.0, pltpu.roll(wide, width - 1, 1)).astype(BF)
        cols_ref[at, 0:channels] = left
        cols_ref[at, deep : deep + channels] = cells
        cols_ref[at, 2 * deep : 2 * deep + channels] = right

    even = even_ref[0]
    put(even * (rows + 1), inward_ref[0])
    put((1 - even) * (rows + 1), outward_ref[0])

    def fill(r, carry):
        put(r + 1, own_ref[r])
        return carry

    lax.fori_loop(0, rows, fill, 0, unroll=12)

    def one(r, carry):
        stack = cols_ref[pl.ds(r, 3)].reshape(9 * deep, width)
        hidden = matmul(taps, stack)
        act = (hidden * jax.nn.sigmoid(hidden)).astype(BF)
        mean_ref[r] = matmul(proj_ref[...], act).astype(BF)
        return carry

    lax.fori_loop(0, rows, one, 0, unroll=12)
    top_ref[...] = mean_ref[0 : rows - 1]
    last_ref[...] = mean_ref[rows - 1 : rows]


def identity(width):
    return (
        lax.broadcasted_iota(jnp.int32, (width, width), 0)
        == lax.broadcasted_iota(jnp.int32, (width, width), 1)
    ).astype(BF)


def paint(eye, pieces):
    return lax.dot_general(eye, jnp.concatenate(pieces, axis=0), NT_FORM, preferred_element_type=F32)


def own_kernel(exchange, deep, count, region_ref, tgt_ref, top_ref, last_ref, table_ref, image, seen):
    tables_kernel(exchange, deep, count, region_ref, table_ref, seen)
    rows, width, wide = image.shape
    eye = identity(width)
    means = [top_ref[r] for r in range(rows - 1)] + [last_ref[0]]
    for r in range(0, rows, 2):
        both = paint(eye, [means[r], tgt_ref[r], means[r + 1], tgt_ref[r + 1]])
        image[r] = both[:, :wide].astype(BF)
        image[r + 1] = both[:, wide:].astype(BF)


def gather_kernel(table_ref, own, mean_ref, tgt_ref, mp_ref, tp_ref, image, evens, odds):
    rows, width, wide = own.shape
    chunks, _, count, _ = mp_ref.shape
    pairs = rows // 2
    eye = identity(width)
    image[0:rows] = own[...].astype(F32)
    for r in range(0, rows - 1, 2):
        many = min(2, rows - 1 - r)
        both = paint(eye, sum([[mean_ref[r + i], tgt_ref[r + i]] for i in range(many)], []))
        for i in range(many):
            image[rows + r + i] = both[:, i * wide : (i + 1) * wide]
    half = wide // 2
    low = lax.broadcasted_iota(jnp.int32, evens.shape, 1) < half
    for chunk in range(chunks):

        def patch(k, carry, chunk=chunk):
            top = table_ref[TOP, chunk * count + k]
            left = table_ref[LEFT, chunk * count + k]
            for r in range(rows):
                span = pl.ds(r * pairs * count + k, pairs, stride=count)
                evens[span, :] = image[top + r, pl.ds(left, pairs, stride=2), :]
                odds[span, :] = image[top + r, pl.ds(left + 1, pairs, stride=2), :]
            return carry

        lax.fori_loop(0, count, patch, 0, unroll=min(UNROLL, count))
        even, odd = evens[...], odds[...]
        mean = jnp.where(low, even, pltpu.roll(odd, half, 1))
        goal = jnp.where(low, pltpu.roll(even, half, 1), odd)
        mp_ref[chunk] = mean.astype(BF).reshape(mp_ref.shape[1:])
        tp_ref[chunk] = goal.astype(BF).reshape(tp_ref.shape[1:])


def chunk_kernel(chunk, last, pieces, *refs):
    table_ref = refs[0]
    noise_refs = refs[1 : 1 + pieces]
    refs = refs[1 + pieces :]
    (mp_ref, tp_ref, embed_ref, w1_ref, w2_ref, v2_ref, po_ref, pg_ref) = refs[:8]
    refs = refs[8:]
    before = None
    if chunk > 0:
        before, refs = refs[0], refs[1:]
    if last:
        keep_ref, send_ref, out_ref = refs[:3]
        refs = refs[3:]
    else:
        out_ref, refs = refs[0], refs[1:]
    (stage, nz, xn, xm, x2n, x2m, e1, o1, e2, o2, slope1, res, noisy, act2, back, gout, gt, emb, fac, by_level) = refs
    _, cells, count, wide = mp_ref.shape
    rows = 12
    pairs = cells // rows
    total = cells * count
    levels = embed_ref.shape[0]

    def entry(field, k):
        return table_ref[field, chunk * count + k]

    values = cells * wide
    level = lax.broadcasted_iota(jnp.int32, (levels, wide), 0).astype(F32)
    sig = 0.1 * jnp.exp(level * (math.log(100.0) / (levels - 1)))
    u = sig * sig + 1.0
    weight = u / (sig * sig)
    root = jnp.sqrt(u)
    scales = [1.0 / root, sig, 1.0 / u, sig / root, 2.0 * weight / values * (sig / root), weight / values]
    for i, scale in enumerate(scales):
        by_level[i] = scale
    group = GROUP
    half = wide // 2

    for ref in (xn, xm, e1, o1, e2, o2):
        for at in (0, rows + 1):
            ref[at] = jnp.zeros(ref.shape[1:], BF)
        for at in (0, pairs + 1):
            ref[1 : rows + 1, at] = jnp.zeros((rows,) + ref.shape[2:], BF)
    at = 0
    for ref in noise_refs:
        stage[at : at + ref.shape[0]] = ref[...]
        at += ref.shape[0]
    for k in range(count):
        piece = stage[entry(SOURCE, k)]
        nz[pl.ds(k, cells, stride=count), :] = piece.astype(F32)
        step = entry(STEP, k)
        emb[pl.ds(k, 1), :] = embed_ref[pl.ds(step, 1), :]
        for i in range(len(scales)):
            fac[i, pl.ds(k, 1), :] = by_level[i, pl.ds(step, 1), :]

    def spread(index):
        return fac[index][None]

    scale_in, sigma, skip, scale_out, grad_scale = (spread(i) for i in range(5))
    lane = lax.broadcasted_iota(jnp.int32, (1, 1, count, wide), 3)

    mean_bf = mp_ref[chunk]
    mean = mean_bf.astype(F32)
    residual = tp_ref[chunk].astype(F32) - mean
    noised = residual + sigma * nz[...].reshape(cells, count, wide)
    res[...] = residual.reshape(total, wide)
    noisy[...] = noised.reshape(total, wide)
    xn[1 : rows + 1, 1 : pairs + 1] = (scale_in * noised).astype(BF).reshape(rows, pairs, count, wide)
    xm[1 : rows + 1, 1 : pairs + 1] = mean_bf.reshape(rows, pairs, count, wide)
    for src, dst in ((xn, x2n), (xm, x2m)):
        dst[...] = jnp.where(
            lane < half, src[:, 2 : pairs + 2].astype(F32), src[:, 0:pairs].astype(F32)
        ).astype(BF)

    def view(ref, at, many, p0):
        return ref[at : at + many, p0 : p0 + pairs].reshape(many * pairs * count, wide)

    def stack_in(at, many):
        return [view(xn, at, many, 1), view(xm, at, many, 1), view(x2n, at, many, 0), view(x2m, at, many, 0)]

    def stack_eo(even, odd, at, many):
        return [view(even, at, many, 1), view(odd, at, many, 1), view(odd, at, many, 0), view(even, at, many, 2)]

    def shape4(value, many):
        return value.reshape(many, pairs, count, value.shape[-1])

    tile = group * pairs * count
    emb_pair = jnp.concatenate([emb[...], emb[...]], axis=1)[None]
    def span_of(g):
        return pl.ds(g * tile, tile)

    def conv(stack, weight_ref, g):
        left = jnp.concatenate(sum([stack(g * group + a, group) for a in range(3)], []), axis=1)
        return matmul(left, weight_ref[...])

    def inner(ref, g):
        return ref.at[g * group + 1 : g * group + 1 + group, 1 : pairs + 1]

    def first(g, pre):
        pre = pre.reshape(group * pairs, count, 2 * wide) + emb_pair
        gate = jax.nn.sigmoid(pre)
        act = shape4((pre * gate).astype(BF), group)
        slope1[span_of(g), :] = (gate * (1.0 + pre * (1.0 - gate))).reshape(tile, 2 * wide)
        inner(e1, g)[...] = act[..., :wide]
        inner(o1, g)[...] = act[..., wide:]

    losses = []

    def second(g, pre):
        span = span_of(g)
        gate = jax.nn.sigmoid(pre)
        act = (pre * gate).astype(BF)
        slope = gate * (1.0 + pre * (1.0 - gate))
        act2[span, :] = act
        output = matmul(act, po_ref[...]).reshape(group * pairs, count, wide)
        error = (
            skip * noisy[span, :].reshape(group * pairs, count, wide)
            + scale_out * output
            - res[span, :].reshape(group * pairs, count, wide)
        )
        losses.append(jnp.sum(error * error, axis=0))
        grad_output = (grad_scale * error).astype(BF).reshape(tile, wide)
        gout[span, :] = grad_output
        grad_pre = shape4((matmul(grad_output, pg_ref[...]) * slope).astype(BF), group)
        inner(e2, g)[...] = grad_pre[..., :wide]
        inner(o2, g)[...] = grad_pre[..., wide:]

    partial = []

    def third(g, pre):
        span = span_of(g)
        grad = (pre * slope1[span, :]).astype(BF)
        back[span, :] = grad
        partial.append(jnp.sum(grad.astype(F32).reshape(group * pairs, count, 2 * wide), axis=0))

    stages = (
        (lambda g: conv(stack_in, w1_ref, g), first),
        (lambda g: conv(lambda at, many: stack_eo(e1, o1, at, many), w2_ref, g), second),
        (lambda g: conv(lambda at, many: stack_eo(e2, o2, at, many), v2_ref, g), third),
    )
    groups = rows // group
    depth = wide
    pending = None
    for index, (product, finish) in enumerate(stages):
        for g in range(groups):
            pre = product(g)
            if pending is not None:
                pending()
            pending = functools.partial(finish, g, pre)
        if groups < 3:
            pending()
            pending = None
    proj = lax.dot_general(gout[...], act2[...], TN_FORM, preferred_element_type=F32)
    gt[0:depth, :] = jnp.transpose(view(e2, 1, rows, 1))
    gt[depth : 2 * depth, :] = jnp.transpose(view(o2, 1, rows, 1))
    if pending is not None:
        pending()
    loss = sum(losses[1:], losses[0])
    sums = sum(partial[1:], partial[0])

    def emit(at, size, value):
        if before is not None:
            value = value + before[at : at + size, :]
        out_ref[at : at + size, :] = value

    emit(18 * depth, half, proj[:half, :wide] + proj[half:, wide:])
    for a in range(3):
        right = jnp.concatenate(stack_eo(e1, o1, a, rows), axis=1)
        got = matmul(gt[...], right)
        h0, h1 = got[:depth], got[depth:]
        base = 9 * depth + 3 * a * depth
        emit(base, depth, h1[:, 0:wide] + h0[:, 2 * wide : 3 * wide])
        emit(base + depth, depth, h0[:, 0:wide] + h1[:, wide : 2 * wide])
        emit(base + 2 * depth, depth, h0[:, wide : 2 * wide] + h1[:, 3 * wide : 4 * wide])

    emb[...] = sums[:, :wide] + sums[:, wide:]
    table = 18 * depth + half
    if before is not None:
        out_ref[table : table + levels, :] = before[table : table + levels, :]
    else:
        out_ref[table : table + levels, :] = jnp.zeros((levels, wide), F32)
    for k in range(count):
        at = table + entry(STEP, k)
        out_ref[pl.ds(at, 1), :] = out_ref[pl.ds(at, 1), :] + emb[pl.ds(k, 1), :]

    levels_end = table + levels
    spots = lax.broadcasted_iota(jnp.int32, (8, wide), 0) * wide + lax.broadcasted_iota(jnp.int32, (8, wide), 1)
    sums = jnp.sum(fac[5] * loss, axis=1, keepdims=True)
    owned = jnp.zeros((8, wide), F32)
    for k in range(count):
        owned = owned + jnp.where(spots == entry(PLACE, k), sums[k : k + 1], 0.0)
    if before is not None:
        owned = owned + before[levels_end : levels_end + 8, :]
    out_ref[levels_end:, :] = jnp.zeros((out_ref.shape[0] - levels_end, wide), F32)
    if last:
        rounded = owned.astype(BF).astype(F32)
        out_ref[levels_end + 8 : levels_end + 16, :] = owned - rounded
        owned = rounded
    out_ref[levels_end : levels_end + 8, :] = owned

    gt[...] = jnp.transpose(back[...])
    low = lax.broadcasted_iota(jnp.int32, (depth, wide), 1) < half
    for a in range(3):
        right = jnp.concatenate(stack_in(a, rows), axis=1)
        got = matmul(gt[...], right)
        h0, h1 = got[:depth], got[depth:]

        def merged(first, second):
            n = first[:, 0:wide], second[:, 0:wide]
            m = first[:, wide:], second[:, wide:]
            noise_part = n[0] + pltpu.roll(n[1], half, 1)
            mean_part = pltpu.roll(m[0], half, 1) + m[1]
            return jnp.where(low, noise_part, mean_part)

        base = 3 * a * depth
        direct, rim = slice(0, 2 * wide), slice(2 * wide, 4 * wide)
        emit(base, depth, merged(h1[:, direct], h0[:, rim]))
        emit(base + depth, depth, merged(h0[:, direct], h1[:, direct]))
        emit(base + 2 * depth, depth, merged(h1[:, rim], h0[:, direct]))

    if last:
        size = keep_ref.shape[0]
        core = lax.axis_index("segment")
        keep_ref[...] = out_ref[pl.ds(pl.multiple_of(core * size, 16), size), :]
        send_ref[...] = out_ref[pl.ds(pl.multiple_of((1 - core) * size, 16), size), :].astype(BF)


def unfold_kernel(own_ref, other_ref, one_ref, two_ref, proj_ref, embed_ref, loss_ref, full):
    size, wide = own_ref.shape
    core = lax.axis_index("segment")
    sample = core * lax.axis_size("dp") + lax.axis_index("dp")
    place = sample * lax.axis_size("rows") + lax.axis_index("rows")
    full[pl.ds(pl.multiple_of(core * size, 16), size), :] = own_ref[...]
    full[pl.ds(pl.multiple_of((1 - core) * size, 16), size), :] = other_ref[...]
    depth = one_ref.shape[0]
    for tap in range(9):
        span = slice(tap * wide, (tap + 1) * wide)
        one_ref[:, span] = full[tap * depth : (tap + 1) * depth].astype(F32)
        two_ref[:, span] = full[(9 + tap) * depth : (10 + tap) * depth].astype(F32)
    at = 18 * depth
    for ref in (proj_ref, embed_ref):
        ref[...] = full[at : at + ref.shape[0]].astype(F32)
        at += ref.shape[0]
    spots = lax.broadcasted_iota(jnp.int32, (8, wide), 0) * wide + lax.broadcasted_iota(jnp.int32, (8, wide), 1)
    both = full[at : at + 16].astype(F32)
    loss = jnp.where(spots == place, both[0:8] + both[8:16], 0.0)
    loss_ref[...] = jnp.sum(jnp.sum(loss, axis=1, keepdims=True), axis=0, keepdims=True)


def weights_kernel(one_ref, two_ref, proj_ref, w1_ref, w2_ref, v2_ref, po_ref, pg_ref):
    wide = one_ref.shape[0]
    half = wide // 2
    left, right = slice(0, wide), slice(wide, 2 * wide)
    for ref in (w1_ref, w2_ref, v2_ref, po_ref, pg_ref):
        ref[...] = jnp.zeros(ref.shape, BF)

    def place(ref, a, b, tap, split):
        base = 4 * wide * a

        def put(member, side):
            if split:
                start = {0: 0, 1: half, 3: 2 * wide, 2: 2 * wide + half}[member] + base
                ref[start : start + half, side] = tap[:half]
                ref[start + wide : start + wide + half, side] = tap[half:]
            else:
                start = base + member * wide
                ref[start : start + wide, side] = tap

        if b == 0:
            put(0, left)
            put(1, right)
        elif b == 1:
            put(1, left)
            put(3, right)
        else:
            put(0, right)
            put(2, left)

    for i, (a, b) in enumerate(TAPS):
        span = slice(i * wide, (i + 1) * wide)
        flipped = slice((8 - i) * wide, (9 - i) * wide)
        place(w1_ref, a + 1, b, jnp.transpose(one_ref[:, span]), True)
        place(w2_ref, a + 1, b, jnp.transpose(two_ref[:, span]), False)
        place(v2_ref, a + 1, b, two_ref[:, flipped], False)
    proj = proj_ref[...]
    pg_ref[0:half, left] = proj
    pg_ref[half:, right] = proj
    flat = jnp.transpose(proj.astype(F32)).astype(BF)
    zero = jnp.zeros_like(flat)
    po_ref[left, :] = jnp.concatenate([flat, zero], axis=1)
    po_ref[right, :] = jnp.concatenate([zero, flat], axis=1)


def by_distance(axis, distance):
    return [(i, i ^ distance) for i in range(lax.axis_size(axis))]


def rounded_to_bf16(values):
    return lax.reduce_precision(values, 8, 7)


def take(pieces, index):
    return lax.dynamic_index_in_dim(pieces, index, 0, keepdims=False)


def scatter_sum(values, axis):
    n = values.shape[0]
    me = lax.axis_index(axis)
    out = take(values, me)
    arrived = [
        lax.ppermute(take(values, me ^ d).astype(BF), axis, by_distance(axis, d)) for d in reversed(range(1, n))
    ]
    for piece in arrived:
        out = out + piece.astype(F32)
    return out


def gather_all(piece, axis):
    n = lax.axis_size(axis)
    me = lax.axis_index(axis)
    moved = {d: lax.ppermute(piece, axis, by_distance(axis, d)) for d in reversed(range(1, n))}
    found = [piece] + [moved[d] for d in range(1, n)]
    return jnp.stack([sum_select(found, me, i) for i in range(n)])


def sum_select(found, me, index):
    out = found[0]
    for d in range(1, len(found)):
        out = jnp.where((me ^ d) == index, found[d], out)
    return out


def rows_sum(piece, axis):
    n = lax.axis_size(axis)
    if n > 4:
        return lax.psum(piece, axis)
    values = [rounded_to_bf16(piece).astype(BF)]
    moved = {d: lax.ppermute(values[0], axis, by_distance(axis, d)) for d in reversed(range(1, n))}
    values += [moved[d] for d in range(1, n)]
    values = [v.astype(F32) for v in values]
    while len(values) > 1:
        values = [values[i] + values[i + 1] for i in range(0, len(values), 2)]
    return values[0]


def per_device(coarse, target, noise, regions, reg_conv, reg_out, conv_one, conv_two, out_proj, step_embed):
    strips = lax.axis_size("rows")
    me = lax.axis_index("rows")
    region = regions[0]
    per_strip = region.shape[1]
    most = noise.shape[2]
    capacity = max(2, (2 * per_strip + strips - 1) // strips)
    phases = 2
    deep = capacity // phases
    count = per_strip // phases
    exchange = strips <= 4
    channels = target.shape[1]
    height, width = target.shape[2:]
    cells = height * height
    wide = 2 * channels
    depth = conv_one.shape[0]
    levels = step_embed.shape[0]

    down = [(i + 1, i) for i in range(strips - 1)]
    own_target = jnp.transpose(target[0], (1, 0, 2))
    own_coarse = jnp.transpose(coarse[0], (1, 0, 2))
    core = lax.axis_index("segment")
    region_table = jnp.transpose(region, (0, 2, 1))

    slot_shape = (cells // 2, wide)
    pieces = strips if exchange else 1

    def packed(phase, region_table, noise):
        return call(
            functools.partial(pack_kernel, phase, exchange, most),
            [jax.ShapeDtypeStruct((strips * deep // pieces,) + slot_shape, BF)] * pieces,
            (region_table, noise[0, 0]),
            (SM, VM),
            [pltpu.SMEM((strips,), jnp.int32)],
            limit=8,
            cost=COSTS[0],
        )

    def sent(packed_pieces):
        if not exchange:
            return [lax.all_to_all(packed_pieces[0], "rows", 0, 0, tiled=True)]
        moved = {d: lax.ppermute(packed_pieces[d], "rows", by_distance("rows", d)) for d in (3, 2, 1) if d < strips}
        return [packed_pieces[0]] + [moved[d] for d in range(1, strips)]

    first_packed = packed(0, region_table, noise)

    reg_channels = reg_conv.shape[1] // 9
    fill = -(-reg_channels // 16) * 16
    per_row = (channels, width)
    even = me % 2 == 0
    pairs = [(i, i ^ 1) for i in range(strips)]
    others = [(i, ((i + 1) ^ 1) - 1) for i in range(1, strips - 1)]
    low_edge, high_edge = own_coarse[:1], own_coarse[height - 1 :]
    inward = lax.ppermute(jnp.where(even, high_edge, low_edge), "rows", pairs)
    outward = lax.ppermute(jnp.where(even, low_edge, high_edge), "rows", others)
    target_low = lax.ppermute(own_target, "rows", down)
    inward, outward = after((inward, outward), (first_packed[0],))
    mean, mean_top, mean_last = call(
        regress_kernel,
        [jax.ShapeDtypeStruct((rows,) + per_row, BF) for rows in (height, height - 1, 1)],
        (even.astype(jnp.int32)[None], inward, own_coarse, outward, reg_conv.T, reg_out),
        (SM,) + (VM,) * 5,
        [pltpu.VMEM((height + 2, 3 * fill, width), BF), pltpu.VMEM((9 * fill, depth), BF)],
        limit=12,
        cost=COSTS[1],
    )
    mean_low = lax.ppermute(mean_top, "rows", down)

    arrived = sent([p if d != 1 else after((p,), (mean_top,))[0] for d, p in enumerate(first_packed)])

    conv_one, conv_two, out_proj = after((conv_one, conv_two, out_proj), (mean_top,))
    stacked = jax.ShapeDtypeStruct((12 * depth, 2 * depth), BF)
    weights = call(
        weights_kernel,
        [stacked] * 3
        + [jax.ShapeDtypeStruct((2 * depth, wide), BF), jax.ShapeDtypeStruct((wide, 2 * depth), BF)],
        (conv_one, conv_two, out_proj),
        (VM,) * 3,
        limit=12,
        cost=COSTS[3],
    )
    patch_shape = jax.ShapeDtypeStruct((phases, cells // 2, count, wide), BF)
    got = pltpu.VMEM((cells // 2 * count, wide), F32)
    table, image = pl.pallas_call(
        functools.partial(own_kernel, exchange, deep, count),
        out_shape=[
            jax.ShapeDtypeStruct((5, per_strip), jnp.int32),
            jax.ShapeDtypeStruct((height, width, wide), BF),
        ],
        in_specs=[SM] + [VM] * 3,
        out_specs=[SM, VM],
        scratch_shapes=[pltpu.SMEM((strips,), jnp.int32)],
        compiler_params=pltpu.CompilerParams(vmem_limit_bytes=16 * MIB),
        cost_estimate=pl.CostEstimate(flops=COSTS[2], bytes_accessed=1, transcendentals=0),
    )(region_table, own_target, mean_top, after((mean_last,), (target_low,))[0])
    later_region, later_noise = after((region_table, noise), (weights[0], image))
    arrived += sent(packed(1, later_region, later_noise))
    mean_p, target_p = call(
        gather_kernel,
        [patch_shape, patch_shape],
        (table, image, mean_low, target_low),
        (SM, VM, VM, VM),
        [pltpu.VMEM((2 * height - 1, width, wide), F32), got, got],
        limit=16,
        cost=COSTS[4],
    )

    cores, groups = lax.axis_size("segment"), lax.axis_size("dp")
    total = cells // 2 * count
    rows_used = 18 * depth + channels + levels
    unit = cores * groups * 16
    rows_all = -(-(rows_used + 16) // unit) * unit
    per_core = rows_all // cores
    sums = jax.ShapeDtypeStruct((rows_all, wide), F32)
    result = ()
    for chunk in range(phases):
        last = chunk == phases - 1
        pad = pltpu.VMEM((height + 2, height // 2 + 2, count, wide), BF)
        rim = pltpu.VMEM((height + 2, height // 2, count, wide), BF)
        used = arrived[: (chunk + 1) * pieces]
        slots_here = sum(piece.shape[0] for piece in used)
        ins = (table,) + tuple(used)
        ins += (mean_p, target_p, step_embed)
        ins += tuple(weights) + tuple(result)
        outs = [sums]
        if last:
            outs = [jax.ShapeDtypeStruct((per_core, wide), F32), jax.ShapeDtypeStruct((per_core, wide), BF)]
        result = call(
            functools.partial(chunk_kernel, chunk, last, len(used)),
            outs,
            ins,
            (SM,) + (VM,) * (len(ins) - 1),
            ([pltpu.VMEM((rows_all, wide), F32)] if last else [])
            + [
                pltpu.VMEM((slots_here, cells // 2, wide), BF),
                pltpu.VMEM((total, wide), F32),
                pad,
                pad,
                rim,
                rim,
                pad,
                pad,
                pad,
                pad,
                pltpu.VMEM((total, 2 * wide), F32),
                pltpu.VMEM((total, wide), F32),
                pltpu.VMEM((total, wide), F32),
                pltpu.VMEM((total, 2 * wide), BF),
                pltpu.VMEM((total, 2 * wide), BF),
                pltpu.VMEM((total, wide), BF),
                pltpu.VMEM((2 * wide, total), BF),
                pltpu.VMEM((count, wide), F32),
                pltpu.VMEM((6, count, wide), F32),
                pltpu.VMEM((6, levels, wide), F32),
            ],
            cost=COSTS[5],
        )

    kept, given = result
    kept = kept + lax.ppermute(given, "segment", by_distance("segment", 1)).astype(F32)
    kept = scatter_sum(kept.reshape(groups, per_core // groups, wide), "dp")
    kept = rows_sum(kept, "rows")
    piece_rows = per_core // groups
    ending = (core == cores - 1) & (lax.axis_index("dp") == groups - 1)
    at = rows_used - (rows_all - piece_rows)
    exact = kept[at : at + 8] + kept[at + 8 : at + 16]
    rounded = rounded_to_bf16(exact)
    pair = jnp.concatenate([rounded, exact - rounded], axis=0)
    pair = jnp.where(ending, pair, kept[at : at + 16])
    kept = rounded_to_bf16(lax.dynamic_update_slice_in_dim(kept, pair, at, 0)).astype(BF)
    kept = gather_all(kept, "dp").reshape(per_core, wide)
    other = lax.ppermute(kept, "segment", by_distance("segment", 1))
    gradient = jax.ShapeDtypeStruct(conv_one.shape, F32)
    grad_one, grad_two, grad_proj, grad_embed, owner_loss = call(
        unfold_kernel,
        [
            gradient,
            gradient,
            jax.ShapeDtypeStruct(out_proj.shape, F32),
            jax.ShapeDtypeStruct(step_embed.shape, F32),
            jax.ShapeDtypeStruct((1, 1), F32),
        ],
        (kept, other),
        (VM, VM),
        [pltpu.VMEM((rows_all, wide), BF)],
        limit=12,
    )
    return jnp.transpose(mean, (1, 0, 2))[None], owner_loss, grad_one, grad_two, grad_proj, grad_embed


def solution(mesh):
    placed = (
        P(("segment", "dp"), None, "rows", None),
        P(("segment", "dp"), None, "rows", None),
        P(("segment", "dp"), "rows", None, None, None),
        P(("segment", "dp"), None, None, None),
        P(),
        P(),
        P(),
        P(),
        P(),
        P(),
    )
    return jax.shard_map(
        per_device,
        mesh=mesh,
        in_specs=placed,
        out_specs=(
            P(("segment", "dp"), None, "rows", None),
            P(("segment", "dp"), "rows"),
            P(),
            P(),
            P(),
            P(),
        ),
        check_vma=False,
    )
```

```python
import functools
import math

import jax
import jax.numpy as jnp
from jax import lax
from jax.experimental import pallas as pl
from jax.experimental.pallas import tpu as pltpu
from jax.sharding import PartitionSpec as P

BF = jnp.bfloat16
F32 = jnp.float32
TAPS = tuple((a, b) for a in (-1, 0, 1) for b in (-1, 0, 1))
NT_FORM = (((1,), (1,)), ((), ()))
TN_FORM = (((0,), (0,)), ((), ()))
MIB = 1024 * 1024
GROUP = 4
COSTS = (1000000000, 1000000000, 10000000000, 1000000000, 10000000000, 10000000000)
UNROLL = 16


def matmul(left, right):
    return jnp.dot(left, right, preferred_element_type=F32)


VM = pl.BlockSpec(memory_space=pltpu.VMEM)
SM = pl.BlockSpec(memory_space=pltpu.SMEM)


def call(kernel, outs, ins, specs, scratch=(), limit=24, cost=0):
    return pl.pallas_call(
        kernel,
        out_shape=outs,
        in_specs=list(specs),
        out_specs=jax.tree.map(lambda _: VM, outs),
        scratch_shapes=list(scratch),
        compiler_params=pltpu.CompilerParams(vmem_limit_bytes=limit * MIB),
        cost_estimate=pl.CostEstimate(flops=cost, bytes_accessed=1, transcendentals=0),
    )(*ins)


def after(values, others):
    return lax.optimization_barrier((values, others))[0]


def starts_kernel(region_ref, starts_ref):
    strips, _, entries = region_ref.shape
    me = lax.axis_index("rows")

    def strip(i, total):
        starts_ref[i] = total

        def entry(k, count):
            return count + jnp.where(region_ref[i, 2, k] == me, 1, 0)

        return lax.fori_loop(0, entries, entry, total, unroll=8)

    lax.fori_loop(0, strips, strip, 0)


def pack_kernel(phase, exchange, most, *refs):
    region_ref, noise_ref = refs[:2]
    out_refs, starts_ref = refs[2:-1], refs[-1]
    starts_kernel(region_ref, starts_ref)
    strips = starts_ref.shape[0]
    me = lax.axis_index("rows")
    channels, cells = noise_ref.shape[1:]
    half = cells // 2
    row = lax.broadcasted_iota(jnp.int32, (half, cells), 0)
    col = lax.broadcasted_iota(jnp.int32, (half, cells), 1)
    even = (col == 2 * row).astype(BF)
    odd = (col == 2 * row + 1).astype(BF)
    low = lax.broadcasted_iota(jnp.int32, (half, 2 * channels), 1) < channels
    deep = out_refs[0].shape[0] * len(out_refs) // strips

    def fill(goal, out_ref, base):
        first_slot = starts_ref[goal] + phase * deep

        def pair(j, carry):
            one_at, two_at = 2 * j, jnp.minimum(2 * j + 1, deep - 1)
            one = noise_ref[jnp.minimum(first_slot + one_at, most - 1)]
            two = noise_ref[jnp.minimum(first_slot + two_at, most - 1)]
            both = jnp.concatenate([one, two], axis=0)
            first = lax.dot_general(even, both, NT_FORM, preferred_element_type=F32)
            second = lax.dot_general(odd, both, NT_FORM, preferred_element_type=F32)
            out_ref[base + two_at] = jnp.where(low, pltpu.roll(first, channels, 1), second).astype(BF)
            out_ref[base + one_at] = jnp.where(low, first, pltpu.roll(second, channels, 1)).astype(BF)
            return carry

        many = (deep + 1) // 2
        lax.fori_loop(0, many, pair, 0, unroll=many)

    if exchange:
        for distance, out_ref in enumerate(out_refs):
            fill(me ^ distance, out_ref, 0)
    else:

        def goal(i, carry):
            fill(i, out_refs[0], i * deep)
            return carry

        lax.fori_loop(0, strips, goal, 0)


SOURCE, STEP, PLACE, TOP, LEFT = range(5)


def tables_kernel(exchange, deep, count, region_ref, table_ref, seen_ref):
    strips, _, entries = region_ref.shape
    me = lax.axis_index("rows")
    sample = lax.axis_index("segment") * lax.axis_size("dp") + lax.axis_index("dp")
    for i in range(strips):
        seen_ref[i] = 0

    def entry(k, carry):
        first, later = carry
        owner = region_ref[me, 2, k]
        rank = seen_ref[owner]
        seen_ref[owner] = rank + 1
        phase = rank // deep
        early = (phase == 0) & (first < count)
        at = jnp.where(early, first, later)
        sender = owner ^ me if exchange else owner
        table_ref[SOURCE, at] = (phase * strips + sender) * deep + rank - phase * deep
        table_ref[STEP, at] = region_ref[me, 3, k]
        table_ref[PLACE, at] = sample * strips + owner
        table_ref[TOP, at] = region_ref[me, 0, k]
        table_ref[LEFT, at] = region_ref[me, 1, k]
        step = jnp.where(early, 1, 0)
        return first + step, later + 1 - step

    lax.fori_loop(0, entries, entry, (0, count))


def regress_kernel(
    even_ref, inward_ref, own_ref, outward_ref, conv_ref, proj_ref, mean_ref, top_ref, last_ref, cols_ref, taps_ref
):
    rows, channels, width = own_ref.shape
    deep = cols_ref.shape[1] // 3
    cols_ref[...] = jnp.zeros(cols_ref.shape, BF)
    taps_ref[...] = jnp.zeros(taps_ref.shape, BF)
    for tap in range(9):
        taps_ref[tap * deep : tap * deep + channels] = (
            conv_ref[tap * channels : (tap + 1) * channels].astype(F32).astype(BF)
        )
    taps = jnp.transpose(taps_ref[...])
    lane = lax.broadcasted_iota(jnp.int32, (channels, width), 1)

    def put(at, cells):
        wide = cells.astype(F32)
        left = jnp.where(lane == 0, 0.0, pltpu.roll(wide, 1, 1)).astype(BF)
        right = jnp.where(lane == width - 1, 0.0, pltpu.roll(wide, width - 1, 1)).astype(BF)
        cols_ref[at, 0:channels] = left
        cols_ref[at, deep : deep + channels] = cells
        cols_ref[at, 2 * deep : 2 * deep + channels] = right

    even = even_ref[0]
    put(even * (rows + 1), inward_ref[0])
    put((1 - even) * (rows + 1), outward_ref[0])

    def fill(r, carry):
        put(r + 1, own_ref[r])
        return carry

    lax.fori_loop(0, rows, fill, 0, unroll=12)

    def one(r, carry):
        stack = cols_ref[pl.ds(r, 3)].reshape(9 * deep, width)
        hidden = matmul(taps, stack)
        act = (hidden * jax.nn.sigmoid(hidden)).astype(BF)
        mean_ref[r] = matmul(proj_ref[...], act).astype(BF)
        return carry

    lax.fori_loop(0, rows, one, 0, unroll=12)
    top_ref[...] = mean_ref[0 : rows - 1]
    last_ref[...] = mean_ref[rows - 1 : rows]


def identity(width):
    return (
        lax.broadcasted_iota(jnp.int32, (width, width), 0)
        == lax.broadcasted_iota(jnp.int32, (width, width), 1)
    ).astype(BF)


def paint(eye, pieces):
    return lax.dot_general(eye, jnp.concatenate(pieces, axis=0), NT_FORM, preferred_element_type=F32)


def own_kernel(exchange, deep, count, region_ref, tgt_ref, top_ref, last_ref, table_ref, image, seen):
    tables_kernel(exchange, deep, count, region_ref, table_ref, seen)
    rows, width, wide = image.shape
    eye = identity(width)
    means = [top_ref[r] for r in range(rows - 1)] + [last_ref[0]]
    for r in range(0, rows, 2):
        both = paint(eye, [means[r], tgt_ref[r], means[r + 1], tgt_ref[r + 1]])
        image[r] = both[:, :wide].astype(BF)
        image[r + 1] = both[:, wide:].astype(BF)


def gather_kernel(table_ref, own, mean_ref, tgt_ref, mp_ref, tp_ref, image, evens, odds):
    rows, width, wide = own.shape
    chunks, _, count, _ = mp_ref.shape
    pairs = rows // 2
    eye = identity(width)
    image[0:rows, 0:width] = own[...].astype(F32)
    for r in range(0, rows - 1, 2):
        many = min(2, rows - 1 - r)
        both = paint(eye, sum([[mean_ref[r + i], tgt_ref[r + i]] for i in range(many)], []))
        for i in range(many):
            image[rows + r + i, 0:width] = both[:, i * wide : (i + 1) * wide]
    half = wide // 2
    total = rows * pairs * count
    low = lax.broadcasted_iota(jnp.int32, (total, wide), 1) < half
    for chunk in range(chunks):

        def patch(k, carry, chunk=chunk):
            top = table_ref[TOP, chunk * count + k]
            left = table_ref[LEFT, chunk * count + k]
            for r in range(rows):
                span = pl.ds(r * pairs * count + k, pairs, stride=count)
                evens[span, :] = image[top + r, pl.ds(left, pairs, stride=2), :]
                odds[span, :] = image[top + r, pl.ds(left + 1, pairs, stride=2), :]
            return carry

        lax.fori_loop(0, count, patch, 0, unroll=min(UNROLL, count))
        even, odd = evens[0:total, :], odds[0:total, :]
        mean = jnp.where(low, even, pltpu.roll(odd, half, 1))
        goal = jnp.where(low, pltpu.roll(even, half, 1), odd)
        mp_ref[chunk] = mean.astype(BF).reshape(mp_ref.shape[1:])
        tp_ref[chunk] = goal.astype(BF).reshape(tp_ref.shape[1:])


def chunk_kernel(chunk, last, pieces, *refs):
    table_ref = refs[0]
    noise_refs = refs[1 : 1 + pieces]
    refs = refs[1 + pieces :]
    (mp_ref, tp_ref, embed_ref, w1_ref, w2_ref, v2_ref, po_ref, pg_ref) = refs[:8]
    refs = refs[8:]
    before = None
    if chunk > 0:
        before, refs = refs[0], refs[1:]
    if last:
        keep_ref, send_ref, out_ref = refs[:3]
        refs = refs[3:]
    else:
        out_ref, refs = refs[0], refs[1:]
    (stage, nz, xn, xm, x2n, x2m, e1, o1, e2, o2, slope1, res, noisy, act2, back, gout, gt, emb, fac, by_level) = refs
    _, cells, count, wide = mp_ref.shape
    rows = 12
    pairs = cells // rows
    total = cells * count
    levels = embed_ref.shape[0]

    def entry(field, k):
        return table_ref[field, chunk * count + k]

    values = cells * wide
    level = lax.broadcasted_iota(jnp.int32, (levels, wide), 0).astype(F32)
    sig = 0.1 * jnp.exp(level * (math.log(100.0) / (levels - 1)))
    u = sig * sig + 1.0
    weight = u / (sig * sig)
    root = jnp.sqrt(u)
    scales = [1.0 / root, sig, 1.0 / u, sig / root, 2.0 * weight / values * (sig / root), weight / values]
    for i, scale in enumerate(scales):
        by_level[i, 0:levels] = scale
    by_level[len(scales), 0:levels] = embed_ref[...]
    group = GROUP
    half = wide // 2

    for ref in (xn, xm, e1, o1, e2, o2):
        for at in (0, rows + 1):
            ref[at] = jnp.zeros(ref.shape[1:], BF)
        for at in (0, pairs + 1):
            ref[1 : rows + 1, at] = jnp.zeros((rows,) + ref.shape[2:], BF)
    at = 0
    for ref in noise_refs:
        stage[at : at + ref.shape[0]] = ref[...]
        at += ref.shape[0]
    for k in range(count):
        piece = stage[entry(SOURCE, k)]
        nz[pl.ds(k, cells, stride=count), :] = piece.astype(F32)
        step = entry(STEP, k)
        emb[pl.ds(k, 1), :] = by_level[len(scales), pl.ds(step, 1), :]
        for i in range(len(scales)):
            fac[i, pl.ds(k, 1), :] = by_level[i, pl.ds(step, 1), :]

    def spread(index):
        return fac[index, 0:count][None]

    scale_in, sigma, skip, scale_out, grad_scale = (spread(i) for i in range(5))
    lane = lax.broadcasted_iota(jnp.int32, (1, 1, count, wide), 3)

    mean_bf = mp_ref[chunk]
    mean = mean_bf.astype(F32)
    residual = tp_ref[chunk].astype(F32) - mean
    noised = residual + sigma * nz[0:total, :].reshape(cells, count, wide)
    res[...] = residual.reshape(total, wide)
    noisy[...] = noised.reshape(total, wide)
    xn[1 : rows + 1, 1 : pairs + 1] = (scale_in * noised).astype(BF).reshape(rows, pairs, count, wide)
    xm[1 : rows + 1, 1 : pairs + 1] = mean_bf.reshape(rows, pairs, count, wide)
    for src, dst in ((xn, x2n), (xm, x2m)):
        dst[...] = jnp.where(
            lane < half, src[:, 2 : pairs + 2].astype(F32), src[:, 0:pairs].astype(F32)
        ).astype(BF)

    def view(ref, at, many, p0):
        return ref[at : at + many, p0 : p0 + pairs].reshape(many * pairs * count, wide)

    def stack_in(at, many):
        return [view(xn, at, many, 1), view(xm, at, many, 1), view(x2n, at, many, 0), view(x2m, at, many, 0)]

    def stack_eo(even, odd, at, many):
        return [view(even, at, many, 1), view(odd, at, many, 1), view(odd, at, many, 0), view(even, at, many, 2)]

    def shape4(value, many):
        return value.reshape(many, pairs, count, value.shape[-1])

    tile = group * pairs * count
    emb_pair = jnp.concatenate([emb[0:count, :], emb[0:count, :]], axis=1)[None]
    def span_of(g):
        return pl.ds(g * tile, tile)

    def conv(stack, weight_ref, g):
        left = jnp.concatenate(sum([stack(g * group + a, group) for a in range(3)], []), axis=1)
        return matmul(left, weight_ref[...])

    def inner(ref, g):
        return ref.at[g * group + 1 : g * group + 1 + group, 1 : pairs + 1]

    def first(g, pre):
        pre = pre.reshape(group * pairs, count, 2 * wide) + emb_pair
        gate = jax.nn.sigmoid(pre)
        act = shape4((pre * gate).astype(BF), group)
        slope1[span_of(g), :] = (gate * (1.0 + pre * (1.0 - gate))).reshape(tile, 2 * wide)
        inner(e1, g)[...] = act[..., :wide]
        inner(o1, g)[...] = act[..., wide:]

    losses = []

    def second(g, pre):
        span = span_of(g)
        gate = jax.nn.sigmoid(pre)
        act = (pre * gate).astype(BF)
        slope = gate * (1.0 + pre * (1.0 - gate))
        act2[span, :] = act
        output = matmul(act, po_ref[...]).reshape(group * pairs, count, wide)
        error = (
            skip * noisy[span, :].reshape(group * pairs, count, wide)
            + scale_out * output
            - res[span, :].reshape(group * pairs, count, wide)
        )
        losses.append(jnp.sum(error * error, axis=0))
        grad_output = (grad_scale * error).astype(BF).reshape(tile, wide)
        gout[span, :] = grad_output
        grad_pre = shape4((matmul(grad_output, pg_ref[...]) * slope).astype(BF), group)
        inner(e2, g)[...] = grad_pre[..., :wide]
        inner(o2, g)[...] = grad_pre[..., wide:]

    partial = []

    def third(g, pre):
        span = span_of(g)
        grad = (pre * slope1[span, :]).astype(BF)
        back[span, :] = grad
        partial.append(jnp.sum(grad.astype(F32).reshape(group * pairs, count, 2 * wide), axis=0))

    stages = (
        (lambda g: conv(stack_in, w1_ref, g), first),
        (lambda g: conv(lambda at, many: stack_eo(e1, o1, at, many), w2_ref, g), second),
        (lambda g: conv(lambda at, many: stack_eo(e2, o2, at, many), v2_ref, g), third),
    )
    groups = rows // group
    depth = wide
    pending = None
    for index, (product, finish) in enumerate(stages):
        for g in range(groups):
            pre = product(g)
            if pending is not None:
                pending()
            pending = functools.partial(finish, g, pre)
        if groups < 3:
            pending()
            pending = None
    proj = lax.dot_general(gout[...], act2[...], TN_FORM, preferred_element_type=F32)
    gt[0:depth, :] = jnp.transpose(view(e2, 1, rows, 1))
    gt[depth : 2 * depth, :] = jnp.transpose(view(o2, 1, rows, 1))
    if pending is not None:
        pending()
    loss = sum(losses[1:], losses[0])
    sums = sum(partial[1:], partial[0])

    def emit(at, size, value):
        if before is not None:
            value = value + before[at : at + size, :]
        out_ref[at : at + size, :] = value

    emit(18 * depth, half, proj[:half, :wide] + proj[half:, wide:])
    for a in range(3):
        right = jnp.concatenate(stack_eo(e1, o1, a, rows), axis=1)
        got = matmul(gt[...], right)
        h0, h1 = got[:depth], got[depth:]
        base = 9 * depth + 3 * a * depth
        emit(base, depth, h1[:, 0:wide] + h0[:, 2 * wide : 3 * wide])
        emit(base + depth, depth, h0[:, 0:wide] + h1[:, wide : 2 * wide])
        emit(base + 2 * depth, depth, h0[:, wide : 2 * wide] + h1[:, 3 * wide : 4 * wide])

    emb[0:count, :] = sums[:, :wide] + sums[:, wide:]
    table = 18 * depth + half
    if before is not None:
        out_ref[table : table + levels, :] = before[table : table + levels, :]
    else:
        out_ref[table : table + levels, :] = jnp.zeros((levels, wide), F32)
    for k in range(count):
        at = table + entry(STEP, k)
        out_ref[pl.ds(at, 1), :] = out_ref[pl.ds(at, 1), :] + emb[pl.ds(k, 1), :]

    levels_end = table + levels
    spots = lax.broadcasted_iota(jnp.int32, (8, wide), 0) * wide + lax.broadcasted_iota(jnp.int32, (8, wide), 1)
    sums = jnp.sum(fac[5, 0:count] * loss, axis=1, keepdims=True)
    owned = jnp.zeros((8, wide), F32)
    for k in range(count):
        owned = owned + jnp.where(spots == entry(PLACE, k), sums[k : k + 1], 0.0)
    if before is not None:
        owned = owned + before[levels_end : levels_end + 8, :]
    out_ref[levels_end:, :] = jnp.zeros((out_ref.shape[0] - levels_end, wide), F32)
    if last:
        rounded = owned.astype(BF).astype(F32)
        out_ref[levels_end + 8 : levels_end + 16, :] = owned - rounded
        owned = rounded
    out_ref[levels_end : levels_end + 8, :] = owned

    gt[...] = jnp.transpose(back[...])
    low = lax.broadcasted_iota(jnp.int32, (depth, wide), 1) < half
    for a in range(3):
        right = jnp.concatenate(stack_in(a, rows), axis=1)
        got = matmul(gt[...], right)
        h0, h1 = got[:depth], got[depth:]

        def merged(first, second):
            n = first[:, 0:wide], second[:, 0:wide]
            m = first[:, wide:], second[:, wide:]
            noise_part = n[0] + pltpu.roll(n[1], half, 1)
            mean_part = pltpu.roll(m[0], half, 1) + m[1]
            return jnp.where(low, noise_part, mean_part)

        base = 3 * a * depth
        direct, rim = slice(0, 2 * wide), slice(2 * wide, 4 * wide)
        emit(base, depth, merged(h1[:, direct], h0[:, rim]))
        emit(base + depth, depth, merged(h0[:, direct], h1[:, direct]))
        emit(base + 2 * depth, depth, merged(h1[:, rim], h0[:, direct]))

    if last:
        size = keep_ref.shape[0]
        core = lax.axis_index("segment")
        keep_ref[...] = out_ref[pl.ds(pl.multiple_of(core * size, 16), size), :]
        send_ref[...] = out_ref[pl.ds(pl.multiple_of((1 - core) * size, 16), size), :].astype(BF)


def unfold_kernel(own_ref, other_ref, one_ref, two_ref, proj_ref, embed_ref, loss_ref, full):
    size, wide = own_ref.shape
    core = lax.axis_index("segment")
    sample = core * lax.axis_size("dp") + lax.axis_index("dp")
    place = sample * lax.axis_size("rows") + lax.axis_index("rows")
    full[pl.ds(pl.multiple_of(core * size, 16), size), :] = own_ref[...]
    full[pl.ds(pl.multiple_of((1 - core) * size, 16), size), :] = other_ref[...]
    depth = one_ref.shape[0]
    for tap in range(9):
        span = slice(tap * wide, (tap + 1) * wide)
        one_ref[:, span] = full[tap * depth : (tap + 1) * depth].astype(F32)
        two_ref[:, span] = full[(9 + tap) * depth : (10 + tap) * depth].astype(F32)
    at = 18 * depth
    for ref in (proj_ref, embed_ref):
        ref[...] = full[at : at + ref.shape[0]].astype(F32)
        at += ref.shape[0]
    spots = lax.broadcasted_iota(jnp.int32, (8, wide), 0) * wide + lax.broadcasted_iota(jnp.int32, (8, wide), 1)
    both = full[at : at + 16].astype(F32)
    loss = jnp.where(spots == place, both[0:8] + both[8:16], 0.0)
    loss_ref[...] = jnp.sum(jnp.sum(loss, axis=1, keepdims=True), axis=0, keepdims=True)


def weights_kernel(one_ref, two_ref, proj_ref, w1_ref, w2_ref, v2_ref, po_ref, pg_ref):
    wide = one_ref.shape[0]
    half = wide // 2
    left, right = slice(0, wide), slice(wide, 2 * wide)
    for ref in (w1_ref, w2_ref, v2_ref, po_ref, pg_ref):
        ref[...] = jnp.zeros(ref.shape, BF)

    def place(ref, a, b, tap, split):
        base = 4 * wide * a

        def put(member, side):
            if split:
                start = {0: 0, 1: half, 3: 2 * wide, 2: 2 * wide + half}[member] + base
                ref[start : start + half, side] = tap[:half]
                ref[start + wide : start + wide + half, side] = tap[half:]
            else:
                start = base + member * wide
                ref[start : start + wide, side] = tap

        if b == 0:
            put(0, left)
            put(1, right)
        elif b == 1:
            put(1, left)
            put(3, right)
        else:
            put(0, right)
            put(2, left)

    for i, (a, b) in enumerate(TAPS):
        span = slice(i * wide, (i + 1) * wide)
        flipped = slice((8 - i) * wide, (9 - i) * wide)
        place(w1_ref, a + 1, b, jnp.transpose(one_ref[:, span]), True)
        place(w2_ref, a + 1, b, jnp.transpose(two_ref[:, span]), False)
        place(v2_ref, a + 1, b, two_ref[:, flipped], False)
    proj = proj_ref[...]
    pg_ref[0:half, left] = proj
    pg_ref[half:, right] = proj
    flat = jnp.transpose(proj.astype(F32)).astype(BF)
    zero = jnp.zeros_like(flat)
    po_ref[left, :] = jnp.concatenate([flat, zero], axis=1)
    po_ref[right, :] = jnp.concatenate([zero, flat], axis=1)


def by_distance(axis, distance):
    return [(i, i ^ distance) for i in range(lax.axis_size(axis))]


def rounded_to_bf16(values):
    return lax.reduce_precision(values, 8, 7)


def take(pieces, index):
    return lax.dynamic_index_in_dim(pieces, index, 0, keepdims=False)


def scatter_sum(values, axis):
    n = values.shape[0]
    me = lax.axis_index(axis)
    out = take(values, me)
    arrived = [
        lax.ppermute(take(values, me ^ d).astype(BF), axis, by_distance(axis, d)) for d in reversed(range(1, n))
    ]
    for piece in arrived:
        out = out + piece.astype(F32)
    return out


def gather_all(piece, axis):
    n = lax.axis_size(axis)
    me = lax.axis_index(axis)
    moved = {d: lax.ppermute(piece, axis, by_distance(axis, d)) for d in reversed(range(1, n))}
    found = [piece] + [moved[d] for d in range(1, n)]
    return jnp.stack([sum_select(found, me, i) for i in range(n)])


def sum_select(found, me, index):
    out = found[0]
    for d in range(1, len(found)):
        out = jnp.where((me ^ d) == index, found[d], out)
    return out


def rows_sum(piece, axis):
    n = lax.axis_size(axis)
    if n > 4:
        return lax.psum(piece, axis)
    values = [rounded_to_bf16(piece).astype(BF)]
    moved = {d: lax.ppermute(values[0], axis, by_distance(axis, d)) for d in reversed(range(1, n))}
    values += [moved[d] for d in range(1, n)]
    values = [v.astype(F32) for v in values]
    while len(values) > 1:
        values = [values[i] + values[i + 1] for i in range(0, len(values), 2)]
    return values[0]


def per_device(coarse, target, noise, regions, reg_conv, reg_out, conv_one, conv_two, out_proj, step_embed):
    strips = lax.axis_size("rows")
    me = lax.axis_index("rows")
    region = regions[0]
    per_strip = region.shape[1]
    most = noise.shape[2]
    capacity = max(2, (2 * per_strip + strips - 1) // strips)
    phases = 2
    deep = capacity // phases
    count = per_strip // phases
    exchange = strips <= 4
    channels = target.shape[1]
    height, width = target.shape[2:]
    cells = height * height
    wide = 2 * channels
    depth = conv_one.shape[0]
    levels = step_embed.shape[0]

    down = [(i + 1, i) for i in range(strips - 1)]
    own_target = jnp.transpose(target[0], (1, 0, 2))
    own_coarse = jnp.transpose(coarse[0], (1, 0, 2))
    core = lax.axis_index("segment")
    region_table = jnp.transpose(region, (0, 2, 1))

    slot_shape = (cells // 2, wide)
    pieces = strips if exchange else 1

    def packed(phase, region_table, noise):
        return call(
            functools.partial(pack_kernel, phase, exchange, most),
            [jax.ShapeDtypeStruct((strips * deep // pieces,) + slot_shape, BF)] * pieces,
            (region_table, noise[0, 0]),
            (SM, VM),
            [pltpu.SMEM((strips,), jnp.int32)],
            limit=8,
            cost=COSTS[0],
        )

    def sent(packed_pieces):
        if not exchange:
            return [lax.all_to_all(packed_pieces[0], "rows", 0, 0, tiled=True)]
        moved = {d: lax.ppermute(packed_pieces[d], "rows", by_distance("rows", d)) for d in (3, 2, 1) if d < strips}
        return [packed_pieces[0]] + [moved[d] for d in range(1, strips)]

    first_packed = packed(0, region_table, noise)

    reg_channels = reg_conv.shape[1] // 9
    fill = -(-reg_channels // 16) * 16
    per_row = (channels, width)
    even = me % 2 == 0
    pairs = [(i, i ^ 1) for i in range(strips)]
    others = [(i, ((i + 1) ^ 1) - 1) for i in range(1, strips - 1)]
    low_edge, high_edge = own_coarse[:1], own_coarse[height - 1 :]
    inward = lax.ppermute(jnp.where(even, high_edge, low_edge), "rows", pairs)
    outward = lax.ppermute(jnp.where(even, low_edge, high_edge), "rows", others)
    target_low = lax.ppermute(own_target, "rows", down)
    inward, outward = after((inward, outward), (first_packed[0],))
    mean, mean_top, mean_last = call(
        regress_kernel,
        [jax.ShapeDtypeStruct((rows,) + per_row, BF) for rows in (height, height - 1, 1)],
        (even.astype(jnp.int32)[None], inward, own_coarse, outward, reg_conv.T, reg_out),
        (SM,) + (VM,) * 5,
        [pltpu.VMEM((height + 2, 3 * fill, width), BF), pltpu.VMEM((9 * fill, depth), BF)],
        limit=12,
        cost=COSTS[1],
    )
    mean_low = lax.ppermute(mean_top, "rows", down)

    arrived = sent([p if d != 1 else after((p,), (mean_top,))[0] for d, p in enumerate(first_packed)])

    conv_one, conv_two, out_proj = after((conv_one, conv_two, out_proj), (mean_top,))
    stacked = jax.ShapeDtypeStruct((12 * depth, 2 * depth), BF)
    weights = call(
        weights_kernel,
        [stacked] * 3
        + [jax.ShapeDtypeStruct((2 * depth, wide), BF), jax.ShapeDtypeStruct((wide, 2 * depth), BF)],
        (conv_one, conv_two, out_proj),
        (VM,) * 3,
        limit=12,
        cost=COSTS[3],
    )
    patch_shape = jax.ShapeDtypeStruct((phases, cells // 2, count, wide), BF)
    got = pltpu.VMEM((cells // 2 * count + 8 * count, wide), F32)
    table, image = pl.pallas_call(
        functools.partial(own_kernel, exchange, deep, count),
        out_shape=[
            jax.ShapeDtypeStruct((5, per_strip), jnp.int32),
            jax.ShapeDtypeStruct((height, width, wide), BF),
        ],
        in_specs=[SM] + [VM] * 3,
        out_specs=[SM, VM],
        scratch_shapes=[pltpu.SMEM((strips,), jnp.int32)],
        compiler_params=pltpu.CompilerParams(vmem_limit_bytes=16 * MIB),
        cost_estimate=pl.CostEstimate(flops=COSTS[2], bytes_accessed=1, transcendentals=0),
    )(region_table, own_target, mean_top, after((mean_last,), (target_low,))[0])
    later_region, later_noise = after((region_table, noise), (weights[0], image))
    arrived += sent(packed(1, later_region, later_noise))
    mean_p, target_p = call(
        gather_kernel,
        [patch_shape, patch_shape],
        (table, image, mean_low, target_low),
        (SM, VM, VM, VM),
        [pltpu.VMEM((2 * height - 1, width + 16, wide), F32), got, got],
        limit=16,
        cost=COSTS[4],
    )

    cores, groups = lax.axis_size("segment"), lax.axis_size("dp")
    total = cells // 2 * count
    rows_used = 18 * depth + channels + levels
    unit = cores * groups * 16
    rows_all = -(-(rows_used + 16) // unit) * unit
    per_core = rows_all // cores
    sums = jax.ShapeDtypeStruct((rows_all, wide), F32)
    result = ()
    for chunk in range(phases):
        last = chunk == phases - 1
        pad = pltpu.VMEM((height + 2, height // 2 + 2, count, wide), BF)
        rim = pltpu.VMEM((height + 2, height // 2, count, wide), BF)
        used = arrived[: (chunk + 1) * pieces]
        slots_here = sum(piece.shape[0] for piece in used)
        ins = (table,) + tuple(used)
        ins += (mean_p, target_p, step_embed)
        ins += tuple(weights) + tuple(result)
        outs = [sums]
        if last:
            outs = [jax.ShapeDtypeStruct((per_core, wide), F32), jax.ShapeDtypeStruct((per_core, wide), BF)]
        result = call(
            functools.partial(chunk_kernel, chunk, last, len(used)),
            outs,
            ins,
            (SM,) + (VM,) * (len(ins) - 1),
            ([pltpu.VMEM((rows_all, wide), F32)] if last else [])
            + [
                pltpu.VMEM((slots_here, cells // 2, wide), BF),
                pltpu.VMEM((total + 8 * count, wide), F32),
                pad,
                pad,
                rim,
                rim,
                pad,
                pad,
                pad,
                pad,
                pltpu.VMEM((total, 2 * wide), F32),
                pltpu.VMEM((total, wide), F32),
                pltpu.VMEM((total, wide), F32),
                pltpu.VMEM((total, 2 * wide), BF),
                pltpu.VMEM((total, 2 * wide), BF),
                pltpu.VMEM((total, wide), BF),
                pltpu.VMEM((2 * wide, total), BF),
                pltpu.VMEM((count + 8, wide), F32),
                pltpu.VMEM((6, count + 8, wide), F32),
                pltpu.VMEM((7, levels + 8, wide), F32),
            ],
            cost=COSTS[5],
        )

    kept, given = result
    kept = kept + lax.ppermute(given, "segment", by_distance("segment", 1)).astype(F32)
    kept = scatter_sum(kept.reshape(groups, per_core // groups, wide), "dp")
    kept = rows_sum(kept, "rows")
    piece_rows = per_core // groups
    ending = (core == cores - 1) & (lax.axis_index("dp") == groups - 1)
    at = rows_used - (rows_all - piece_rows)
    exact = kept[at : at + 8] + kept[at + 8 : at + 16]
    rounded = rounded_to_bf16(exact)
    pair = jnp.concatenate([rounded, exact - rounded], axis=0)
    pair = jnp.where(ending, pair, kept[at : at + 16])
    kept = rounded_to_bf16(lax.dynamic_update_slice_in_dim(kept, pair, at, 0)).astype(BF)
    kept = gather_all(kept, "dp").reshape(per_core, wide)
    other = lax.ppermute(kept, "segment", by_distance("segment", 1))
    gradient = jax.ShapeDtypeStruct(conv_one.shape, F32)
    grad_one, grad_two, grad_proj, grad_embed, owner_loss = call(
        unfold_kernel,
        [
            gradient,
            gradient,
            jax.ShapeDtypeStruct(out_proj.shape, F32),
            jax.ShapeDtypeStruct(step_embed.shape, F32),
            jax.ShapeDtypeStruct((1, 1), F32),
        ],
        (kept, other),
        (VM, VM),
        [pltpu.VMEM((rows_all, wide), BF)],
        limit=12,
    )
    return jnp.transpose(mean, (1, 0, 2))[None], owner_loss, grad_one, grad_two, grad_proj, grad_embed


def solution(mesh):
    placed = (
        P(("segment", "dp"), None, "rows", None),
        P(("segment", "dp"), None, "rows", None),
        P(("segment", "dp"), "rows", None, None, None),
        P(("segment", "dp"), None, None, None),
        P(),
        P(),
        P(),
        P(),
        P(),
        P(),
    )
    return jax.shard_map(
        per_device,
        mesh=mesh,
        in_specs=placed,
        out_specs=(
            P(("segment", "dp"), None, "rows", None),
            P(("segment", "dp"), "rows"),
            P(),
            P(),
            P(),
            P(),
        ),
        check_vma=False,
    )
```
